128 devices in a mesh: ctx: 16 (over y, z), tp: 8 (over x, core).
Axes of the slice: x: 4, y: 4, z: 4, core: 2. Of those that a mesh axis runs over, the one named last changes fastest.
Arguments:
- text_hidden: bfloat16 [8192, 4096], P('ctx', 'tp'), may hold values from -20 to 20
- patch_rows: bfloat16 [16, 256, 4096], P(None, ('ctx', 'tp')), may hold values from -6 to 6
- image_start: int32 [16], replicated, may hold values from 0 to 7936, as said below
- w_query: bfloat16 [4096, 2048], P(None, 'tp'), may hold values from -0.09375 to 0.09375
- w_key: bfloat16 [4096, 2048], P(None, 'tp'), may hold values from -0.09375 to 0.09375
- w_value: bfloat16 [4096, 2048], P(None, 'tp'), may hold values from -0.09375 to 0.09375
- d_attn: bfloat16 [8192, 2048], P('ctx', 'tp'), may hold values from -6 to 6
Outputs:
- attn_out: bfloat16 [8192, 2048], P('ctx', 'tp')
- d_text: bfloat16 [8192, 4096], P('ctx', 'tp')
- d_patch: bfloat16 [16, 256, 4096], P(None, ('ctx', 'tp'))
- dw_query: float32 [4096, 2048], P('ctx', 'tp')
- dw_key: float32 [4096, 2048], P('ctx', 'tp')
- dw_value: float32 [4096, 2048], P('ctx', 'tp')
The draws below stay inside these ranges and needn't reach their ends.
Inputs may be any that keep to these rules, and one draw needn't show every extreme that they name: `image_start`: the document's positions fall into consecutive blocks of 512; each block holds exactly one image of 256 consecutive positions, wholly inside the block.
All inputs are finite; a program needn't handle non-finite values.
Results may differ from the reference program's by a relative error of at most 0.025.
The reference program's roundings to bfloat16 on the way count: a program that leaves them out, or rounds other values in their place, can miss the bound.
Values may be sent and summed in bfloat16 or wider, within the bound.
No kernel may reach another device: no remote copies, remote signals or barrier semaphores. Data moves between devices by JAX's collectives and lax.ppermute only.
A program may use at most 128 MiB of HBM per device.

```python
import jax
import jax.numpy as jnp
from jax import lax

D = 4096
HD = 128
HEADS_DEV = 2
PATCH = 256
SEQ_DEV = 512
TOKENS = 8192
IMAGES = 16
HEADS = 16
N_TP = 8


def draw_text_hidden(key, part):
    key = jax.random.fold_in(key, 5)
    base_key = jax.random.fold_in(key, 0)
    values = jnp.clip(jax.random.normal(base_key, (TOKENS, D), jnp.float32), -4.0, 4.0)
    return values.astype(jnp.bfloat16)


def draw_image_start(key, part):
    key = jax.random.fold_in(key, 9)
    order_key, offset_key = jax.random.split(key)
    shards = jax.random.permutation(order_key, IMAGES)
    offsets = jax.random.randint(offset_key, (IMAGES,), 0, SEQ_DEV - PATCH + 1)
    offsets = jnp.where(shards == 0, 0, jnp.where(shards == IMAGES - 1, SEQ_DEV - PATCH, offsets))
    return (shards * SEQ_DEV + offsets).astype(jnp.int32)


def levels(key, dims, cuts, low, high):
    factor_of, own = 1.0, jax.random.fold_in(key, 6)
    for position, blocks in cuts:
        steps = jnp.exp(jax.random.uniform(jax.random.fold_in(own, position), (blocks,), jnp.float32, low / len(cuts), high / len(cuts)))
        factor_of = factor_of * jnp.repeat(steps, dims[position] // blocks).reshape([-1 if axis == position else 1 for axis in range(len(dims))])
    return factor_of


def centred(own_key, extent, scale, limit, cuts=(), kind=jnp.bfloat16):
    result = scale * jax.random.normal(own_key, extent, jnp.float32)
    if cuts:
        result = result * levels(own_key, extent, cuts, -0.22, 0.18)
    return jnp.clip(result, -limit, limit).astype(kind)


def setup_inputs(seed: int = 0) -> dict:
    key_of = jax.random.split(jax.random.key(seed), 8)
    return {
        "text_hidden": draw_text_hidden(jax.random.fold_in(key_of[7], 71), 0),
        "patch_rows": centred(key_of[1], (IMAGES, PATCH, D), 1.0, 6.0, ((1, 128),)),
        "image_start": draw_image_start(jax.random.fold_in(key_of[7], 71), 0),
        "w_query": centred(key_of[3], (D, HEADS * HD), D ** -0.5, 0.09375, ((1, 8),)),
        "w_key": centred(key_of[4], (D, HEADS * HD), D ** -0.5, 0.09375, ((1, 8),)),
        "w_value": centred(key_of[5], (D, HEADS * HD), D ** -0.5, 0.09375, ((1, 8),)),
        "d_attn": centred(key_of[6], (TOKENS, HEADS * HD), 1.0, 6.0, ((0, 16), (1, 8))),
    }


NEG_LARGE = -1e30


def reference(text_hidden, patch_rows, image_start, w_query, w_key, w_value, d_attn):
    positions = jnp.arange(TOKENS, dtype=jnp.int32)
    offsets = positions[:, None] - image_start[None, :]
    inside = (offsets >= 0) & (offsets < PATCH)
    is_img = jnp.any(inside, axis=1)
    img_id = jnp.sum(jnp.where(inside, jnp.arange(1, IMAGES + 1, dtype=jnp.int32)[None, :], 0), axis=1).astype(jnp.int32)
    source_row = jnp.sum(jnp.where(inside, offsets + (jnp.arange(IMAGES, dtype=jnp.int32) * PATCH)[None, :], 0), axis=1).astype(jnp.int32)
    flat_rows = patch_rows.reshape(IMAGES * PATCH, D)
    mixed_rows = jnp.where(is_img[:, None], jnp.take(flat_rows, source_row, axis=0), text_hidden)
    queries = jnp.dot(mixed_rows, w_query, preferred_element_type=jnp.float32).astype(jnp.bfloat16)
    key_rows = jnp.dot(mixed_rows, w_key, preferred_element_type=jnp.float32).astype(jnp.bfloat16)
    value_rows = jnp.dot(mixed_rows, w_value, preferred_element_type=jnp.float32).astype(jnp.bfloat16)
    allowed = (positions[None, :] <= positions[:, None]) | ((img_id[:, None] == img_id[None, :]) & (img_id[:, None] > 0))
    score_scale = 1.0 / (HD ** 0.5)

    def split_heads(rows):
        return rows.reshape(TOKENS, HEADS, HD).transpose(1, 0, 2)

    def one_head(inputs):
        q_head, k_head, v_head, g_head = inputs
        scores = jnp.dot(q_head, k_head.T, preferred_element_type=jnp.float32) * score_scale
        row_max = jnp.max(jnp.where(allowed, scores, NEG_LARGE), axis=1)
        row_sum = jnp.sum(jnp.where(allowed, jnp.exp(scores - row_max[:, None]), 0.0), axis=1)
        lse = row_max + jnp.log(row_sum)
        probs = jnp.where(allowed, jnp.exp(scores - lse[:, None]), 0.0)
        rounded = probs.astype(jnp.bfloat16)
        attended = jnp.dot(rounded, v_head, preferred_element_type=jnp.float32).astype(jnp.bfloat16)
        row_dots = jnp.sum(g_head.astype(jnp.float32) * attended.astype(jnp.float32), axis=1)
        prob_grads = jnp.dot(g_head, v_head.T, preferred_element_type=jnp.float32)
        score_grads = (probs * (prob_grads - row_dots[:, None]) * score_scale).astype(jnp.bfloat16)
        dq_head = jnp.dot(score_grads, k_head, preferred_element_type=jnp.float32).astype(jnp.bfloat16)
        dk_head = jnp.dot(score_grads.T, q_head, preferred_element_type=jnp.float32).astype(jnp.bfloat16)
        dv_head = jnp.dot(rounded.T, g_head, preferred_element_type=jnp.float32).astype(jnp.bfloat16)
        return attended, dq_head, dk_head, dv_head

    attended, dq_heads, dk_heads, dv_heads = lax.map(
        one_head, (split_heads(queries), split_heads(key_rows), split_heads(value_rows), split_heads(d_attn)))

    def merge_heads(stacked):
        return stacked.transpose(1, 0, 2).reshape(TOKENS, HEADS * HD)

    attn_out = merge_heads(attended)
    grad_q = merge_heads(dq_heads)
    grad_k = merge_heads(dk_heads)
    grad_v = merge_heads(dv_heads)
    group_cols = HEADS_DEV * HD

    def group_term(total, group):
        low = group * group_cols
        term = jnp.dot(lax.dynamic_slice_in_dim(grad_q, low, group_cols, 1), lax.dynamic_slice_in_dim(w_query, low, group_cols, 1).T, preferred_element_type=jnp.float32)
        term = term + jnp.dot(lax.dynamic_slice_in_dim(grad_k, low, group_cols, 1), lax.dynamic_slice_in_dim(w_key, low, group_cols, 1).T, preferred_element_type=jnp.float32)
        term = term + jnp.dot(lax.dynamic_slice_in_dim(grad_v, low, group_cols, 1), lax.dynamic_slice_in_dim(w_value, low, group_cols, 1).T, preferred_element_type=jnp.float32)
        stored = lax.optimization_barrier(term.astype(jnp.bfloat16))
        return total + stored.astype(jnp.float32), None

    grad_mixed, _ = lax.scan(group_term, jnp.zeros((TOKENS, D), jnp.float32), jnp.arange(N_TP, dtype=jnp.int32))
    d_text = jnp.where(is_img[:, None], 0.0, grad_mixed).astype(jnp.bfloat16)
    patch_index = (image_start[:, None] + jnp.arange(PATCH, dtype=jnp.int32)[None, :]).astype(jnp.int32)
    d_patch = jnp.take(grad_mixed, patch_index.reshape(-1), axis=0).reshape(IMAGES, PATCH, D).astype(jnp.bfloat16)
    dw_query = jnp.dot(mixed_rows.T, grad_q, preferred_element_type=jnp.float32)
    dw_key = jnp.dot(mixed_rows.T, grad_k, preferred_element_type=jnp.float32)
    dw_value = jnp.dot(mixed_rows.T, grad_v, preferred_element_type=jnp.float32)
    return (attn_out, d_text, d_patch, dw_query, dw_key, dw_value)
```

```python
import functools
import math

import jax
import jax.numpy as jnp
import numpy as np
from jax import lax
from jax.experimental import pallas as pl
from jax.experimental.pallas import tpu as pltpu
from jax.sharding import PartitionSpec as P

HD = 128
PATCH = 256
SEQ = 512
RING = 4
OFFSETS = (0, 3, 1, 2)
NEG_LARGE = -1e30
SCALE = 1.0 / math.sqrt(HD)
LOG2E = math.log2(math.e)
SMALL_LIMIT = 12 * 1024 * 1024
STATS_LIMIT = 20 * 1024 * 1024
GRADS_LIMIT = 26 * 1024 * 1024
Z_GROUPS = [[RING * y + z for z in range(RING)] for y in range(RING)]
Y_GROUPS = [[RING * y + z for y in range(RING)] for z in range(RING)]
BF16 = jnp.bfloat16
F32 = jnp.float32


def pair_table():
    rows = []
    for ctx in range(RING * RING):
        y, z = divmod(ctx, RING)
        own = []
        for q in range(RING):
            for k in range(RING):
                if RING * k + z < RING * y + q:
                    own.append(8 * q + RING + k)
                if RING * y + k < RING * q + z:
                    own.append(8 * (RING + q) + k)
        assert len(own) == 15
        rows.append(own)
    return np.asarray(rows, np.int32)


def ctx_send(value, dy, dz):
    perm = [
        (RING * y + z, RING * ((y + dy) % RING) + (z + dz) % RING)
        for y in range(RING)
        for z in range(RING)
    ]
    return lax.ppermute(value, "ctx", perm)


def send_z(value, step):
    return ctx_send(value, 0, step)


def send_y(value, step):
    return ctx_send(value, step, 0)


def send_x(value, step):
    perm = [(2 * x + core, 2 * ((x + step) % RING) + core) for x in range(RING) for core in range(2)]
    return lax.ppermute(value, "tp", perm)


def send_core(value):
    return lax.ppermute(value, "tp", [(i, i ^ 1) for i in range(2 * RING)])


def ring_gather(value, send):
    half = value.shape[0] // 2
    before = send(value, 1)
    after = send(value, -1)
    far_low = send(before[:half], 1)
    far_high = send(after[half:], -1)
    return value, before, after, far_low, far_high


def add_to(piece, part, at):
    total = (lax.slice_in_dim(piece, at, at + part.shape[0]).astype(F32) + part.astype(F32)).astype(BF16)
    return lax.dynamic_update_slice_in_dim(piece, total, at, 0)


def scatter_far(pieces, send):
    own, before, after, far_low, far_high = pieces
    after = add_to(after, send(far_low, 1), 0)
    before = add_to(before, send(far_high, -1), far_low.shape[0])
    return own, before, after


def scatter_near(pieces, send):
    own, before, after = pieces
    return own, send(after, 1), send(before, -1)


def ring_scatter(pieces, send):
    return scatter_near(scatter_far(pieces, send), send)


def direct_scatter(pieces, send):
    own, before, after, far = pieces
    return own, send(before, -1), send(after, 1), send(far, 2)


def total(parts):
    return sum(part.astype(F32) for part in parts)


def dot_nn(a, b):
    return jnp.dot(a, b, preferred_element_type=F32)


def dot_nt(a, b):
    return lax.dot_general(a, b, (((1,), (1,)), ((), ())), preferred_element_type=F32)


def dot_tn(a, b):
    return lax.dot_general(a, b, (((0,), (0,)), ((), ())), preferred_element_type=F32)


QUERY, KEY, VALUE, COT = (slice(i * HD, (i + 1) * HD) for i in range(4))
JOINED = ((0, 0), (1, 1), (2, 1), (0, 1), (1, 0), (2, 0))
CHUNK = 1024
CHUNKS = 4096 // CHUNK


def join_kernel(wq, wk, wv, joined, sems):
    weights = (wq, wk, wv)
    copies = []
    for i, (part, head) in enumerate(JOINED):
        source = weights[part].at[:, head * HD : (head + 1) * HD]
        target = joined.at[:, i * HD : (i + 1) * HD]
        copies.append(pltpu.make_async_copy(source, target, sems.at[i]))
    for copy in copies:
        copy.start()
    for copy in copies:
        copy.wait()


def join_weights(wq, wk, wv):
    return pl.pallas_call(
        join_kernel,
        out_shape=jax.ShapeDtypeStruct((4096, 6 * HD), BF16),
        in_specs=[pl.BlockSpec(memory_space=pltpu.HBM)] * 3,
        out_specs=pl.BlockSpec(memory_space=pltpu.VMEM),
        scratch_shapes=[pltpu.SemaphoreType.DMA((6,))],
        compiler_params=pltpu.CompilerParams(vmem_limit_bytes=SMALL_LIMIT),
        cost_estimate=pl.CostEstimate(flops=0, bytes_accessed=12_000_000, transcendentals=0),
        name="join_weights",
    )(wq, wk, wv)


def pack(acc, cot, z_out, y_out):
    for head, out in enumerate((z_out, y_out)):
        out[:, : 3 * HD] = acc[:, head * 3 * HD : (head + 1) * 3 * HD].astype(BF16)
        out[:, COT] = cot[:, head * HD : (head + 1) * HD]


def block_rows(slices, j):
    return pl.ds(pl.multiple_of(slices[j] * SEQ, SEQ), SEQ)


def text_kernel(slices, own, oth, joined, cot, flipped, z_out, y_out):
    acc = None
    for j in range(2 * RING):
        part = own if j < RING else oth
        block = part[:, (j % RING) * SEQ : (j % RING + 1) * SEQ]
        depth = block_rows(slices, j)
        term = dot_nn(block, joined[depth, :])
        acc = term if acc is None else acc + term
        flipped[depth, :] = block.T
    pack(acc, cot[:PATCH], z_out, y_out)


def image_kernel(own, oth, joined, cot, flipped, z_out, y_out):
    acc = None
    for step in range(CHUNKS):
        depth = slice(step * CHUNK, (step + 1) * CHUNK)
        block = jnp.concatenate([own[:, depth], oth[:, depth]], axis=0)
        term = dot_nn(block, joined[depth, :])
        acc = term if acc is None else acc + term
        flipped[depth, :] = block.T
    pack(acc, cot[PATCH:], z_out, y_out)


def project(body, name, scalars, *operands):
    return pl.pallas_call(
        body,
        out_shape=[jax.ShapeDtypeStruct((4096, PATCH), BF16)]
        + [jax.ShapeDtypeStruct((PATCH, 4 * HD), BF16)] * 2,
        in_specs=smem(len(scalars)) + whole(4),
        out_specs=whole(3),
        compiler_params=pltpu.CompilerParams(vmem_limit_bytes=SMALL_LIMIT),
        cost_estimate=pl.CostEstimate(
            flops=2 * PATCH * 4096 * 768, bytes_accessed=2_000_000, transcendentals=0
        ),
        name=name,
    )(*scalars, *operands)


def ranks(off, shape, dim):
    index = lax.broadcasted_iota(jnp.int32, shape, dim)
    return jnp.where(index < PATCH, 2 * index, 2 * off - 1)


def diagonal_mask(off):
    return ranks(off, (SEQ, 1), 0) <= ranks(off, (1, SEQ), 1)


def fetch(refs, blocks, sems, y, z):
    copies = []
    for base, at, parts in ((0, z, refs[0:8]), (RING, y, refs[8:16])):
        for rel, off in enumerate(OFFSETS):
            slot = base + lax.rem(at + off, RING)
            for half in range(2):
                target = blocks.at[slot, half * PATCH : (half + 1) * PATCH]
                part = parts[2 * rel + half]
                copies.append(pltpu.make_async_copy(part, target, sems.at[len(copies)]))
    first = copies[0:2] + copies[8:10]
    rest = copies[2:8] + copies[10:]
    for copy in first + rest:
        copy.start()
    return first, rest


def own_pairs(meta, advance):
    y, z, off = meta[0], meta[1], meta[2]
    advance([(z, RING + y), (RING + y, z)], diagonal_mask(off))


def other_pairs(table, advance):
    def step(i, carry):
        codes = [table[3 * i + j] for j in range(3)]
        advance([(lax.div(code, 8), lax.rem(code, 8)) for code in codes], None)
        return carry

    lax.fori_loop(0, 5, step, 0)


def flip_all(dest, blocks, cols):
    for i in range(2 * RING):
        dest[i] = blocks[i, :, cols].T


def flip_own(dest, blocks, cols, y, z):
    dest[z] = blocks[z, :, cols].T
    dest[RING + y] = blocks[RING + y, :, cols].T


def stats_kernel(meta, table, *refs):
    z_out, y_out, o_out, blocks, vt, top, total, sems = refs[16:]
    y, z = meta[0], meta[1]
    first, rest = fetch(refs, blocks, sems, y, z)
    top[...] = jnp.full_like(top, NEG_LARGE)
    total[...] = jnp.zeros_like(total)
    o_out[...] = jnp.zeros_like(o_out)

    def advance(pairs, allowed):
        scores = [dot_nt(blocks[k, :, KEY], blocks[q, :, QUERY]) * (SCALE * LOG2E) for q, k in pairs]
        if allowed is not None:
            scores = [jnp.where(allowed, score, NEG_LARGE) for score in scores]
        highs = [jnp.max(score, axis=0, keepdims=True) for score in scores]
        for (q, k), score, high in zip(pairs, scores, highs):
            old = top[q]
            new = jnp.maximum(old, high)
            probs = jnp.exp2(score - new)
            shrink = jnp.exp2(old - new)
            top[q] = new
            total[q] = total[q] * shrink + jnp.sum(probs, axis=0, keepdims=True)
            o_out[q] = o_out[q] * shrink + dot_nn(vt[k], probs.astype(BF16))

    for copy in first:
        copy.wait()
    flip_own(vt, blocks, VALUE, y, z)
    own_pairs(meta, advance)
    for copy in rest:
        copy.wait()
    flip_all(vt, blocks, VALUE)
    other_pairs(table, advance)
    for head, out in ((0, z_out), (1, y_out)):
        for i in range(RING):
            at = head * RING + i
            count = total[at]
            some = count > 0.0
            safe = jnp.where(some, count, 1.0)
            partial = o_out[at] / safe
            o_out[at] = partial
            flipped = blocks[at, :, COT].astype(F32).T
            out[i : i + 1, :] = jnp.where(some, top[at] + jnp.log(safe) * LOG2E, NEG_LARGE)
            out[RING + i : RING + i + 1, :] = jnp.sum(partial * flipped, axis=0, keepdims=True)


def whole(count):
    return [pl.BlockSpec(memory_space=pltpu.VMEM)] * count


def in_hbm(count):
    return [pl.BlockSpec(memory_space=pltpu.HBM)] * count


def smem(count):
    return [pl.BlockSpec(memory_space=pltpu.SMEM)] * count


def attention_stats(meta, table, pieces):
    row = pltpu.VMEM((2 * RING, 1, SEQ), F32)
    return pl.pallas_call(
        stats_kernel,
        out_shape=[jax.ShapeDtypeStruct((2 * RING, SEQ), F32)] * 2
        + [jax.ShapeDtypeStruct((2 * RING, HD, SEQ), F32)],
        in_specs=smem(2) + in_hbm(16),
        out_specs=whole(3),
        scratch_shapes=[
            pltpu.VMEM((2 * RING, SEQ, 4 * HD), BF16),
            pltpu.VMEM((2 * RING, HD, SEQ), BF16),
            row,
            row,
            pltpu.SemaphoreType.DMA((16,)),
        ],
        compiler_params=pltpu.CompilerParams(vmem_limit_bytes=STATS_LIMIT),
        cost_estimate=pl.CostEstimate(
            flops=17 * 2 * 2 * SEQ * SEQ * HD,
            bytes_accessed=5_000_000,
            transcendentals=17 * SEQ * SEQ,
        ),
        name="stats",
    )(meta, table, *pieces)


def grads_kernel(meta, table, *refs):
    o_part = refs[16]
    stats = (refs[17:21], refs[21:25])
    outs = refs[25:35]
    blocks, kt, lse, dots, keep, dq_sum, dk_sum, dv_sum, sems = refs[35:]
    y, z = meta[0], meta[1]
    first, rest = fetch(refs, blocks, sems, y, z)
    dq_sum[...] = jnp.zeros_like(dq_sum)
    dk_sum[...] = jnp.zeros_like(dk_sum)
    dv_sum[...] = jnp.zeros_like(dv_sum)
    for head in range(2):
        parts = [ref[...] for ref in stats[head]]
        logs = [part[:RING] for part in parts]
        top = functools.reduce(jnp.maximum, logs)
        shares = [jnp.exp2(log - top) for log in logs]
        norm = sum(shares)
        full = top + jnp.log(norm) * LOG2E
        dot = sum(share * part[RING:] for share, part in zip(shares, parts)) / norm
        weight = jnp.exp2(logs[0] - full)
        for i in range(RING):
            lse[head * RING + i] = full[i : i + 1]
            dots[head * RING + i] = dot[i : i + 1]
            keep[head * RING + i] = weight[i : i + 1]

    def advance(pairs, allowed):
        for q, k in pairs:
            query, cot = blocks[q, :, QUERY], blocks[q, :, COT]
            probs = jnp.exp2(dot_nt(blocks[k, :, KEY], query) * (SCALE * LOG2E) - lse[q])
            if allowed is not None:
                probs = jnp.where(allowed, probs, 0.0)
            prob_grads = dot_nt(blocks[k, :, VALUE], cot)
            slope = (probs * (prob_grads - dots[q]) * SCALE).astype(BF16)
            dv_sum[k] += dot_nn(probs.astype(BF16), cot)
            dk_sum[k] += dot_nn(slope, query)
            dq_sum[q] += dot_nn(kt[k], slope)

    for copy in first:
        copy.wait()
    flip_own(kt, blocks, KEY, y, z)
    own_pairs(meta, advance)
    for copy in rest:
        copy.wait()
    flip_all(kt, blocks, KEY)
    other_pairs(table, advance)
    half = SEQ // 2
    for base, at, parts in ((0, z, outs[:5]), (RING, y, outs[5:])):
        for rel, shift in enumerate(OFFSETS):
            slot = base + lax.rem(at + shift, RING)
            terms = (
                dq_sum[slot].T.astype(BF16),
                dk_sum[slot].astype(BF16),
                dv_sum[slot].astype(BF16),
                (o_part[slot] * keep[slot]).T.astype(BF16),
            )
            for cols, term in zip((QUERY, KEY, VALUE, COT), terms):
                if rel < 3:
                    parts[rel][:, cols] = term
                else:
                    parts[3][:, cols] = term[:half]
                    parts[4][:, cols] = term[half:]


def attention_grads(meta, table, pieces, o_part, z_stats, y_stats):
    row = pltpu.VMEM((2 * RING, 1, SEQ), F32)
    tall = pltpu.VMEM((2 * RING, SEQ, HD), F32)
    flat = pltpu.VMEM((2 * RING, HD, SEQ), F32)
    full = jax.ShapeDtypeStruct((SEQ, 4 * HD), BF16)
    half = jax.ShapeDtypeStruct((SEQ // 2, 4 * HD), BF16)
    return pl.pallas_call(
        grads_kernel,
        out_shape=([full] * 3 + [half] * 2) * 2,
        in_specs=smem(2) + in_hbm(16) + whole(9),
        out_specs=whole(10),
        scratch_shapes=[
            pltpu.VMEM((2 * RING, SEQ, 4 * HD), BF16),
            pltpu.VMEM((2 * RING, HD, SEQ), BF16),
            row,
            row,
            row,
            flat,
            tall,
            tall,
            pltpu.SemaphoreType.DMA((16,)),
        ],
        compiler_params=pltpu.CompilerParams(vmem_limit_bytes=GRADS_LIMIT),
        cost_estimate=pl.CostEstimate(
            flops=17 * 5 * 2 * SEQ * SEQ * HD,
            bytes_accessed=10_000_000,
            transcendentals=17 * SEQ * SEQ,
        ),
        name="grads",
    )(meta, table, *pieces, o_part, *z_stats, *y_stats)


def hidden_kernel(slices, gz, gy, joined, own, oth):
    grads = jnp.concatenate([gz[:, : 3 * HD], gy[:, : 3 * HD]], axis=1)
    for j in range(2 * RING):
        out = own if j < RING else oth
        term = dot_nt(grads, joined[block_rows(slices, j), :]).astype(BF16)
        out[j % RING, :PATCH] = term[:PATCH]
        at = pl.ds(pl.multiple_of(PATCH + slices[j] * 32, 32), 32)
        for i in range(2 * RING):
            piece = own if i < RING else oth
            piece[i % RING, at, :] = term[PATCH + 32 * i : PATCH + 32 * (i + 1)]


def hidden_grads(slices, gz, gy, joined):
    return pl.pallas_call(
        hidden_kernel,
        out_shape=[jax.ShapeDtypeStruct((RING, SEQ, SEQ), BF16)] * 2,
        in_specs=smem(1) + whole(3),
        out_specs=whole(2),
        compiler_params=pltpu.CompilerParams(vmem_limit_bytes=SMALL_LIMIT),
        cost_estimate=pl.CostEstimate(
            flops=2 * SEQ * 4096 * 768, bytes_accessed=4_000_000, transcendentals=0
        ),
        name="hidden_grads",
    )(slices, gz, gy, joined)


def weight_kernel(meta, text, image, gz, gy, *refs):
    z_parts, y_parts, held = refs[:5], refs[5:10], refs[10]
    y, z = meta[0], meta[1]
    width = 3 * HD
    rows = 256
    grads = jnp.concatenate([gz[:, :width], gy[:, :width]], axis=1)

    def step(rel, shift):
        at = pl.multiple_of(lax.rem(y + shift, RING) * CHUNK, CHUNK)
        depth = pl.ds(at, CHUNK)
        term = dot_nn(text[depth, :], grads[:PATCH]) + dot_nn(image[depth, :], grads[PATCH:])
        held[...] = term.astype(BF16)
        for other, other_shift in enumerate(OFFSETS):
            source = pl.ds(pl.multiple_of(lax.rem(z + other_shift, RING) * rows, rows), rows)
            for parts, piece, place, cols in (
                (z_parts, rel, other, slice(0, width)),
                (y_parts, other, rel, slice(width, 2 * width)),
            ):
                if piece < 3:
                    parts[piece][place * rows : (place + 1) * rows, :] = held[source, cols]
                else:
                    low = place % 2
                    parts[3 + place // 2][low * rows : (low + 1) * rows, :] = held[source, cols]

    for rel, shift in enumerate(OFFSETS):
        step(rel, shift)


def weight_grads(meta, text, image, gz, gy):
    full = jax.ShapeDtypeStruct((CHUNK, 3 * HD), BF16)
    half = jax.ShapeDtypeStruct((CHUNK // 2, 3 * HD), BF16)
    return pl.pallas_call(
        weight_kernel,
        out_shape=([full] * 3 + [half] * 2) * 2,
        in_specs=smem(1) + whole(4),
        out_specs=whole(10),
        scratch_shapes=[pltpu.VMEM((CHUNK, 6 * HD), BF16)],
        compiler_params=pltpu.CompilerParams(vmem_limit_bytes=SMALL_LIMIT),
        cost_estimate=pl.CostEstimate(
            flops=2 * SEQ * 4096 * 768, bytes_accessed=4_000_000, transcendentals=0
        ),
        name="weight_grads",
    )(meta, text, image, gz, gy)


def local(text_hidden, patch_rows, image_start, w_query, w_key, w_value, d_attn):
    ctx = lax.axis_index("ctx")
    y, z = ctx // RING, ctx % RING
    images, pieces, width = patch_rows.shape
    owners = image_start // SEQ
    placing = (jnp.arange(images, dtype=jnp.int32)[:, None] == owners[None, :]).astype(BF16)
    off = jnp.sum(jnp.where(owners == ctx, image_start, 0)) - ctx * SEQ
    meta = jnp.stack([y, z, off]).astype(jnp.int32)
    table = lax.dynamic_index_in_dim(jnp.asarray(pair_table()), ctx, 0, keepdims=False)

    tp = lax.axis_index("tp")
    x, core = tp // 2, tp % 2
    columns = (x + jnp.asarray(OFFSETS, jnp.int32)) % RING
    slices = jnp.concatenate([columns * 2 + core, columns * 2 + 1 - core]).astype(jnp.int32)

    index = jnp.arange(SEQ, dtype=jnp.int32)
    rel = (index - PATCH) // 32
    shift = rel % RING
    shift = jnp.where(shift == 0, 0, jnp.where(shift == 1, 3, shift - 1))
    sender = 2 * ((x + shift) % RING) + jnp.where(rel < RING, core, 1 - core)
    text_pos = jnp.where(index < off, index, index + PATCH)
    image_pos = off + 16 * ((index % 32) // 2) + 2 * sender + index % 2
    pos = jnp.where(index < PATCH, text_pos, image_pos)
    placed = (index[:, None] == pos[None, :]).astype(BF16)

    by_shard = jnp.einsum("sk,krd->srd", placing, patch_rows, preferred_element_type=F32)
    by_shard, text_hidden = lax.optimization_barrier((by_shard.astype(BF16), text_hidden))
    arrived = lax.all_to_all(by_shard, "ctx", split_axis=0, concat_axis=0, tiled=True)
    kept = index[:PATCH, None] < off
    text = jnp.where(kept, text_hidden[:PATCH], text_hidden[PATCH:])
    t_ring = ring_gather(text, send_x)
    t_far = jnp.concatenate(t_ring[3:], axis=0)
    t_own = jnp.concatenate([*t_ring[:3], t_far], axis=1)
    t_oth = send_core(t_own)

    image = arrived.reshape(images * pieces, width)
    before, after = send_x(image, 1), send_x(image, -1)
    cot = dot_tn(placed, d_attn).astype(BF16)
    joined = join_weights(w_query, w_key, w_value)
    before, after, cot, joined = lax.optimization_barrier((before, after, cot, joined))
    half = image.shape[0] // 2
    far = (send_x(before[:half], 1), send_x(after[half:], -1))
    i_own = jnp.concatenate([image, before, after, *far], axis=0)
    i_oth = send_core(i_own)

    text_flipped, z_text, y_text = project(
        text_kernel, "qkv_text", (slices,), t_own, t_oth, joined, cot
    )
    image_flipped, z_image, y_image = project(
        image_kernel, "qkv_image", (), i_own, i_oth, joined, cot
    )

    def ring_of_halves(first, second, send):
        first_before, first_after = send(first, 1), send(first, -1)
        second_before, second_after = send(second, 1), send(second, -1)
        far = (send(first_before, 1), send(second_after, -1))
        return first, second, first_before, second_before, first_after, second_after, *far

    z_ring = ring_of_halves(z_text, z_image, send_z)
    y_ring = ring_of_halves(y_text, y_image, send_y)
    operands = (*z_ring, *y_ring)
    z_stats, y_stats, o_part = attention_stats(meta, table, operands)
    z_stats = [z_stats] + [send_z(z_stats, step) for step in (1, -1, 2)]
    y_stats = [y_stats] + [send_y(y_stats, step) for step in (1, -1, 2)]
    outs = attention_grads(meta, table, operands, o_part, z_stats, y_stats)
    gz = total(ring_scatter(outs[:5], send_z)).astype(BF16)
    gy = total(ring_scatter(outs[5:], send_y)).astype(BF16)

    parts = weight_grads(meta, text_flipped, image_flipped, gz, gy)
    parts, gz, gy = lax.optimization_barrier((parts, gz, gy))
    kept_part, sent_part = hidden_grads(slices, gz, gy, joined)
    got_part = send_core(sent_part)

    def x_piece(at, low=0, high=SEQ):
        return total((kept_part[at, low:high], got_part[at, low:high])).astype(BF16)

    x_pieces = [x_piece(0), x_piece(1), x_piece(2), x_piece(3, 0, PATCH), x_piece(3, PATCH, SEQ)]
    z_sum = scatter_far(parts[:5], send_y)
    y_sum = scatter_far(parts[5:], send_z)
    z_sum, y_sum, x_pieces = lax.optimization_barrier((z_sum, y_sum, x_pieces))
    x_sum = scatter_far(x_pieces, send_x)
    z_sum = scatter_near(z_sum, send_y)
    y_sum = scatter_near(y_sum, send_z)
    grad_mixed = total(scatter_near(x_sum, send_x)).astype(BF16)
    z_sum, y_sum, grad_mixed = lax.optimization_barrier((z_sum, y_sum, grad_mixed))
    t_grad = grad_mixed[:PATCH]
    i_grad = grad_mixed[PATCH:].reshape(8, images * pieces, SEQ).transpose(1, 0, 2)

    attended = jnp.concatenate([gz[:, COT], gy[:, COT]], axis=1)
    attn_out = dot_nn(placed, attended).astype(BF16)

    def second_phase(sums, send):
        parts = [lax.slice_in_dim(part, 0, 256) for part in sums]
        own = total(parts)
        others = []
        for i in range(1, RING):
            piece = [lax.slice_in_dim(part, i * 256, (i + 1) * 256) for part in sums]
            others.append(total(piece).astype(BF16))
        return total(direct_scatter((own, *others), send))

    z_dw = second_phase(z_sum, send_z)
    y_dw = second_phase(y_sum, send_y)

    in_image = (index >= off) & (index < off + PATCH)
    d_text = jnp.where(in_image[:, None], 0.0, jnp.concatenate([t_grad, t_grad], axis=0))
    returned = lax.all_to_all(
        i_grad.reshape(images, pieces, width), "ctx", split_axis=0, concat_axis=0, tiled=True
    )
    d_patch = jnp.einsum("sk,srd->krd", placing, returned, preferred_element_type=F32)
    dw_query = jnp.concatenate([z_dw[:, QUERY], y_dw[:, QUERY]], axis=1)
    dw_key = jnp.concatenate([y_dw[:, KEY], z_dw[:, KEY]], axis=1)
    dw_value = jnp.concatenate([y_dw[:, VALUE], z_dw[:, VALUE]], axis=1)
    return (
        attn_out,
        d_text.astype(BF16),
        d_patch.astype(BF16),
        dw_query,
        dw_key,
        dw_value,
    )


def solution(mesh):
    in_specs = (
        P("ctx", "tp"),
        P(None, ("ctx", "tp"), None),
        P(),
        P(None, "tp"),
        P(None, "tp"),
        P(None, "tp"),
        P("ctx", "tp"),
    )
    out_specs = (
        P("ctx", "tp"),
        P("ctx", "tp"),
        P(None, ("ctx", "tp"), None),
        P("ctx", "tp"),
        P("ctx", "tp"),
        P("ctx", "tp"),
    )
    return jax.shard_map(local, mesh=mesh, in_specs=in_specs, out_specs=out_specs, check_vma=False)
```

```python
import functools
import math

import jax
import jax.numpy as jnp
import numpy as np
from jax import lax
from jax.experimental import pallas as pl
from jax.experimental.pallas import tpu as pltpu
from jax.sharding import PartitionSpec as P

HD = 128
PATCH = 256
SEQ = 512
RING = 4
OFFSETS = (0, 3, 1, 2)
NEG_LARGE = -1e30
SCALE = 1.0 / math.sqrt(HD)
LOG2E = math.log2(math.e)
SMALL_LIMIT = 8 * 1024 * 1024
STATS_LIMIT = 16 * 1024 * 1024
GRADS_LIMIT = 22 * 1024 * 1024
Z_GROUPS = [[RING * y + z for z in range(RING)] for y in range(RING)]
Y_GROUPS = [[RING * y + z for y in range(RING)] for z in range(RING)]
BF16 = jnp.bfloat16
F32 = jnp.float32


def pair_table():
    rows = []
    for ctx in range(RING * RING):
        y, z = divmod(ctx, RING)
        own = []
        for q in range(RING):
            for k in range(RING):
                if RING * k + z < RING * y + q:
                    own.append(8 * q + RING + k)
                if RING * y + k < RING * q + z:
                    own.append(8 * (RING + q) + k)
        assert len(own) == 15
        rows.append(own)
    return np.asarray(rows, np.int32)


def ctx_send(value, dy, dz):
    perm = [
        (RING * y + z, RING * ((y + dy) % RING) + (z + dz) % RING)
        for y in range(RING)
        for z in range(RING)
    ]
    return lax.ppermute(value, "ctx", perm)


def send_z(value, step):
    return ctx_send(value, 0, step)


def send_y(value, step):
    return ctx_send(value, step, 0)


def send_x(value, step):
    perm = [(2 * x + core, 2 * ((x + step) % RING) + core) for x in range(RING) for core in range(2)]
    return lax.ppermute(value, "tp", perm)


def send_core(value):
    return lax.ppermute(value, "tp", [(i, i ^ 1) for i in range(2 * RING)])


def ring_gather(value, send):
    half = value.shape[0] // 2
    before = send(value, 1)
    after = send(value, -1)
    far_low = send(before[:half], 1)
    far_high = send(after[half:], -1)
    return value, before, after, far_low, far_high


def add_to(piece, part, at):
    total = (lax.slice_in_dim(piece, at, at + part.shape[0]).astype(F32) + part.astype(F32)).astype(BF16)
    return lax.dynamic_update_slice_in_dim(piece, total, at, 0)


def scatter_far(pieces, send):
    own, before, after, far_low, far_high = pieces
    after = add_to(after, send(far_low, 1), 0)
    before = add_to(before, send(far_high, -1), far_low.shape[0])
    return own, before, after


def scatter_near(pieces, send):
    own, before, after = pieces
    return own, send(after, 1), send(before, -1)


def ring_scatter(pieces, send):
    return scatter_near(scatter_far(pieces, send), send)


def direct_scatter(pieces, send):
    own, before, after, far = pieces
    return own, send(before, -1), send(after, 1), send(far, 2)


def total(parts):
    return sum(part.astype(F32) for part in parts)


def dot_nn(a, b):
    return jnp.dot(a, b, preferred_element_type=F32)


def dot_nt(a, b):
    return lax.dot_general(a, b, (((1,), (1,)), ((), ())), preferred_element_type=F32)


def dot_tn(a, b):
    return lax.dot_general(a, b, (((0,), (0,)), ((), ())), preferred_element_type=F32)


def small_call(body, name, out_shape, scalars, operands):
    return pl.pallas_call(
        body,
        out_shape=out_shape,
        in_specs=smem(len(scalars)) + whole(len(operands)),
        out_specs=whole(len(out_shape)),
        compiler_params=pltpu.CompilerParams(vmem_limit_bytes=SMALL_LIMIT),
        cost_estimate=pl.CostEstimate(flops=2_000_000, bytes_accessed=2_000_000, transcendentals=0),
        name=name,
    )(*scalars, *operands)


def place_kernel(starts, patches, out):
    for k in range(16):
        out[lax.div(starts[k], SEQ)] = patches[k]


def take_kernel(starts, returned, out):
    for k in range(16):
        out[k] = returned[lax.div(starts[k], SEQ)]


def move_patches(body, name, starts, patches):
    shape = [jax.ShapeDtypeStruct(patches.shape, BF16)]
    return small_call(body, name, shape, (starts,), (patches,))[0]


QUERY, KEY, VALUE, COT = (slice(i * HD, (i + 1) * HD) for i in range(4))
JOINED = ((0, 0), (1, 1), (2, 1), (0, 1), (1, 0), (2, 0))
CHUNK = 1024
CHUNKS = 4096 // CHUNK


def join_kernel(wq, wk, wv, joined, sems):
    weights = (wq, wk, wv)
    copies = []
    for i, (part, head) in enumerate(JOINED):
        source = weights[part].at[:, head * HD : (head + 1) * HD]
        target = joined.at[:, i * HD : (i + 1) * HD]
        copies.append(pltpu.make_async_copy(source, target, sems.at[i]))
    for copy in copies:
        copy.start()
    for copy in copies:
        copy.wait()


def join_weights(wq, wk, wv):
    return pl.pallas_call(
        join_kernel,
        out_shape=jax.ShapeDtypeStruct((4096, 6 * HD), BF16),
        in_specs=[pl.BlockSpec(memory_space=pltpu.HBM)] * 3,
        out_specs=pl.BlockSpec(memory_space=pltpu.VMEM),
        scratch_shapes=[pltpu.SemaphoreType.DMA((6,))],
        compiler_params=pltpu.CompilerParams(vmem_limit_bytes=SMALL_LIMIT),
        cost_estimate=pl.CostEstimate(flops=0, bytes_accessed=12_000_000, transcendentals=0),
        name="join_weights",
    )(wq, wk, wv)


def pack(acc, cot, z_out, y_out):
    for head, out in enumerate((z_out, y_out)):
        out[:, : 3 * HD] = acc[:, head * 3 * HD : (head + 1) * 3 * HD].astype(BF16)
        out[:, COT] = cot[:, head * HD : (head + 1) * HD]


def block_rows(slices, j):
    return pl.ds(pl.multiple_of(slices[j] * SEQ, SEQ), SEQ)


def text_kernel(slices, own, oth, joined, cot, flipped, z_out, y_out):
    acc = None
    for j in range(2 * RING):
        part = own if j < RING else oth
        block = part[:, (j % RING) * SEQ : (j % RING + 1) * SEQ]
        depth = block_rows(slices, j)
        term = dot_nn(block, joined[depth, :])
        acc = term if acc is None else acc + term
        flipped[depth, :] = block.T
    pack(acc, cot[:PATCH], z_out, y_out)


def image_kernel(own, oth, joined, cot, flipped, z_out, y_out):
    acc = None
    for step in range(CHUNKS):
        depth = slice(step * CHUNK, (step + 1) * CHUNK)
        block = jnp.concatenate([own[:, depth], oth[:, depth]], axis=0)
        term = dot_nn(block, joined[depth, :])
        acc = term if acc is None else acc + term
        flipped[depth, :] = block.T
    pack(acc, cot[PATCH:], z_out, y_out)


def project(body, name, scalars, *operands):
    return pl.pallas_call(
        body,
        out_shape=[jax.ShapeDtypeStruct((4096, PATCH), BF16)]
        + [jax.ShapeDtypeStruct((PATCH, 4 * HD), BF16)] * 2,
        in_specs=smem(len(scalars)) + whole(4),
        out_specs=whole(3),
        compiler_params=pltpu.CompilerParams(vmem_limit_bytes=SMALL_LIMIT),
        cost_estimate=pl.CostEstimate(
            flops=2 * PATCH * 4096 * 768, bytes_accessed=2_000_000, transcendentals=0
        ),
        name=name,
    )(*scalars, *operands)


def ranks(off, shape, dim):
    index = lax.broadcasted_iota(jnp.int32, shape, dim)
    return jnp.where(index < PATCH, 2 * index, 2 * off - 1)


def diagonal_mask(off):
    return ranks(off, (SEQ, 1), 0) <= ranks(off, (1, SEQ), 1)


def fetch(refs, blocks, sems, y, z):
    copies = []
    for base, at, parts in ((0, z, refs[0:8]), (RING, y, refs[8:16])):
        for rel, off in enumerate(OFFSETS):
            slot = base + lax.rem(at + off, RING)
            for half in range(2):
                target = blocks.at[slot, half * PATCH : (half + 1) * PATCH]
                part = parts[2 * rel + half]
                copies.append(pltpu.make_async_copy(part, target, sems.at[len(copies)]))
    first = copies[0:2] + copies[8:10]
    rest = copies[2:8] + copies[10:]
    for copy in first + rest:
        copy.start()
    return first, rest


def own_pairs(meta, advance):
    y, z, off = meta[0], meta[1], meta[2]
    advance([(z, RING + y), (RING + y, z)], diagonal_mask(off))


def other_pairs(table, advance):
    def step(i, carry):
        codes = [table[3 * i + j] for j in range(3)]
        advance([(lax.div(code, 8), lax.rem(code, 8)) for code in codes], None)
        return carry

    lax.fori_loop(0, 5, step, 0)


def flip_all(dest, blocks, cols):
    for i in range(2 * RING):
        dest[i] = blocks[i, :, cols].T


def flip_own(dest, blocks, cols, y, z):
    dest[z] = blocks[z, :, cols].T
    dest[RING + y] = blocks[RING + y, :, cols].T


def stats_kernel(meta, table, *refs):
    z_out, y_out, o_out, blocks, vt, top, total, sems = refs[16:]
    y, z = meta[0], meta[1]
    first, rest = fetch(refs, blocks, sems, y, z)
    top[...] = jnp.full_like(top, NEG_LARGE)
    total[...] = jnp.zeros_like(total)
    o_out[...] = jnp.zeros_like(o_out)

    def advance(pairs, allowed):
        scores = [dot_nt(blocks[k, :, KEY], blocks[q, :, QUERY]) * (SCALE * LOG2E) for q, k in pairs]
        if allowed is not None:
            scores = [jnp.where(allowed, score, NEG_LARGE) for score in scores]
        highs = [jnp.max(score, axis=0, keepdims=True) for score in scores]
        for (q, k), score, high in zip(pairs, scores, highs):
            old = top[q]
            new = jnp.maximum(old, high)
            probs = jnp.exp2(score - new)
            shrink = jnp.exp2(old - new)
            top[q] = new
            total[q] = total[q] * shrink + jnp.sum(probs, axis=0, keepdims=True)
            o_out[q] = o_out[q] * shrink + dot_nn(vt[k], probs.astype(BF16))

    for copy in first:
        copy.wait()
    flip_own(vt, blocks, VALUE, y, z)
    own_pairs(meta, advance)
    for copy in rest:
        copy.wait()
    flip_all(vt, blocks, VALUE)
    other_pairs(table, advance)
    for head, out in ((0, z_out), (1, y_out)):
        for i in range(RING):
            at = head * RING + i
            count = total[at]
            some = count > 0.0
            safe = jnp.where(some, count, 1.0)
            partial = o_out[at] / safe
            o_out[at] = partial
            flipped = blocks[at, :, COT].astype(F32).T
            out[i : i + 1, :] = jnp.where(some, top[at] + jnp.log(safe) * LOG2E, NEG_LARGE)
            out[RING + i : RING + i + 1, :] = jnp.sum(partial * flipped, axis=0, keepdims=True)


def whole(count):
    return [pl.BlockSpec(memory_space=pltpu.VMEM)] * count


def in_hbm(count):
    return [pl.BlockSpec(memory_space=pltpu.HBM)] * count


def smem(count):
    return [pl.BlockSpec(memory_space=pltpu.SMEM)] * count


def attention_stats(meta, table, pieces):
    row = pltpu.VMEM((2 * RING, 1, SEQ), F32)
    return pl.pallas_call(
        stats_kernel,
        out_shape=[jax.ShapeDtypeStruct((2 * RING, SEQ), F32)] * 2
        + [jax.ShapeDtypeStruct((2 * RING, HD, SEQ), F32)],
        in_specs=smem(2) + in_hbm(16),
        out_specs=whole(3),
        scratch_shapes=[
            pltpu.VMEM((2 * RING, SEQ, 4 * HD), BF16),
            pltpu.VMEM((2 * RING, HD, SEQ), BF16),
            row,
            row,
            pltpu.SemaphoreType.DMA((16,)),
        ],
        compiler_params=pltpu.CompilerParams(vmem_limit_bytes=STATS_LIMIT),
        cost_estimate=pl.CostEstimate(
            flops=17 * 2 * 2 * SEQ * SEQ * HD,
            bytes_accessed=5_000_000,
            transcendentals=17 * SEQ * SEQ,
        ),
        name="stats",
    )(meta, table, *pieces)


def grads_kernel(meta, table, *refs):
    o_part = refs[16]
    stats = (refs[17:21], refs[21:25])
    outs = refs[25:35]
    blocks, kt, lse, dots, keep, dq_sum, dk_sum, dv_sum, sems = refs[35:]
    y, z = meta[0], meta[1]
    first, rest = fetch(refs, blocks, sems, y, z)
    dq_sum[...] = jnp.zeros_like(dq_sum)
    dk_sum[...] = jnp.zeros_like(dk_sum)
    dv_sum[...] = jnp.zeros_like(dv_sum)
    for head in range(2):
        parts = [ref[...] for ref in stats[head]]
        logs = [part[:RING] for part in parts]
        top = functools.reduce(jnp.maximum, logs)
        shares = [jnp.exp2(log - top) for log in logs]
        norm = sum(shares)
        full = top + jnp.log(norm) * LOG2E
        dot = sum(share * part[RING:] for share, part in zip(shares, parts)) / norm
        weight = jnp.exp2(logs[0] - full)
        for i in range(RING):
            lse[head * RING + i] = full[i : i + 1]
            dots[head * RING + i] = dot[i : i + 1]
            keep[head * RING + i] = weight[i : i + 1]

    def advance(pairs, allowed):
        for q, k in pairs:
            query, cot = blocks[q, :, QUERY], blocks[q, :, COT]
            probs = jnp.exp2(dot_nt(blocks[k, :, KEY], query) * (SCALE * LOG2E) - lse[q])
            if allowed is not None:
                probs = jnp.where(allowed, probs, 0.0)
            prob_grads = dot_nt(blocks[k, :, VALUE], cot)
            slope = (probs * (prob_grads - dots[q]) * SCALE).astype(BF16)
            dv_sum[k] += dot_nn(probs.astype(BF16), cot)
            dk_sum[k] += dot_nn(slope, query)
            dq_sum[q] += dot_nn(kt[k], slope)

    for copy in first:
        copy.wait()
    flip_own(kt, blocks, KEY, y, z)
    own_pairs(meta, advance)
    for copy in rest:
        copy.wait()
    flip_all(kt, blocks, KEY)
    other_pairs(table, advance)
    half = SEQ // 2
    for base, at, parts in ((0, z, outs[:5]), (RING, y, outs[5:])):
        for rel, shift in enumerate(OFFSETS):
            slot = base + lax.rem(at + shift, RING)
            terms = (
                dq_sum[slot].T.astype(BF16),
                dk_sum[slot].astype(BF16),
                dv_sum[slot].astype(BF16),
                (o_part[slot] * keep[slot]).T.astype(BF16),
            )
            for cols, term in zip((QUERY, KEY, VALUE, COT), terms):
                if rel < 3:
                    parts[rel][:, cols] = term
                else:
                    parts[3][:, cols] = term[:half]
                    parts[4][:, cols] = term[half:]


def attention_grads(meta, table, pieces, o_part, z_stats, y_stats):
    row = pltpu.VMEM((2 * RING, 1, SEQ), F32)
    tall = pltpu.VMEM((2 * RING, SEQ, HD), F32)
    flat = pltpu.VMEM((2 * RING, HD, SEQ), F32)
    full = jax.ShapeDtypeStruct((SEQ, 4 * HD), BF16)
    half = jax.ShapeDtypeStruct((SEQ // 2, 4 * HD), BF16)
    return pl.pallas_call(
        grads_kernel,
        out_shape=([full] * 3 + [half] * 2) * 2,
        in_specs=smem(2) + in_hbm(16) + whole(9),
        out_specs=whole(10),
        scratch_shapes=[
            pltpu.VMEM((2 * RING, SEQ, 4 * HD), BF16),
            pltpu.VMEM((2 * RING, HD, SEQ), BF16),
            row,
            row,
            row,
            flat,
            tall,
            tall,
            pltpu.SemaphoreType.DMA((16,)),
        ],
        compiler_params=pltpu.CompilerParams(vmem_limit_bytes=GRADS_LIMIT),
        cost_estimate=pl.CostEstimate(
            flops=17 * 5 * 2 * SEQ * SEQ * HD,
            bytes_accessed=10_000_000,
            transcendentals=17 * SEQ * SEQ,
        ),
        name="grads",
    )(meta, table, *pieces, o_part, *z_stats, *y_stats)


def hidden_kernel(slices, *refs):
    joined, gz, gy, own, oth = refs[6:]
    for parts, grads in ((refs[:3], gz), (refs[3:6], gy)):
        grads[...] = total([part[...] for part in parts]).astype(BF16)
    grads = jnp.concatenate([gz[:, : 3 * HD], gy[:, : 3 * HD]], axis=1)
    for j in range(2 * RING):
        out = own if j < RING else oth
        term = dot_nt(grads, joined[block_rows(slices, j), :]).astype(BF16)
        out[j % RING, :PATCH] = term[:PATCH]
        at = pl.ds(pl.multiple_of(PATCH + slices[j] * 32, 32), 32)
        for i in range(2 * RING):
            piece = own if i < RING else oth
            piece[i % RING, at, :] = term[PATCH + 32 * i : PATCH + 32 * (i + 1)]


def hidden_grads(slices, z_parts, y_parts, joined):
    return pl.pallas_call(
        hidden_kernel,
        out_shape=[jax.ShapeDtypeStruct((SEQ, 4 * HD), BF16)] * 2
        + [jax.ShapeDtypeStruct((RING, SEQ, SEQ), BF16)] * 2,
        in_specs=smem(1) + whole(7),
        out_specs=whole(4),
        compiler_params=pltpu.CompilerParams(vmem_limit_bytes=SMALL_LIMIT),
        cost_estimate=pl.CostEstimate(
            flops=2 * SEQ * 4096 * 768, bytes_accessed=4_000_000, transcendentals=0
        ),
        name="hidden_grads",
    )(slices, *z_parts, *y_parts, joined)


def x_kernel(kept, got, *outs):
    for rel in range(3):
        outs[rel][...] = total((kept[rel], got[rel])).astype(BF16)
    for half in range(2):
        rows = slice(half * PATCH, (half + 1) * PATCH)
        outs[3 + half][...] = total((kept[3, rows], got[3, rows])).astype(BF16)


def x_pieces_of(kept, got):
    full = jax.ShapeDtypeStruct((SEQ, SEQ), BF16)
    half = jax.ShapeDtypeStruct((PATCH, SEQ), BF16)
    return small_call(x_kernel, "x_pieces", [full] * 3 + [half] * 2, (), (kept, got))


def split_kernel(*refs):
    for parts, outs in ((refs[:3], refs[6:10]), (refs[3:6], refs[10:14])):
        for i, out in enumerate(outs):
            rows = slice(i * 256, (i + 1) * 256)
            out[...] = total([part[rows] for part in parts]).astype(out.dtype)


def split_phase(z_sum, y_sum):
    own = jax.ShapeDtypeStruct((256, 3 * HD), F32)
    other = jax.ShapeDtypeStruct((256, 3 * HD), BF16)
    outs = small_call(split_kernel, "split", [own, other, other, other] * 2, (), (*z_sum, *y_sum))
    return outs[:4], outs[4:]


def mixed_kernel(meta, own, before, after, text_out, image_out):
    off = meta[2]
    grads = total((own[...], before[...], after[...])).astype(BF16).astype(F32)
    text = grads[:PATCH]
    row = lax.broadcasted_iota(jnp.int32, (PATCH, 1), 0)
    text_out[:PATCH] = jnp.where(row < off, text, 0.0).astype(BF16)
    text_out[PATCH:] = jnp.where(row < off, 0.0, text).astype(BF16)
    for i in range(8):
        rows = slice(PATCH + 32 * i, PATCH + 32 * (i + 1))
        image_out[:, i * SEQ : (i + 1) * SEQ] = grads[rows].astype(BF16)


def mixed_grads(meta, parts):
    shapes = [jax.ShapeDtypeStruct((SEQ, SEQ), BF16), jax.ShapeDtypeStruct((32, 4096), BF16)]
    return small_call(mixed_kernel, "mixed_grads", shapes, (meta,), parts)


def final_kernel(*refs):
    z_sum = total([ref[...] for ref in refs[:4]])
    y_sum = total([ref[...] for ref in refs[4:8]])
    for cols, out, first, second in (
        (QUERY, refs[8], z_sum, y_sum),
        (KEY, refs[9], y_sum, z_sum),
        (VALUE, refs[10], y_sum, z_sum),
    ):
        out[:, :HD] = first[:, cols]
        out[:, HD:] = second[:, cols]


def final_sums(z_parts, y_parts):
    shape = jax.ShapeDtypeStruct((256, 2 * HD), F32)
    return small_call(final_kernel, "final_sums", [shape] * 3, (), (*z_parts, *y_parts))


def weight_kernel(meta, text, image, gz, gy, *refs):
    z_parts, y_parts, held = refs[:5], refs[5:10], refs[10]
    y, z = meta[0], meta[1]
    width = 3 * HD
    rows = 256
    grads = jnp.concatenate([gz[:, :width], gy[:, :width]], axis=1)

    def step(rel, shift):
        at = pl.multiple_of(lax.rem(y + shift, RING) * CHUNK, CHUNK)
        depth = pl.ds(at, CHUNK)
        term = dot_nn(text[depth, :], grads[:PATCH]) + dot_nn(image[depth, :], grads[PATCH:])
        held[...] = term.astype(BF16)
        for other, other_shift in enumerate(OFFSETS):
            source = pl.ds(pl.multiple_of(lax.rem(z + other_shift, RING) * rows, rows), rows)
            for parts, piece, place, cols in (
                (z_parts, rel, other, slice(0, width)),
                (y_parts, other, rel, slice(width, 2 * width)),
            ):
                if piece < 3:
                    parts[piece][place * rows : (place + 1) * rows, :] = held[source, cols]
                else:
                    low = place % 2
                    parts[3 + place // 2][low * rows : (low + 1) * rows, :] = held[source, cols]

    for rel, shift in enumerate(OFFSETS):
        step(rel, shift)


def weight_grads(meta, text, image, gz, gy):
    full = jax.ShapeDtypeStruct((CHUNK, 3 * HD), BF16)
    half = jax.ShapeDtypeStruct((CHUNK // 2, 3 * HD), BF16)
    return pl.pallas_call(
        weight_kernel,
        out_shape=([full] * 3 + [half] * 2) * 2,
        in_specs=smem(1) + whole(4),
        out_specs=whole(10),
        scratch_shapes=[pltpu.VMEM((CHUNK, 6 * HD), BF16)],
        compiler_params=pltpu.CompilerParams(vmem_limit_bytes=SMALL_LIMIT),
        cost_estimate=pl.CostEstimate(
            flops=2 * SEQ * 4096 * 768, bytes_accessed=4_000_000, transcendentals=0
        ),
        name="weight_grads",
    )(meta, text, image, gz, gy)


def local(text_hidden, patch_rows, image_start, w_query, w_key, w_value, d_attn):
    ctx = lax.axis_index("ctx")
    y, z = ctx // RING, ctx % RING
    images, pieces, width = patch_rows.shape
    owners = image_start // SEQ
    off = jnp.sum(jnp.where(owners == ctx, image_start, 0)) - ctx * SEQ
    meta = jnp.stack([y, z, off]).astype(jnp.int32)
    table = lax.dynamic_index_in_dim(jnp.asarray(pair_table()), ctx, 0, keepdims=False)

    tp = lax.axis_index("tp")
    x, core = tp // 2, tp % 2
    columns = (x + jnp.asarray(OFFSETS, jnp.int32)) % RING
    slices = jnp.concatenate([columns * 2 + core, columns * 2 + 1 - core]).astype(jnp.int32)

    index = jnp.arange(SEQ, dtype=jnp.int32)
    rel = (index - PATCH) // 32
    shift = rel % RING
    shift = jnp.where(shift == 0, 0, jnp.where(shift == 1, 3, shift - 1))
    sender = 2 * ((x + shift) % RING) + jnp.where(rel < RING, core, 1 - core)
    text_pos = jnp.where(index < off, index, index + PATCH)
    image_pos = off + 16 * ((index % 32) // 2) + 2 * sender + index % 2
    pos = jnp.where(index < PATCH, text_pos, image_pos)
    placed = (index[:, None] == pos[None, :]).astype(BF16)

    by_shard = move_patches(place_kernel, "place_patches", image_start, patch_rows)
    by_shard, text_hidden = lax.optimization_barrier((by_shard, text_hidden))
    arrived = lax.all_to_all(by_shard, "ctx", split_axis=0, concat_axis=0, tiled=True)
    kept = index[:PATCH, None] < off
    text = jnp.where(kept, text_hidden[:PATCH], text_hidden[PATCH:])
    t_ring = ring_gather(text, send_x)
    arrived, t_ring = lax.optimization_barrier((arrived, t_ring))
    t_far = jnp.concatenate(t_ring[3:], axis=0)
    t_own = jnp.concatenate([*t_ring[:3], t_far], axis=1)
    t_oth = send_core(t_own)

    image = arrived.reshape(images * pieces, width)
    before, after = send_x(image, 1), send_x(image, -1)
    cot = dot_tn(placed, d_attn).astype(BF16)
    joined = join_weights(w_query, w_key, w_value)
    half = image.shape[0] // 2
    far = (send_x(before[:half], 1), send_x(after[half:], -1))
    i_own = jnp.concatenate([image, before, after, *far], axis=0)
    i_oth = send_core(i_own)

    text_flipped, z_text, y_text = project(
        text_kernel, "qkv_text", (slices,), t_own, t_oth, joined, cot
    )
    image_flipped, z_image, y_image = project(
        image_kernel, "qkv_image", (), i_own, i_oth, joined, cot
    )

    def ring_of_halves(first, second, send):
        first_before, first_after = send(first, 1), send(first, -1)
        second_before, second_after = send(second, 1), send(second, -1)
        far = (send(first_before, 1), send(second_after, -1))
        return first, second, first_before, second_before, first_after, second_after, *far

    z_ring = ring_of_halves(z_text, z_image, send_z)
    y_ring = ring_of_halves(y_text, y_image, send_y)
    operands = (*z_ring, *y_ring)
    z_stats, y_stats, o_part = attention_stats(meta, table, operands)
    z_stats = [z_stats] + [send_z(z_stats, step) for step in (1, -1, 2)]
    y_stats = [y_stats] + [send_y(y_stats, step) for step in (1, -1, 2)]
    outs = attention_grads(meta, table, operands, o_part, z_stats, y_stats)
    z_parts, y_parts = ring_scatter(outs[:5], send_z), ring_scatter(outs[5:], send_y)
    gz, gy, kept_part, sent_part = hidden_grads(slices, z_parts, y_parts, joined)
    got_part = send_core(sent_part)
    parts = weight_grads(meta, text_flipped, image_flipped, gz, gy)
    x_pieces = x_pieces_of(kept_part, got_part)
    z_sum = scatter_far(parts[:5], send_y)
    y_sum = scatter_far(parts[5:], send_z)
    z_sum, y_sum, x_pieces = lax.optimization_barrier((z_sum, y_sum, x_pieces))
    x_sum = scatter_far(x_pieces, send_x)
    z_sum = scatter_near(z_sum, send_y)
    y_sum = scatter_near(y_sum, send_z)
    d_text, i_grad = mixed_grads(meta, scatter_near(x_sum, send_x))

    attended = jnp.concatenate([gz[:, COT], gy[:, COT]], axis=1)
    attn_out = dot_nn(placed, attended).astype(BF16)

    returned = lax.all_to_all(
        i_grad.reshape(images, pieces, width), "ctx", split_axis=0, concat_axis=0, tiled=True
    )
    d_patch = move_patches(take_kernel, "take_patches", image_start, returned)
    z_pieces, y_pieces = split_phase(z_sum, y_sum)
    dw_query, dw_key, dw_value = final_sums(
        direct_scatter(z_pieces, send_z), direct_scatter(y_pieces, send_y)
    )
    return (
        attn_out,
        d_text,
        d_patch,
        dw_query,
        dw_key,
        dw_value,
    )


def solution(mesh):
    in_specs = (
        P("ctx", "tp"),
        P(None, ("ctx", "tp"), None),
        P(),
        P(None, "tp"),
        P(None, "tp"),
        P(None, "tp"),
        P("ctx", "tp"),
    )
    out_specs = (
        P("ctx", "tp"),
        P("ctx", "tp"),
        P(None, ("ctx", "tp"), None),
        P("ctx", "tp"),
        P("ctx", "tp"),
        P("ctx", "tp"),
    )
    return jax.shard_map(local, mesh=mesh, in_specs=in_specs, out_specs=out_specs, check_vma=False)
```

```python
import functools
import math

import jax
import jax.numpy as jnp
import numpy as np
from jax import lax
from jax.experimental import pallas as pl
from jax.experimental.pallas import tpu as pltpu
from jax.sharding import PartitionSpec as P

HD = 128
PATCH = 256
SEQ = 512
RING = 4
OFFSETS = (0, 3, 1, 2)
NEG_LARGE = -1e30
SCALE = 1.0 / math.sqrt(HD)
LOG2E = math.log2(math.e)
SMALL_LIMIT = 8 * 1024 * 1024
STREAM_LIMIT = 15 * 1024 * 1024
STATS_LIMIT = 16 * 1024 * 1024
GRADS_LIMIT = 22 * 1024 * 1024
Z_GROUPS = [[RING * y + z for z in range(RING)] for y in range(RING)]
Y_GROUPS = [[RING * y + z for y in range(RING)] for z in range(RING)]
BF16 = jnp.bfloat16
F32 = jnp.float32


def pair_table():
    rows = []
    for ctx in range(RING * RING):
        y, z = divmod(ctx, RING)
        own = []
        for q in range(RING):
            for k in range(RING):
                if RING * k + z < RING * y + q:
                    own.append(8 * q + RING + k)
                if RING * y + k < RING * q + z:
                    own.append(8 * (RING + q) + k)
        assert len(own) == 15
        rows.append(own)
    return np.asarray(rows, np.int32)


def ctx_send(value, dy, dz):
    perm = [
        (RING * y + z, RING * ((y + dy) % RING) + (z + dz) % RING)
        for y in range(RING)
        for z in range(RING)
    ]
    return lax.ppermute(value, "ctx", perm)


def send_z(value, step):
    return ctx_send(value, 0, step)


def send_y(value, step):
    return ctx_send(value, step, 0)


def send_x(value, step):
    perm = [(2 * x + core, 2 * ((x + step) % RING) + core) for x in range(RING) for core in range(2)]
    return lax.ppermute(value, "tp", perm)


def send_core(value):
    return lax.ppermute(value, "tp", [(i, i ^ 1) for i in range(2 * RING)])


def ring_gather(value, send):
    half = value.shape[0] // 2
    before = send(value, 1)
    after = send(value, -1)
    far_low = send(before[:half], 1)
    far_high = send(after[half:], -1)
    return value, before, after, far_low, far_high


def add_to(piece, part, at):
    total = (lax.slice_in_dim(piece, at, at + part.shape[0]).astype(F32) + part.astype(F32)).astype(BF16)
    return lax.dynamic_update_slice_in_dim(piece, total, at, 0)


def scatter_far(pieces, send):
    own, before, after, far_low, far_high = pieces
    after = add_to(after, send(far_low, 1), 0)
    before = add_to(before, send(far_high, -1), far_low.shape[0])
    return own, before, after


def scatter_near(pieces, send):
    own, before, after = pieces
    return own, send(after, 1), send(before, -1)


def ring_scatter(pieces, send):
    return scatter_near(scatter_far(pieces, send), send)


def direct_scatter(pieces, send):
    own, before, after, far = pieces
    return own, send(before, -1), send(after, 1), send(far, 2)


def total(parts):
    return sum(part.astype(F32) for part in parts)


def dot_nn(a, b):
    return jnp.dot(a, b, preferred_element_type=F32)


def dot_nt(a, b):
    return lax.dot_general(a, b, (((1,), (1,)), ((), ())), preferred_element_type=F32)


def dot_tn(a, b):
    return lax.dot_general(a, b, (((0,), (0,)), ((), ())), preferred_element_type=F32)


def small_call(body, name, out_shape, scalars, operands):
    return pl.pallas_call(
        body,
        out_shape=out_shape,
        in_specs=smem(len(scalars)) + whole(len(operands)),
        out_specs=whole(len(out_shape)),
        compiler_params=pltpu.CompilerParams(vmem_limit_bytes=SMALL_LIMIT),
        cost_estimate=pl.CostEstimate(flops=2_000_000, bytes_accessed=2_000_000, transcendentals=0),
        name=name,
    )(*scalars, *operands)


def place_kernel(owners, patches, out, sems):
    copies = [
        pltpu.make_async_copy(patches.at[k], out.at[owners[k]], sems.at[k])
        for k in range(16)
    ]
    for copy in copies:
        copy.start()
    for copy in copies:
        copy.wait()


def place_patches(owners, patches):
    return pl.pallas_call(
        place_kernel,
        out_shape=jax.ShapeDtypeStruct(patches.shape, BF16),
        in_specs=smem(1) + in_hbm(1),
        out_specs=whole(1)[0],
        scratch_shapes=[pltpu.SemaphoreType.DMA((16,))],
        compiler_params=pltpu.CompilerParams(vmem_limit_bytes=SMALL_LIMIT),
        cost_estimate=pl.CostEstimate(flops=0, bytes_accessed=500_000, transcendentals=0),
        name="place_patches",
    )(owners, *from_hbm(patches))


def take_kernel(owners, returned, out):
    for k in range(16):
        out[k] = returned[owners[k]]


def move_patches(body, name, owners, patches):
    shape = [jax.ShapeDtypeStruct(patches.shape, BF16)]
    return small_call(body, name, shape, (owners,), (patches,))[0]


QUERY, KEY, VALUE, COT = (slice(i * HD, (i + 1) * HD) for i in range(4))
CHUNK = 1024
CHUNKS = 4096 // CHUNK


def pack(acc, cot, z_out, y_out):
    for head, cols, out in ((0, (0, 3, 5), z_out), (1, (1, 2, 4), y_out)):
        for at, col in enumerate(cols):
            out[:, at * HD : (at + 1) * HD] = acc[:, col * HD : (col + 1) * HD].astype(BF16)
        out[:, COT] = cot[:, head * HD : (head + 1) * HD]


def block_rows(slices, j):
    return pl.ds(pl.multiple_of(slices[j] * SEQ, SEQ), SEQ)


def stream(weights, held, sems, depths):
    groups = []
    for j, depth in enumerate(depths):
        groups.append(
            [
                pltpu.make_async_copy(
                    ref.at[depth], held.at[depth, i * 256 : (i + 1) * 256], sems.at[j, i]
                )
                for i, ref in enumerate(weights)
            ]
        )
    for group in groups:
        for copy in group:
            copy.start()
    return groups


def multiply(block_of, depths, weights, cot, flipped, z_out, y_out, held, turned, sems):
    groups = stream(weights, held, sems, depths)
    acc = None
    outgoing = []
    for j, (depth, group) in enumerate(zip(depths, groups)):
        block = block_of(j)
        turned[depth, :] = block.T
        copy = pltpu.make_async_copy(turned.at[depth], flipped.at[depth], sems.at[j, 3])
        copy.start()
        outgoing.append(copy)
        for copy in group:
            copy.wait()
        term = dot_nn(block, held[depth, :])
        acc = term if acc is None else acc + term
    pack(acc, cot, z_out, y_out)
    for copy in outgoing:
        copy.wait()


def text_kernel(slices, own, oth, cot, wq, wk, wv, flipped, z_out, y_out, held, turned, sems):
    def block_of(j):
        part = own if j < RING else oth
        return part[:, (j % RING) * SEQ : (j % RING + 1) * SEQ]

    depths = [block_rows(slices, j) for j in range(8)]
    outs = (flipped, z_out, y_out, held, turned, sems)
    multiply(block_of, depths, (wq, wk, wv), cot[:PATCH], *outs)


def image_kernel(own, oth, cot, wq, wk, wv, flipped, z_out, y_out, held, turned, sems):
    depths = [slice(j * SEQ, (j + 1) * SEQ) for j in range(8)]

    def block_of(j):
        return jnp.concatenate([own[:, depths[j]], oth[:, depths[j]]], axis=0)

    outs = (flipped, z_out, y_out, held, turned, sems)
    multiply(block_of, depths, (wq, wk, wv), cot[PATCH:], *outs)


def from_hbm(*arrays):
    return [pltpu.with_memory_space_constraint(array, pltpu.HBM) for array in arrays]


def project(body, name, scalars, own, oth, cot, weights):
    return pl.pallas_call(
        body,
        out_shape=[pltpu.HBM((4096, PATCH), BF16)]
        + [jax.ShapeDtypeStruct((PATCH, 4 * HD), BF16)] * 2,
        in_specs=smem(len(scalars)) + whole(3) + in_hbm(3),
        out_specs=in_hbm(1) + whole(2),
        scratch_shapes=[
            pltpu.VMEM((4096, 6 * HD), BF16),
            pltpu.VMEM((4096, PATCH), BF16),
            pltpu.SemaphoreType.DMA((8, 4)),
        ],
        compiler_params=pltpu.CompilerParams(vmem_limit_bytes=STREAM_LIMIT),
        cost_estimate=pl.CostEstimate(
            flops=2 * PATCH * 4096 * 768, bytes_accessed=8_000_000, transcendentals=0
        ),
        name=name,
    )(*scalars, own, oth, cot, *from_hbm(*weights))


def ranks(off, shape, dim):
    index = lax.broadcasted_iota(jnp.int32, shape, dim)
    return jnp.where(index < PATCH, 2 * index, 2 * off - 1)


def diagonal_mask(off):
    return ranks(off, (SEQ, 1), 0) <= ranks(off, (1, SEQ), 1)


def fetch(refs, blocks, sems, y, z):
    copies = []
    for base, at, parts in ((0, z, refs[0:8]), (RING, y, refs[8:16])):
        for rel, off in enumerate(OFFSETS):
            slot = base + lax.rem(at + off, RING)
            for half in range(2):
                target = blocks.at[slot, half * PATCH : (half + 1) * PATCH]
                part = parts[2 * rel + half]
                copies.append(pltpu.make_async_copy(part, target, sems.at[len(copies)]))
    first = copies[0:2] + copies[8:10]
    rest = copies[2:8] + copies[10:]
    for copy in first + rest:
        copy.start()
    return first, rest


def own_pairs(meta, advance):
    y, z, off = meta[0], meta[1], meta[2]
    advance([(z, RING + y), (RING + y, z)], diagonal_mask(off))


def other_pairs(table, advance):
    def step(i, carry):
        codes = [table[3 * i + j] for j in range(3)]
        advance([(lax.div(code, 8), lax.rem(code, 8)) for code in codes], None)
        return carry

    lax.fori_loop(0, 5, step, 0)


def flip_all(dest, blocks, cols):
    for i in range(2 * RING):
        dest[i] = blocks[i, :, cols].T


def flip_own(dest, blocks, cols, y, z):
    dest[z] = blocks[z, :, cols].T
    dest[RING + y] = blocks[RING + y, :, cols].T


def stats_kernel(meta, table, *refs):
    z_out, y_out, o_out, blocks, vt, top, total, sems = refs[16:]
    y, z = meta[0], meta[1]
    first, rest = fetch(refs, blocks, sems, y, z)
    top[...] = jnp.full_like(top, NEG_LARGE)
    total[...] = jnp.zeros_like(total)
    o_out[...] = jnp.zeros_like(o_out)

    def advance(pairs, allowed):
        scores = [dot_nt(blocks[k, :, KEY], blocks[q, :, QUERY]) * (SCALE * LOG2E) for q, k in pairs]
        if allowed is not None:
            scores = [jnp.where(allowed, score, NEG_LARGE) for score in scores]
        highs = [jnp.max(score, axis=0, keepdims=True) for score in scores]
        for (q, k), score, high in zip(pairs, scores, highs):
            old = top[q]
            new = jnp.maximum(old, high)
            probs = jnp.exp2(score - new)
            shrink = jnp.exp2(old - new)
            top[q] = new
            total[q] = total[q] * shrink + jnp.sum(probs, axis=0, keepdims=True)
            o_out[q] = o_out[q] * shrink + dot_nn(vt[k], probs.astype(BF16))

    for copy in first:
        copy.wait()
    flip_own(vt, blocks, VALUE, y, z)
    own_pairs(meta, advance)
    for copy in rest:
        copy.wait()
    flip_all(vt, blocks, VALUE)
    other_pairs(table, advance)
    for head, out in ((0, z_out), (1, y_out)):
        for i in range(RING):
            at = head * RING + i
            count = total[at]
            some = count > 0.0
            safe = jnp.where(some, count, 1.0)
            partial = o_out[at] / safe
            o_out[at] = partial
            flipped = blocks[at, :, COT].astype(F32).T
            out[i : i + 1, :] = jnp.where(some, top[at] + jnp.log(safe) * LOG2E, NEG_LARGE)
            out[RING + i : RING + i + 1, :] = jnp.sum(partial * flipped, axis=0, keepdims=True)


def whole(count):
    return [pl.BlockSpec(memory_space=pltpu.VMEM)] * count


def in_hbm(count):
    return [pl.BlockSpec(memory_space=pltpu.HBM)] * count


def smem(count):
    return [pl.BlockSpec(memory_space=pltpu.SMEM)] * count


def attention_stats(meta, table, pieces):
    row = pltpu.VMEM((2 * RING, 1, SEQ), F32)
    return pl.pallas_call(
        stats_kernel,
        out_shape=[jax.ShapeDtypeStruct((2 * RING, SEQ), F32)] * 2
        + [jax.ShapeDtypeStruct((2 * RING, HD, SEQ), F32)],
        in_specs=smem(2) + in_hbm(16),
        out_specs=whole(3),
        scratch_shapes=[
            pltpu.VMEM((2 * RING, SEQ, 4 * HD), BF16),
            pltpu.VMEM((2 * RING, HD, SEQ), BF16),
            row,
            row,
            pltpu.SemaphoreType.DMA((16,)),
        ],
        compiler_params=pltpu.CompilerParams(vmem_limit_bytes=STATS_LIMIT),
        cost_estimate=pl.CostEstimate(
            flops=17 * 2 * 2 * SEQ * SEQ * HD,
            bytes_accessed=5_000_000,
            transcendentals=17 * SEQ * SEQ,
        ),
        name="stats",
    )(meta, table, *pieces)


def grads_kernel(meta, table, *refs):
    o_part = refs[16]
    stats = (refs[17:21], refs[21:25])
    outs = refs[25:35]
    blocks, kt, lse, dots, keep, dq_sum, dk_sum, dv_sum, sems = refs[35:]
    y, z = meta[0], meta[1]
    first, rest = fetch(refs, blocks, sems, y, z)
    dq_sum[...] = jnp.zeros_like(dq_sum)
    dk_sum[...] = jnp.zeros_like(dk_sum)
    dv_sum[...] = jnp.zeros_like(dv_sum)
    for head in range(2):
        parts = [ref[...] for ref in stats[head]]
        logs = [part[:RING] for part in parts]
        top = functools.reduce(jnp.maximum, logs)
        shares = [jnp.exp2(log - top) for log in logs]
        norm = sum(shares)
        full = top + jnp.log(norm) * LOG2E
        dot = sum(share * part[RING:] for share, part in zip(shares, parts)) / norm
        weight = jnp.exp2(logs[0] - full)
        for i in range(RING):
            lse[head * RING + i] = full[i : i + 1]
            dots[head * RING + i] = dot[i : i + 1]
            keep[head * RING + i] = weight[i : i + 1]

    def advance(pairs, allowed):
        for q, k in pairs:
            query, cot = blocks[q, :, QUERY], blocks[q, :, COT]
            probs = jnp.exp2(dot_nt(blocks[k, :, KEY], query) * (SCALE * LOG2E) - lse[q])
            if allowed is not None:
                probs = jnp.where(allowed, probs, 0.0)
            prob_grads = dot_nt(blocks[k, :, VALUE], cot)
            slope = (probs * (prob_grads - dots[q]) * SCALE).astype(BF16)
            dv_sum[k] += dot_nn(probs.astype(BF16), cot)
            dk_sum[k] += dot_nn(slope, query)
            dq_sum[q] += dot_nn(kt[k], slope)

    for copy in first:
        copy.wait()
    flip_own(kt, blocks, KEY, y, z)
    own_pairs(meta, advance)
    for copy in rest:
        copy.wait()
    flip_all(kt, blocks, KEY)
    other_pairs(table, advance)
    half = SEQ // 2
    for base, at, parts in ((0, z, outs[:5]), (RING, y, outs[5:])):
        for rel, shift in enumerate(OFFSETS):
            slot = base + lax.rem(at + shift, RING)
            terms = (
                dq_sum[slot].T.astype(BF16),
                dk_sum[slot].astype(BF16),
                dv_sum[slot].astype(BF16),
                (o_part[slot] * keep[slot]).T.astype(BF16),
            )
            for cols, term in zip((QUERY, KEY, VALUE, COT), terms):
                if rel < 3:
                    parts[rel][:, cols] = term
                else:
                    parts[3][:, cols] = term[:half]
                    parts[4][:, cols] = term[half:]


def attention_grads(meta, table, pieces, o_part, z_stats, y_stats):
    row = pltpu.VMEM((2 * RING, 1, SEQ), F32)
    tall = pltpu.VMEM((2 * RING, SEQ, HD), F32)
    flat = pltpu.VMEM((2 * RING, HD, SEQ), F32)
    full = jax.ShapeDtypeStruct((SEQ, 4 * HD), BF16)
    half = jax.ShapeDtypeStruct((SEQ // 2, 4 * HD), BF16)
    return pl.pallas_call(
        grads_kernel,
        out_shape=([full] * 3 + [half] * 2) * 2,
        in_specs=smem(2) + in_hbm(16) + whole(9),
        out_specs=whole(10),
        scratch_shapes=[
            pltpu.VMEM((2 * RING, SEQ, 4 * HD), BF16),
            pltpu.VMEM((2 * RING, HD, SEQ), BF16),
            row,
            row,
            row,
            flat,
            tall,
            tall,
            pltpu.SemaphoreType.DMA((16,)),
        ],
        compiler_params=pltpu.CompilerParams(vmem_limit_bytes=GRADS_LIMIT),
        cost_estimate=pl.CostEstimate(
            flops=17 * 5 * 2 * SEQ * SEQ * HD,
            bytes_accessed=10_000_000,
            transcendentals=17 * SEQ * SEQ,
        ),
        name="grads",
    )(meta, table, *pieces, o_part, *z_stats, *y_stats)


def tail_kernel(meta, slices, *refs):
    text, image = refs[6:8]
    weights = refs[8:11]
    gz, gy, own, oth, oth_before, oth_far = refs[11:17]
    z_parts, y_parts = refs[17:21], refs[21:25]
    held, products, sems = refs[25:]
    y, z = meta[0], meta[1]
    depths = [block_rows(slices, j) for j in range(8)]
    groups = stream(weights, held, sems, depths)
    for parts, grads in ((refs[:3], gz), (refs[3:6], gy)):
        grads[...] = total([part[...] for part in parts]).astype(BF16)
    width = 3 * HD
    rows = 256
    grads = jnp.concatenate([gz[:, :width], gy[:, :width]], axis=1)
    for rel, shift in enumerate(OFFSETS):
        depth = pl.ds(pl.multiple_of(lax.rem(y + shift, RING) * CHUNK, CHUNK), CHUNK)
        term = dot_nn(text[depth, :], grads[:PATCH]) + dot_nn(image[depth, :], grads[PATCH:])
        products[...] = term.astype(BF16)
        for other, other_shift in enumerate(OFFSETS):
            source = pl.ds(pl.multiple_of(lax.rem(z + other_shift, RING) * rows, rows), rows)
            z_parts[rel][other * rows : (other + 1) * rows, :] = products[source, :width]
            y_parts[other][rel * rows : (rel + 1) * rows, :] = products[source, width:]

    columns = [ref[:, cols] for cols in (QUERY, KEY, VALUE) for ref in (gz, gy)]
    columns = [columns[i] for i in (0, 1, 3, 2, 5, 4)]
    grads = jnp.concatenate(columns, axis=1)
    pieces = [own.at[i] for i in range(RING)]
    pieces += [oth.at[0], oth_before, oth.at[1], oth_far]
    for j, (depth, group) in enumerate(zip(depths, groups)):
        for copy in group:
            copy.wait()
        term = dot_nt(grads, held[depth, :]).astype(BF16)
        pieces[j][:PATCH] = term[:PATCH]
        at = pl.ds(pl.multiple_of(PATCH + slices[j] * 32, 32), 32)
        for i, piece in enumerate(pieces):
            piece[at, :] = term[PATCH + 32 * i : PATCH + 32 * (i + 1)]


def tail_grads(meta, slices, z_parts, y_parts, text, image, weights):
    piece = jax.ShapeDtypeStruct((CHUNK, 3 * HD), BF16)
    return pl.pallas_call(
        tail_kernel,
        out_shape=[jax.ShapeDtypeStruct((SEQ, 4 * HD), BF16)] * 2
        + [jax.ShapeDtypeStruct((RING, SEQ, SEQ), BF16)]
        + [jax.ShapeDtypeStruct((2, SEQ, SEQ), BF16)]
        + [jax.ShapeDtypeStruct((SEQ, SEQ), BF16)] * 2
        + [piece] * 8,
        in_specs=smem(2) + whole(8) + in_hbm(3),
        out_specs=whole(14),
        scratch_shapes=[
            pltpu.VMEM((4096, 6 * HD), BF16),
            pltpu.VMEM((CHUNK, 6 * HD), BF16),
            pltpu.SemaphoreType.DMA((8, 3)),
        ],
        compiler_params=pltpu.CompilerParams(vmem_limit_bytes=STREAM_LIMIT),
        cost_estimate=pl.CostEstimate(
            flops=4 * SEQ * 4096 * 768, bytes_accessed=8_000_000, transcendentals=0
        ),
        name="tail_grads",
    )(meta, slices, *z_parts, *y_parts, text, image, *from_hbm(*weights))


def x_before_kernel(kept, got, out):
    out[...] = total((kept[1], got[...])).astype(BF16)


def x_far_kernel(kept, got, out):
    out[...] = total((kept[3], got[...])).astype(BF16)


def x_rest_kernel(kept, got, own, after):
    own[...] = total((kept[0], got[0])).astype(BF16)
    after[...] = total((kept[2], got[1])).astype(BF16)


def split_kernel(*refs):
    for parts, outs in ((refs[:3], refs[6:10]), (refs[3:6], refs[10:14])):
        for i, out in enumerate(outs):
            rows = slice(i * 256, (i + 1) * 256)
            out[...] = total([part[rows] for part in parts]).astype(out.dtype)


def split_phase(z_sum, y_sum):
    own = jax.ShapeDtypeStruct((256, 3 * HD), F32)
    other = jax.ShapeDtypeStruct((256, 3 * HD), BF16)
    outs = small_call(split_kernel, "split", [own, other, other, other] * 2, (), (*z_sum, *y_sum))
    return outs[:4], outs[4:]


def mixed_kernel(meta, own, before, after, text_out, image_out):
    off = meta[2]
    grads = total((own[...], before[...], after[...])).astype(BF16).astype(F32)
    text = grads[:PATCH]
    row = lax.broadcasted_iota(jnp.int32, (PATCH, 1), 0)
    text_out[:PATCH] = jnp.where(row < off, text, 0.0).astype(BF16)
    text_out[PATCH:] = jnp.where(row < off, 0.0, text).astype(BF16)
    for i in range(8):
        rows = slice(PATCH + 32 * i, PATCH + 32 * (i + 1))
        image_out[:, i * SEQ : (i + 1) * SEQ] = grads[rows].astype(BF16)


def mixed_grads(meta, parts):
    shapes = [jax.ShapeDtypeStruct((SEQ, SEQ), BF16), jax.ShapeDtypeStruct((32, 4096), BF16)]
    return small_call(mixed_kernel, "mixed_grads", shapes, (meta,), parts)


def final_kernel(*refs):
    z_sum = total([ref[...] for ref in refs[:4]])
    y_sum = total([ref[...] for ref in refs[4:8]])
    for cols, out, first, second in (
        (QUERY, refs[8], z_sum, y_sum),
        (KEY, refs[9], y_sum, z_sum),
        (VALUE, refs[10], y_sum, z_sum),
    ):
        out[:, :HD] = first[:, cols]
        out[:, HD:] = second[:, cols]


def final_sums(z_parts, y_parts):
    shape = jax.ShapeDtypeStruct((256, 2 * HD), F32)
    return small_call(final_kernel, "final_sums", [shape] * 3, (), (*z_parts, *y_parts))


def local(text_hidden, patch_rows, image_start, w_query, w_key, w_value, d_attn):
    ctx = lax.axis_index("ctx")
    y, z = ctx // RING, ctx % RING
    images, pieces, width = patch_rows.shape
    owners = image_start // SEQ
    off = jnp.sum(jnp.where(owners == ctx, image_start, 0)) - ctx * SEQ
    meta = jnp.stack([y, z, off]).astype(jnp.int32)
    table = lax.dynamic_index_in_dim(jnp.asarray(pair_table()), ctx, 0, keepdims=False)

    tp = lax.axis_index("tp")
    x, core = tp // 2, tp % 2
    columns = (x + jnp.asarray(OFFSETS, jnp.int32)) % RING
    slices = jnp.concatenate([columns * 2 + core, columns * 2 + 1 - core]).astype(jnp.int32)

    index = jnp.arange(SEQ, dtype=jnp.int32)
    rel = (index - PATCH) // 32
    shift = rel % RING
    shift = jnp.where(shift == 0, 0, jnp.where(shift == 1, 3, shift - 1))
    sender = 2 * ((x + shift) % RING) + jnp.where(rel < RING, core, 1 - core)
    text_pos = jnp.where(index < off, index, index + PATCH)
    image_pos = off + 16 * ((index % 32) // 2) + 2 * sender + index % 2
    pos = jnp.where(index < PATCH, text_pos, image_pos)
    placed = (index[:, None] == pos[None, :]).astype(BF16)

    by_shard = place_patches(owners, patch_rows)
    by_shard, text_hidden = lax.optimization_barrier((by_shard, text_hidden))
    arrived = lax.all_to_all(by_shard, "ctx", split_axis=0, concat_axis=0, tiled=True)
    kept = index[:PATCH, None] < off
    text = jnp.where(kept, text_hidden[:PATCH], text_hidden[PATCH:])
    t_ring = ring_gather(text, send_x)
    arrived, t_ring = lax.optimization_barrier((arrived, t_ring))
    t_far = jnp.concatenate(t_ring[3:], axis=0)
    t_own = jnp.concatenate([*t_ring[:3], t_far], axis=1)
    t_oth = send_core(t_own)

    image = arrived.reshape(images * pieces, width)
    before, after = send_x(image, 1), send_x(image, -1)
    cot = dot_tn(placed, d_attn).astype(BF16)
    weights = (w_query, w_key, w_value)
    half = image.shape[0] // 2
    far = (send_x(before[:half], 1), send_x(after[half:], -1))
    i_own = jnp.concatenate([image, before, after, *far], axis=0)
    i_oth = send_core(i_own)

    text_flipped, z_text, y_text = project(
        text_kernel, "qkv_text", (slices,), t_own, t_oth, cot, weights
    )
    image_flipped, z_image, y_image = project(
        image_kernel, "qkv_image", (), i_own, i_oth, cot, weights
    )

    z_before, z_after = send_z(z_text, 1), send_z(z_text, -1)
    y_before, y_after = send_y(y_text, 1), send_y(y_text, -1)
    z_before, y_before, z_image = lax.optimization_barrier((z_before, y_before, z_image))
    z_image_before, z_image_after = send_z(z_image, 1), send_z(z_image, -1)
    y_image_before, y_image_after = send_y(y_image, 1), send_y(y_image, -1)
    z_ring = (z_text, z_image, z_before, z_image_before, z_after, z_image_after)
    z_ring += (send_z(z_before, 1), send_z(z_image_after, -1))
    y_ring = (y_text, y_image, y_before, y_image_before, y_after, y_image_after)
    y_ring += (send_y(y_before, 1), send_y(y_image_after, -1))
    operands = (*z_ring, *y_ring)
    z_stats, y_stats, o_part = attention_stats(meta, table, operands)
    z_stats = [z_stats] + [send_z(z_stats, step) for step in (1, -1, 2)]
    y_stats = [y_stats] + [send_y(y_stats, step) for step in (1, -1, 2)]
    outs = attention_grads(meta, table, operands, o_part, z_stats, y_stats)
    z_parts, y_parts = ring_scatter(outs[:5], send_z), ring_scatter(outs[5:], send_y)
    gz, gy, kept_part, sent_part, sent_before, sent_far, *parts = tail_grads(
        meta, slices, z_parts, y_parts, text_flipped, image_flipped, weights
    )
    x_shape = jax.ShapeDtypeStruct((SEQ, SEQ), BF16)
    got_far, got_before, got_part = send_core(sent_far), send_core(sent_before), send_core(sent_part)
    z_own, z_before, z_after, z_far = parts[:4]
    y_own, y_before, y_after, y_far = parts[4:]
    z_far, y_far = send_y(z_far, 1), send_z(y_far, 1)
    (x_far,) = small_call(x_far_kernel, "x_far", [x_shape], (), (kept_part, got_far))
    (x_before,) = small_call(x_before_kernel, "x_before", [x_shape], (), (kept_part, got_before))
    x_far, x_before = send_x(x_far, 1), send_x(x_before, -1)
    x_own, x_after = small_call(x_rest_kernel, "x_rest", [x_shape] * 2, (), (kept_part, got_part))
    x_after, z_before = lax.optimization_barrier((x_after, z_before))
    z_before = send_y(z_before, -1)
    z_far, y_far, y_before = lax.optimization_barrier((z_far, y_far, y_before))
    z_sum = (z_own, send_y(total((z_after, z_far)).astype(BF16), 1), z_before)
    y_sum = (y_own, send_z(total((y_after, y_far)).astype(BF16), 1), send_z(y_before, -1))
    x_after = send_x(total((x_after, x_far)).astype(BF16), 1)
    d_text, i_grad = mixed_grads(meta, (x_own, x_after, x_before))
    z_sum, y_sum, i_grad = lax.optimization_barrier((z_sum, y_sum, i_grad))

    attended = jnp.concatenate([gz[:, COT], gy[:, COT]], axis=1)
    attn_out = dot_nn(placed, attended).astype(BF16)

    returned = lax.all_to_all(
        i_grad.reshape(images, pieces, width), "ctx", split_axis=0, concat_axis=0, tiled=True
    )
    d_patch = move_patches(take_kernel, "take_patches", owners, returned)
    z_pieces, y_pieces = split_phase(z_sum, y_sum)
    dw_query, dw_key, dw_value = final_sums(
        direct_scatter(z_pieces, send_z), direct_scatter(y_pieces, send_y)
    )
    return (
        attn_out,
        d_text,
        d_patch,
        dw_query,
        dw_key,
        dw_value,
    )


def solution(mesh):
    in_specs = (
        P("ctx", "tp"),
        P(None, ("ctx", "tp"), None),
        P(),
        P(None, "tp"),
        P(None, "tp"),
        P(None, "tp"),
        P("ctx", "tp"),
    )
    out_specs = (
        P("ctx", "tp"),
        P("ctx", "tp"),
        P(None, ("ctx", "tp"), None),
        P("ctx", "tp"),
        P("ctx", "tp"),
        P("ctx", "tp"),
    )
    return jax.shard_map(local, mesh=mesh, in_specs=in_specs, out_specs=out_specs, check_vma=False)
```

```python
import functools
import math

import jax
import jax.numpy as jnp
import numpy as np
from jax import lax
from jax.experimental import pallas as pl
from jax.experimental.pallas import tpu as pltpu
from jax.sharding import PartitionSpec as P

HD = 128
PATCH = 256
SEQ = 512
RING = 4
OFFSETS = (0, 3, 1, 2)
NEG_LARGE = -1e30
SCALE = 1.0 / math.sqrt(HD)
LOG2E = math.log2(math.e)
SMALL_LIMIT = 8 * 1024 * 1024
STREAM_LIMIT = 15 * 1024 * 1024
STATS_LIMIT = 16 * 1024 * 1024
GRADS_LIMIT = 22 * 1024 * 1024
Z_GROUPS = [[RING * y + z for z in range(RING)] for y in range(RING)]
Y_GROUPS = [[RING * y + z for y in range(RING)] for z in range(RING)]
BF16 = jnp.bfloat16
F32 = jnp.float32


def pair_table():
    rows = []
    for ctx in range(RING * RING):
        y, z = divmod(ctx, RING)
        own = []
        for q in range(RING):
            for k in range(RING):
                if RING * k + z < RING * y + q:
                    own.append(8 * q + RING + k)
                if RING * y + k < RING * q + z:
                    own.append(8 * (RING + q) + k)
        assert len(own) == 15
        rows.append(own)
    return np.asarray(rows, np.int32)


def ctx_send(value, dy, dz):
    perm = [
        (RING * y + z, RING * ((y + dy) % RING) + (z + dz) % RING)
        for y in range(RING)
        for z in range(RING)
    ]
    return lax.ppermute(value, "ctx", perm)


def send_z(value, step):
    return ctx_send(value, 0, step)


def send_y(value, step):
    return ctx_send(value, step, 0)


def send_x(value, step):
    perm = [(2 * x + core, 2 * ((x + step) % RING) + core) for x in range(RING) for core in range(2)]
    return lax.ppermute(value, "tp", perm)


def send_core(value):
    return lax.ppermute(value, "tp", [(i, i ^ 1) for i in range(2 * RING)])


def ring_gather(value, send):
    half = value.shape[0] // 2
    before = send(value, 1)
    after = send(value, -1)
    far_low = send(before[:half], 1)
    far_high = send(after[half:], -1)
    return value, before, after, far_low, far_high


def add_to(piece, part, at):
    total = (lax.slice_in_dim(piece, at, at + part.shape[0]).astype(F32) + part.astype(F32)).astype(BF16)
    return lax.dynamic_update_slice_in_dim(piece, total, at, 0)


def scatter_far(pieces, send):
    own, before, after, far_low, far_high = pieces
    after = add_to(after, send(far_low, 1), 0)
    before = add_to(before, send(far_high, -1), far_low.shape[0])
    return own, before, after


def scatter_near(pieces, send):
    own, before, after = pieces
    return own, send(after, 1), send(before, -1)


def ring_scatter(pieces, send):
    return scatter_near(scatter_far(pieces, send), send)


def direct_scatter(pieces, send):
    own, before, after, far = pieces
    return own, send(before, -1), send(after, 1), send(far, 2)


def total(parts):
    return sum(part.astype(F32) for part in parts)


def dot_nn(a, b):
    return jnp.dot(a, b, preferred_element_type=F32)


def dot_nt(a, b):
    return lax.dot_general(a, b, (((1,), (1,)), ((), ())), preferred_element_type=F32)


def dot_tn(a, b):
    return lax.dot_general(a, b, (((0,), (0,)), ((), ())), preferred_element_type=F32)


def small_call(body, name, out_shape, scalars, operands, flops=2_000_000):
    return pl.pallas_call(
        body,
        out_shape=out_shape,
        in_specs=smem(len(scalars)) + whole(len(operands)),
        out_specs=whole(len(out_shape)),
        compiler_params=pltpu.CompilerParams(vmem_limit_bytes=SMALL_LIMIT),
        cost_estimate=pl.CostEstimate(flops=flops, bytes_accessed=2_000_000, transcendentals=0),
        name=name,
    )(*scalars, *operands)


def place_kernel(owners, patches, out, sems):
    copies = [
        pltpu.make_async_copy(patches.at[k], out.at[owners[k]], sems.at[k])
        for k in range(16)
    ]
    for copy in copies:
        copy.start()
    for copy in copies:
        copy.wait()


def place_patches(owners, patches):
    return pl.pallas_call(
        place_kernel,
        out_shape=jax.ShapeDtypeStruct(patches.shape, BF16),
        in_specs=smem(1) + in_hbm(1),
        out_specs=whole(1)[0],
        scratch_shapes=[pltpu.SemaphoreType.DMA((16,))],
        compiler_params=pltpu.CompilerParams(vmem_limit_bytes=SMALL_LIMIT),
        cost_estimate=pl.CostEstimate(flops=0, bytes_accessed=500_000, transcendentals=0),
        name="place_patches",
    )(owners, *from_hbm(patches))


def take_kernel(owners, returned, out):
    for k in range(16):
        out[k] = returned[owners[k]]


def move_patches(body, name, owners, patches):
    shape = [jax.ShapeDtypeStruct(patches.shape, BF16)]
    return small_call(body, name, shape, (owners,), (patches,))[0]


QUERY, KEY, VALUE, COT = (slice(i * HD, (i + 1) * HD) for i in range(4))
CHUNK = 1024
CHUNKS = 4096 // CHUNK


def pack(acc, cot, z_out, y_out):
    for head, cols, out in ((0, (0, 3, 5), z_out), (1, (1, 2, 4), y_out)):
        for at, col in enumerate(cols):
            out[:, at * HD : (at + 1) * HD] = acc[:, col * HD : (col + 1) * HD].astype(BF16)
        out[:, COT] = cot[:, head * HD : (head + 1) * HD]


def block_rows(slices, j):
    return pl.ds(pl.multiple_of(slices[j] * SEQ, SEQ), SEQ)


def stream(weights, held, sems, depths):
    groups = []
    for j, depth in enumerate(depths):
        groups.append(
            [
                pltpu.make_async_copy(
                    ref.at[depth], held.at[depth, i * 256 : (i + 1) * 256], sems.at[j, i]
                )
                for i, ref in enumerate(weights)
            ]
        )
    for group in groups:
        for copy in group:
            copy.start()
    return groups


def text_kernel(slices, own, oth, cot, wq, wk, wv, flipped, z_keep, y_keep, z_out, y_out, held, turned, sems):
    depths = [block_rows(slices, j) for j in range(8)]
    groups = stream((wq, wk, wv), held, sems, depths)
    acc = None
    outgoing = []
    for j, (depth, group) in enumerate(zip(depths, groups)):
        part = own if j < RING else oth
        block = part[:, (j % RING) * SEQ : (j % RING + 1) * SEQ]
        turned[depth, :] = block.T
        outgoing.append(pltpu.make_async_copy(turned.at[depth], flipped.at[depth], sems.at[j, 3]))
        outgoing[-1].start()
        for copy in group:
            copy.wait()
        term = dot_nn(block, held[depth, :])
        acc = term if acc is None else acc + term
    pack(acc, cot[:PATCH], z_out, y_out)
    for i, (out, keep) in enumerate(((z_out, z_keep), (y_out, y_keep))):
        outgoing.append(pltpu.make_async_copy(out, keep, sems.at[8, i]))
        outgoing[-1].start()
    for copy in outgoing:
        copy.wait()


def image_kernel(own, oth, cot, held, flipped, z_out, y_out, turned, sems):
    acc = None
    outgoing = []
    for j in range(CHUNKS):
        depth = slice(j * CHUNK, (j + 1) * CHUNK)
        block = jnp.concatenate([own[:, depth], oth[:, depth]], axis=0)
        turned[depth, :] = block.T
        outgoing.append(pltpu.make_async_copy(turned.at[depth], flipped.at[depth], sems.at[j]))
        outgoing[-1].start()
        term = dot_nn(block, held[depth, :])
        acc = term if acc is None else acc + term
    pack(acc, cot[PATCH:], z_out, y_out)
    for copy in outgoing:
        copy.wait()


def from_hbm(*arrays):
    return [pltpu.with_memory_space_constraint(array, pltpu.HBM) for array in arrays]


def project_text(slices, own, oth, cot, weights):
    rows = (PATCH, 4 * HD)
    return pl.pallas_call(
        text_kernel,
        out_shape=[pltpu.HBM((4096, PATCH), BF16)]
        + [pltpu.HBM(rows, BF16)] * 2
        + [jax.ShapeDtypeStruct(rows, BF16)] * 2
        + [jax.ShapeDtypeStruct((4096, 6 * HD), BF16)],
        in_specs=smem(1) + whole(3) + in_hbm(3),
        out_specs=in_hbm(3) + whole(3),
        scratch_shapes=[pltpu.VMEM((4096, PATCH), BF16), pltpu.SemaphoreType.DMA((9, 4))],
        compiler_params=pltpu.CompilerParams(vmem_limit_bytes=SMALL_LIMIT),
        cost_estimate=pl.CostEstimate(
            flops=2 * PATCH * 4096 * 768, bytes_accessed=8_000_000, transcendentals=0
        ),
        name="qkv_text",
    )(slices, own, oth, cot, *from_hbm(*weights))


def project_image(own, oth, cot, held):
    rows = (PATCH, 4 * HD)
    return pl.pallas_call(
        image_kernel,
        out_shape=[pltpu.HBM((4096, PATCH), BF16)] + [jax.ShapeDtypeStruct(rows, BF16)] * 2,
        in_specs=whole(4),
        out_specs=in_hbm(1) + whole(2),
        scratch_shapes=[pltpu.VMEM((4096, PATCH), BF16), pltpu.SemaphoreType.DMA((CHUNKS,))],
        compiler_params=pltpu.CompilerParams(vmem_limit_bytes=SMALL_LIMIT),
        cost_estimate=pl.CostEstimate(
            flops=2 * PATCH * 4096 * 768, bytes_accessed=2_000_000, transcendentals=0
        ),
        name="qkv_image",
    )(own, oth, cot, held)


def ranks(off, shape, dim):
    index = lax.broadcasted_iota(jnp.int32, shape, dim)
    return jnp.where(index < PATCH, 2 * index, 2 * off - 1)


def diagonal_mask(off):
    return ranks(off, (SEQ, 1), 0) <= ranks(off, (1, SEQ), 1)


def fetch(refs, blocks, sems, y, z):
    copies = []
    for base, at, parts in ((0, z, refs[0:8]), (RING, y, refs[8:16])):
        for rel, off in enumerate(OFFSETS):
            slot = base + lax.rem(at + off, RING)
            for half in range(2):
                target = blocks.at[slot, half * PATCH : (half + 1) * PATCH]
                part = parts[2 * rel + half]
                copies.append(pltpu.make_async_copy(part, target, sems.at[len(copies)]))
    first = copies[0:2] + copies[8:10]
    rest = copies[2:8] + copies[10:]
    for copy in first + rest:
        copy.start()
    return first, rest


def own_pairs(meta, advance):
    y, z, off = meta[0], meta[1], meta[2]
    advance([(z, RING + y), (RING + y, z)], diagonal_mask(off))


def other_pairs(table, advance):
    def step(i, carry):
        codes = [table[3 * i + j] for j in range(3)]
        advance([(lax.div(code, 8), lax.rem(code, 8)) for code in codes], None)
        return carry

    lax.fori_loop(0, 5, step, 0)


def flip_all(dest, blocks, cols):
    for i in range(2 * RING):
        dest[i] = blocks[i, :, cols].T


def flip_own(dest, blocks, cols, y, z):
    dest[z] = blocks[z, :, cols].T
    dest[RING + y] = blocks[RING + y, :, cols].T


def stats_kernel(meta, table, *refs):
    z_out, y_out, o_out, blocks, vt, top, total, sems = refs[16:]
    y, z = meta[0], meta[1]
    first, rest = fetch(refs, blocks, sems, y, z)
    top[...] = jnp.full_like(top, NEG_LARGE)
    total[...] = jnp.zeros_like(total)
    o_out[...] = jnp.zeros_like(o_out)

    def advance(pairs, allowed):
        scores = [dot_nt(blocks[k, :, KEY], blocks[q, :, QUERY]) * (SCALE * LOG2E) for q, k in pairs]
        if allowed is not None:
            scores = [jnp.where(allowed, score, NEG_LARGE) for score in scores]
        highs = [jnp.max(score, axis=0, keepdims=True) for score in scores]
        for (q, k), score, high in zip(pairs, scores, highs):
            old = top[q]
            new = jnp.maximum(old, high)
            probs = jnp.exp2(score - new)
            shrink = jnp.exp2(old - new)
            top[q] = new
            total[q] = total[q] * shrink + jnp.sum(probs, axis=0, keepdims=True)
            o_out[q] = o_out[q] * shrink + dot_nn(vt[k], probs.astype(BF16))

    for copy in first:
        copy.wait()
    flip_own(vt, blocks, VALUE, y, z)
    own_pairs(meta, advance)
    for copy in rest:
        copy.wait()
    flip_all(vt, blocks, VALUE)
    other_pairs(table, advance)
    for head, out in ((0, z_out), (1, y_out)):
        for i in range(RING):
            at = head * RING + i
            count = total[at]
            some = count > 0.0
            safe = jnp.where(some, count, 1.0)
            partial = o_out[at] / safe
            o_out[at] = partial
            flipped = blocks[at, :, COT].astype(F32).T
            out[i : i + 1, :] = jnp.where(some, top[at] + jnp.log(safe) * LOG2E, NEG_LARGE)
            out[RING + i : RING + i + 1, :] = jnp.sum(partial * flipped, axis=0, keepdims=True)


def whole(count):
    return [pl.BlockSpec(memory_space=pltpu.VMEM)] * count


def in_hbm(count):
    return [pl.BlockSpec(memory_space=pltpu.HBM)] * count


def smem(count):
    return [pl.BlockSpec(memory_space=pltpu.SMEM)] * count


def attention_stats(meta, table, pieces):
    row = pltpu.VMEM((2 * RING, 1, SEQ), F32)
    return pl.pallas_call(
        stats_kernel,
        out_shape=[jax.ShapeDtypeStruct((2 * RING, SEQ), F32)] * 2
        + [jax.ShapeDtypeStruct((2 * RING, HD, SEQ), F32)],
        in_specs=smem(2) + in_hbm(16),
        out_specs=whole(3),
        scratch_shapes=[
            pltpu.VMEM((2 * RING, SEQ, 4 * HD), BF16),
            pltpu.VMEM((2 * RING, HD, SEQ), BF16),
            row,
            row,
            pltpu.SemaphoreType.DMA((16,)),
        ],
        compiler_params=pltpu.CompilerParams(vmem_limit_bytes=STATS_LIMIT),
        cost_estimate=pl.CostEstimate(
            flops=17 * 2 * 2 * SEQ * SEQ * HD,
            bytes_accessed=5_000_000,
            transcendentals=17 * SEQ * SEQ,
        ),
        name="stats",
    )(meta, table, *pieces)


def grads_kernel(meta, table, *refs):
    o_part = refs[16]
    stats = (refs[17:21], refs[21:25])
    outs = refs[25:35]
    blocks, kt, lse, dots, keep, dq_sum, dk_sum, dv_sum, sems = refs[35:]
    y, z = meta[0], meta[1]
    first, rest = fetch(refs, blocks, sems, y, z)
    dq_sum[...] = jnp.zeros_like(dq_sum)
    dk_sum[...] = jnp.zeros_like(dk_sum)
    dv_sum[...] = jnp.zeros_like(dv_sum)
    for head in range(2):
        parts = [ref[...] for ref in stats[head]]
        logs = [part[:RING] for part in parts]
        top = functools.reduce(jnp.maximum, logs)
        shares = [jnp.exp2(log - top) for log in logs]
        norm = sum(shares)
        full = top + jnp.log(norm) * LOG2E
        dot = sum(share * part[RING:] for share, part in zip(shares, parts)) / norm
        weight = jnp.exp2(logs[0] - full)
        for i in range(RING):
            lse[head * RING + i] = full[i : i + 1]
            dots[head * RING + i] = dot[i : i + 1]
            keep[head * RING + i] = weight[i : i + 1]

    def advance(pairs, allowed):
        for q, k in pairs:
            query, cot = blocks[q, :, QUERY], blocks[q, :, COT]
            probs = jnp.exp2(dot_nt(blocks[k, :, KEY], query) * (SCALE * LOG2E) - lse[q])
            if allowed is not None:
                probs = jnp.where(allowed, probs, 0.0)
            prob_grads = dot_nt(blocks[k, :, VALUE], cot)
            slope = (probs * (prob_grads - dots[q]) * SCALE).astype(BF16)
            dv_sum[k] += dot_nn(probs.astype(BF16), cot)
            dk_sum[k] += dot_nn(slope, query)
            dq_sum[q] += dot_nn(kt[k], slope)

    for copy in first:
        copy.wait()
    flip_own(kt, blocks, KEY, y, z)
    own_pairs(meta, advance)
    for copy in rest:
        copy.wait()
    flip_all(kt, blocks, KEY)
    other_pairs(table, advance)
    half = SEQ // 2
    for base, at, parts in ((0, z, outs[:5]), (RING, y, outs[5:])):
        for rel, shift in enumerate(OFFSETS):
            slot = base + lax.rem(at + shift, RING)
            terms = (
                dq_sum[slot].T.astype(BF16),
                dk_sum[slot].astype(BF16),
                dv_sum[slot].astype(BF16),
                (o_part[slot] * keep[slot]).T.astype(BF16),
            )
            for cols, term in zip((QUERY, KEY, VALUE, COT), terms):
                if rel < 3:
                    parts[rel][:, cols] = term
                else:
                    parts[3][:, cols] = term[:half]
                    parts[4][:, cols] = term[half:]


def attention_grads(meta, table, pieces, o_part, z_stats, y_stats):
    row = pltpu.VMEM((2 * RING, 1, SEQ), F32)
    tall = pltpu.VMEM((2 * RING, SEQ, HD), F32)
    flat = pltpu.VMEM((2 * RING, HD, SEQ), F32)
    full = jax.ShapeDtypeStruct((SEQ, 4 * HD), BF16)
    half = jax.ShapeDtypeStruct((SEQ // 2, 4 * HD), BF16)
    return pl.pallas_call(
        grads_kernel,
        out_shape=([full] * 3 + [half] * 2) * 2,
        in_specs=smem(2) + in_hbm(16) + whole(9),
        out_specs=whole(10),
        scratch_shapes=[
            pltpu.VMEM((2 * RING, SEQ, 4 * HD), BF16),
            pltpu.VMEM((2 * RING, HD, SEQ), BF16),
            row,
            row,
            row,
            flat,
            tall,
            tall,
            pltpu.SemaphoreType.DMA((16,)),
        ],
        compiler_params=pltpu.CompilerParams(vmem_limit_bytes=GRADS_LIMIT),
        cost_estimate=pl.CostEstimate(
            flops=17 * 5 * 2 * SEQ * SEQ * HD,
            bytes_accessed=10_000_000,
            transcendentals=17 * SEQ * SEQ,
        ),
        name="grads",
    )(meta, table, *pieces, o_part, *z_stats, *y_stats)


def tail_kernel(meta, slices, *refs):
    text, image = refs[6:8]
    weights = refs[8:11]
    gz, gy, own, oth, oth_before, oth_far = refs[11:17]
    z_parts, y_parts = refs[17:21], refs[21:25]
    held, products, sems = refs[25:]
    y, z = meta[0], meta[1]
    depths = [block_rows(slices, j) for j in range(8)]
    groups = stream(weights, held, sems, depths)
    for parts, grads in ((refs[:3], gz), (refs[3:6], gy)):
        grads[...] = total([part[...] for part in parts]).astype(BF16)
    width = 3 * HD
    rows = 256
    grads = jnp.concatenate([gz[:, :width], gy[:, :width]], axis=1)
    for rel, shift in enumerate(OFFSETS):
        depth = pl.ds(pl.multiple_of(lax.rem(y + shift, RING) * CHUNK, CHUNK), CHUNK)
        term = dot_nn(text[depth, :], grads[:PATCH]) + dot_nn(image[depth, :], grads[PATCH:])
        products[...] = term.astype(BF16)
        for other, other_shift in enumerate(OFFSETS):
            source = pl.ds(pl.multiple_of(lax.rem(z + other_shift, RING) * rows, rows), rows)
            z_parts[rel][other * rows : (other + 1) * rows, :] = products[source, :width]
            y_parts[other][rel * rows : (rel + 1) * rows, :] = products[source, width:]

    columns = [ref[:, cols] for cols in (QUERY, KEY, VALUE) for ref in (gz, gy)]
    columns = [columns[i] for i in (0, 1, 3, 2, 5, 4)]
    grads = jnp.concatenate(columns, axis=1)
    pieces = [own.at[i] for i in range(RING)]
    pieces += [oth.at[0], oth_before, oth.at[1], oth_far]
    for j, (depth, group) in enumerate(zip(depths, groups)):
        for copy in group:
            copy.wait()
        term = dot_nt(grads, held[depth, :]).astype(BF16)
        pieces[j][:PATCH] = term[:PATCH]
        at = pl.ds(pl.multiple_of(PATCH + slices[j] * 32, 32), 32)
        for i, piece in enumerate(pieces):
            piece[at, :] = term[PATCH + 32 * i : PATCH + 32 * (i + 1)]


def tail_grads(meta, slices, z_parts, y_parts, text, image, weights):
    piece = jax.ShapeDtypeStruct((CHUNK, 3 * HD), BF16)
    return pl.pallas_call(
        tail_kernel,
        out_shape=[jax.ShapeDtypeStruct((SEQ, 4 * HD), BF16)] * 2
        + [jax.ShapeDtypeStruct((RING, SEQ, SEQ), BF16)]
        + [jax.ShapeDtypeStruct((2, SEQ, SEQ), BF16)]
        + [jax.ShapeDtypeStruct((SEQ, SEQ), BF16)] * 2
        + [piece] * 8,
        in_specs=smem(2) + whole(8) + in_hbm(3),
        out_specs=whole(14),
        scratch_shapes=[
            pltpu.VMEM((4096, 6 * HD), BF16),
            pltpu.VMEM((CHUNK, 6 * HD), BF16),
            pltpu.SemaphoreType.DMA((8, 3)),
        ],
        compiler_params=pltpu.CompilerParams(vmem_limit_bytes=STREAM_LIMIT),
        cost_estimate=pl.CostEstimate(
            flops=4 * SEQ * 4096 * 768, bytes_accessed=8_000_000, transcendentals=0
        ),
        name="tail_grads",
    )(meta, slices, *z_parts, *y_parts, text, image, *from_hbm(*weights))


def x_before_kernel(kept, got, out):
    out[...] = total((kept[1], got[...])).astype(BF16)


def x_far_kernel(kept, got, out):
    out[...] = total((kept[3], got[...])).astype(BF16)


def x_rest_kernel(kept, got, own, after):
    own[...] = total((kept[0], got[0])).astype(BF16)
    after[...] = total((kept[2], got[1])).astype(BF16)


def split_kernel(*refs):
    for parts, outs in ((refs[:3], refs[6:10]), (refs[3:6], refs[10:14])):
        for i, out in enumerate(outs):
            rows = slice(i * 256, (i + 1) * 256)
            out[...] = total([part[rows] for part in parts]).astype(out.dtype)


def split_phase(z_sum, y_sum):
    own = jax.ShapeDtypeStruct((256, 3 * HD), F32)
    other = jax.ShapeDtypeStruct((256, 3 * HD), BF16)
    outs = small_call(split_kernel, "split", [own, other, other, other] * 2, (), (*z_sum, *y_sum))
    return outs[:4], outs[4:]


def mixed_kernel(meta, own, before, after, text_out, image_out):
    off = meta[2]
    grads = total((own[...], before[...], after[...])).astype(BF16).astype(F32)
    text = grads[:PATCH]
    row = lax.broadcasted_iota(jnp.int32, (PATCH, 1), 0)
    text_out[:PATCH] = jnp.where(row < off, text, 0.0).astype(BF16)
    text_out[PATCH:] = jnp.where(row < off, 0.0, text).astype(BF16)
    for i in range(8):
        rows = slice(PATCH + 32 * i, PATCH + 32 * (i + 1))
        image_out[:, i * SEQ : (i + 1) * SEQ] = grads[rows].astype(BF16)


def mixed_grads(meta, parts):
    shapes = [jax.ShapeDtypeStruct((SEQ, SEQ), BF16), jax.ShapeDtypeStruct((32, 4096), BF16)]
    return small_call(mixed_kernel, "mixed_grads", shapes, (meta,), parts, 5_000_000_000)


def final_kernel(*refs):
    z_sum = total([ref[...] for ref in refs[:4]])
    y_sum = total([ref[...] for ref in refs[4:8]])
    for cols, out, first, second in (
        (QUERY, refs[8], z_sum, y_sum),
        (KEY, refs[9], y_sum, z_sum),
        (VALUE, refs[10], y_sum, z_sum),
    ):
        out[:, :HD] = first[:, cols]
        out[:, HD:] = second[:, cols]


def final_sums(z_parts, y_parts):
    shape = jax.ShapeDtypeStruct((256, 2 * HD), F32)
    return small_call(final_kernel, "final_sums", [shape] * 3, (), (*z_parts, *y_parts))


def local(text_hidden, patch_rows, image_start, w_query, w_key, w_value, d_attn):
    ctx = lax.axis_index("ctx")
    y, z = ctx // RING, ctx % RING
    images, pieces, width = patch_rows.shape
    owners = image_start // SEQ
    off = jnp.sum(jnp.where(owners == ctx, image_start, 0)) - ctx * SEQ
    meta = jnp.stack([y, z, off]).astype(jnp.int32)
    table = lax.dynamic_index_in_dim(jnp.asarray(pair_table()), ctx, 0, keepdims=False)

    tp = lax.axis_index("tp")
    x, core = tp // 2, tp % 2
    columns = (x + jnp.asarray(OFFSETS, jnp.int32)) % RING
    slices = jnp.concatenate([columns * 2 + core, columns * 2 + 1 - core]).astype(jnp.int32)

    index = jnp.arange(SEQ, dtype=jnp.int32)
    rel = (index - PATCH) // 32
    shift = rel % RING
    shift = jnp.where(shift == 0, 0, jnp.where(shift == 1, 3, shift - 1))
    sender = 2 * ((x + shift) % RING) + jnp.where(rel < RING, core, 1 - core)
    text_pos = jnp.where(index < off, index, index + PATCH)
    image_pos = off + 16 * ((index % 32) // 2) + 2 * sender + index % 2
    pos = jnp.where(index < PATCH, text_pos, image_pos)
    placed = (index[:, None] == pos[None, :]).astype(BF16)

    by_shard = place_patches(owners, patch_rows)
    by_shard, text_hidden = lax.optimization_barrier((by_shard, text_hidden))
    arrived = lax.all_to_all(by_shard, "ctx", split_axis=0, concat_axis=0, tiled=True)
    kept = index[:PATCH, None] < off
    text = jnp.where(kept, text_hidden[:PATCH], text_hidden[PATCH:])
    t_ring = ring_gather(text, send_x)
    arrived, t_ring = lax.optimization_barrier((arrived, t_ring))
    t_far = jnp.concatenate(t_ring[3:], axis=0)
    t_own = jnp.concatenate([*t_ring[:3], t_far], axis=1)
    t_oth = send_core(t_own)

    image = arrived.reshape(images * pieces, width)
    before, after = send_x(image, 1), send_x(image, -1)
    cot = dot_tn(placed, d_attn).astype(BF16)
    weights = (w_query, w_key, w_value)
    half = image.shape[0] // 2
    far = (send_x(before[:half], 1), send_x(after[half:], -1))
    i_own = jnp.concatenate([image, before, after, *far], axis=0)
    i_oth = send_core(i_own)

    text_flipped, z_keep, y_keep, z_text, y_text, held = project_text(
        slices, t_own, t_oth, cot, weights
    )
    image_flipped, z_image, y_image = project_image(i_own, i_oth, cot, held)
    z_keep, y_keep = from_hbm(z_keep, y_keep)

    z_before, z_after = send_z(z_text, 1), send_z(z_text, -1)
    y_before, y_after = send_y(y_text, 1), send_y(y_text, -1)
    z_before, y_before, z_image = lax.optimization_barrier((z_before, y_before, z_image))
    z_image_before, z_image_after = send_z(z_image, 1), send_z(z_image, -1)
    y_image_before, y_image_after = send_y(y_image, 1), send_y(y_image, -1)
    z_ring = (z_keep, z_image, z_before, z_image_before, z_after, z_image_after)
    z_ring += (send_z(z_before, 1), send_z(z_image_after, -1))
    y_ring = (y_keep, y_image, y_before, y_image_before, y_after, y_image_after)
    y_ring += (send_y(y_before, 1), send_y(y_image_after, -1))
    operands = (*z_ring, *y_ring)
    z_stats, y_stats, o_part = attention_stats(meta, table, operands)
    z_stats = [z_stats] + [send_z(z_stats, step) for step in (1, -1, 2)]
    y_stats = [y_stats] + [send_y(y_stats, step) for step in (1, -1, 2)]
    outs = attention_grads(meta, table, operands, o_part, z_stats, y_stats)
    z_parts, y_parts = ring_scatter(outs[:5], send_z), ring_scatter(outs[5:], send_y)
    gz, gy, kept_part, sent_part, sent_before, sent_far, *parts = tail_grads(
        meta, slices, z_parts, y_parts, text_flipped, image_flipped, weights
    )
    x_shape = jax.ShapeDtypeStruct((SEQ, SEQ), BF16)
    got_far, got_before = send_core(sent_far), send_core(sent_before)
    got_far, sent_part = lax.optimization_barrier((got_far, sent_part))
    got_part = send_core(sent_part)
    z_own, z_before, z_after, z_far = parts[:4]
    y_own, y_before, y_after, y_far = parts[4:]
    z_far, y_far = send_y(z_far, 1), send_z(y_far, 1)
    (x_far,) = small_call(x_far_kernel, "x_far", [x_shape], (), (kept_part, got_far))
    (x_before,) = small_call(x_before_kernel, "x_before", [x_shape], (), (kept_part, got_before))
    x_far, x_before = send_x(x_far, 1), send_x(x_before, -1)
    x_own, x_after = small_call(x_rest_kernel, "x_rest", [x_shape] * 2, (), (kept_part, got_part))
    x_after, z_before = lax.optimization_barrier((x_after, z_before))
    z_before = send_y(z_before, -1)
    x_after = total((x_after, x_far)).astype(BF16)
    x_after = send_x(x_after, 1)
    z_far, y_far, y_before = lax.optimization_barrier((z_far, y_far, y_before))
    z_sum = (z_own, send_y(total((z_after, z_far)).astype(BF16), 1), z_before)
    y_sum = (y_own, send_z(total((y_after, y_far)).astype(BF16), 1), send_z(y_before, -1))
    d_text, i_grad = mixed_grads(meta, (x_own, x_after, x_before))
    z_sum, y_sum, i_grad = lax.optimization_barrier((z_sum, y_sum, i_grad))

    attended = jnp.concatenate([gz[:, COT], gy[:, COT]], axis=1)
    attn_out = dot_nn(placed, attended).astype(BF16)

    returned = lax.all_to_all(
        i_grad.reshape(images, pieces, width), "ctx", split_axis=0, concat_axis=0, tiled=True
    )
    d_patch = move_patches(take_kernel, "take_patches", owners, returned)
    z_pieces, y_pieces = split_phase(z_sum, y_sum)
    dw_query, dw_key, dw_value = final_sums(
        direct_scatter(z_pieces, send_z), direct_scatter(y_pieces, send_y)
    )
    return (
        attn_out,
        d_text,
        d_patch,
        dw_query,
        dw_key,
        dw_value,
    )


def solution(mesh):
    in_specs = (
        P("ctx", "tp"),
        P(None, ("ctx", "tp"), None),
        P(),
        P(None, "tp"),
        P(None, "tp"),
        P(None, "tp"),
        P("ctx", "tp"),
    )
    out_specs = (
        P("ctx", "tp"),
        P("ctx", "tp"),
        P(None, ("ctx", "tp"), None),
        P("ctx", "tp"),
        P("ctx", "tp"),
        P("ctx", "tp"),
    )
    return jax.shard_map(local, mesh=mesh, in_specs=in_specs, out_specs=out_specs, check_vma=False)
```

```python
import functools
import math

import jax
import jax.numpy as jnp
import numpy as np
from jax import lax
from jax.experimental import pallas as pl
from jax.experimental.pallas import tpu as pltpu
from jax.sharding import PartitionSpec as P

HD = 128
PATCH = 256
SEQ = 512
RING = 4
OFFSETS = (0, 3, 1, 2)
NEG_LARGE = -1e30
SCALE = 1.0 / math.sqrt(HD)
LOG2E = math.log2(math.e)
SMALL_LIMIT = 8 * 1024 * 1024
STREAM_LIMIT = 15 * 1024 * 1024
STATS_LIMIT = 16 * 1024 * 1024
GRADS_LIMIT = 22 * 1024 * 1024
Z_GROUPS = [[RING * y + z for z in range(RING)] for y in range(RING)]
Y_GROUPS = [[RING * y + z for y in range(RING)] for z in range(RING)]
BF16 = jnp.bfloat16
F32 = jnp.float32


def pair_table():
    rows = []
    for ctx in range(RING * RING):
        y, z = divmod(ctx, RING)
        own = []
        for q in range(RING):
            for k in range(RING):
                if RING * k + z < RING * y + q:
                    own.append(8 * q + RING + k)
                if RING * y + k < RING * q + z:
                    own.append(8 * (RING + q) + k)
        assert len(own) == 15
        rows.append(own)
    return np.asarray(rows, np.int32)


def ctx_send(value, dy, dz):
    perm = [
        (RING * y + z, RING * ((y + dy) % RING) + (z + dz) % RING)
        for y in range(RING)
        for z in range(RING)
    ]
    return lax.ppermute(value, "ctx", perm)


def send_z(value, step):
    return ctx_send(value, 0, step)


def send_y(value, step):
    return ctx_send(value, step, 0)


def send_x(value, step):
    perm = [(2 * x + core, 2 * ((x + step) % RING) + core) for x in range(RING) for core in range(2)]
    return lax.ppermute(value, "tp", perm)


def send_core(value):
    return lax.ppermute(value, "tp", [(i, i ^ 1) for i in range(2 * RING)])


def ring_gather(value, send):
    half = value.shape[0] // 2
    before = send(value, 1)
    after = send(value, -1)
    far_low = send(before[:half], 1)
    far_high = send(after[half:], -1)
    return value, before, after, far_low, far_high


def add_to(piece, part, at):
    total = (lax.slice_in_dim(piece, at, at + part.shape[0]).astype(F32) + part.astype(F32)).astype(BF16)
    return lax.dynamic_update_slice_in_dim(piece, total, at, 0)


def scatter_far(pieces, send):
    own, before, after, far_low, far_high = pieces
    after = add_to(after, send(far_low, 1), 0)
    before = add_to(before, send(far_high, -1), far_low.shape[0])
    return own, before, after


def scatter_near(pieces, send):
    own, before, after = pieces
    return own, send(after, 1), send(before, -1)


def ring_scatter(pieces, send):
    return scatter_near(scatter_far(pieces, send), send)


def direct_scatter(pieces, send):
    own, before, after, far = pieces
    return own, send(before, -1), send(after, 1), send(far, 2)


def total(parts):
    return sum(part.astype(F32) for part in parts)


def dot_nn(a, b):
    return jnp.dot(a, b, preferred_element_type=F32)


def dot_nt(a, b):
    return lax.dot_general(a, b, (((1,), (1,)), ((), ())), preferred_element_type=F32)


def dot_tn(a, b):
    return lax.dot_general(a, b, (((0,), (0,)), ((), ())), preferred_element_type=F32)


def small_call(body, name, out_shape, scalars, operands, flops=2_000_000):
    return pl.pallas_call(
        body,
        out_shape=out_shape,
        in_specs=smem(len(scalars)) + whole(len(operands)),
        out_specs=whole(len(out_shape)),
        compiler_params=pltpu.CompilerParams(vmem_limit_bytes=SMALL_LIMIT),
        cost_estimate=pl.CostEstimate(flops=flops, bytes_accessed=2_000_000, transcendentals=0),
        name=name,
    )(*scalars, *operands)


def place_kernel(owners, patches, out, sems):
    copies = [
        pltpu.make_async_copy(patches.at[k], out.at[owners[k]], sems.at[k])
        for k in range(16)
    ]
    for copy in copies:
        copy.start()
    for copy in copies:
        copy.wait()


def place_patches(owners, patches):
    return pl.pallas_call(
        place_kernel,
        out_shape=jax.ShapeDtypeStruct(patches.shape, BF16),
        in_specs=smem(1) + in_hbm(1),
        out_specs=whole(1)[0],
        scratch_shapes=[pltpu.SemaphoreType.DMA((16,))],
        compiler_params=pltpu.CompilerParams(vmem_limit_bytes=SMALL_LIMIT),
        cost_estimate=pl.CostEstimate(flops=0, bytes_accessed=500_000, transcendentals=0),
        name="place_patches",
    )(owners, *from_hbm(patches))


def take_kernel(owners, returned, out):
    for k in range(16):
        out[k] = returned[owners[k]]


def move_patches(body, name, owners, patches):
    shape = [jax.ShapeDtypeStruct(patches.shape, BF16)]
    return small_call(body, name, shape, (owners,), (patches,))[0]


QUERY, KEY, VALUE, COT = (slice(i * HD, (i + 1) * HD) for i in range(4))
CHUNK = 1024
CHUNKS = 4096 // CHUNK


def pack(acc, cot, z_out, y_out):
    for head, cols, out in ((0, (0, 3, 5), z_out), (1, (1, 2, 4), y_out)):
        for at, col in enumerate(cols):
            out[:, at * HD : (at + 1) * HD] = acc[:, col * HD : (col + 1) * HD].astype(BF16)
        out[:, COT] = cot[:, head * HD : (head + 1) * HD]


def block_rows(slices, j):
    return pl.ds(pl.multiple_of(slices[j] * SEQ, SEQ), SEQ)


def stream(weights, held, sems, depths):
    groups = []
    for j, depth in enumerate(depths):
        groups.append(
            [
                pltpu.make_async_copy(
                    ref.at[depth], held.at[depth, i * 256 : (i + 1) * 256], sems.at[j, i]
                )
                for i, ref in enumerate(weights)
            ]
        )
    for group in groups:
        for copy in group:
            copy.start()
    return groups


def text_kernel(slices, own, oth, cot, wq, wk, wv, flipped, z_keep, y_keep, z_out, y_out, held, turned, sems):
    depths = [block_rows(slices, j) for j in range(8)]
    groups = stream((wq, wk, wv), held, sems, depths)
    acc = None
    outgoing = []
    for j, (depth, group) in enumerate(zip(depths, groups)):
        part = own if j < RING else oth
        block = part[:, (j % RING) * SEQ : (j % RING + 1) * SEQ]
        turned[depth, :] = block.T
        outgoing.append(pltpu.make_async_copy(turned.at[depth], flipped.at[depth], sems.at[j, 3]))
        outgoing[-1].start()
        for copy in group:
            copy.wait()
        term = dot_nn(block, held[depth, :])
        acc = term if acc is None else acc + term
    pack(acc, cot[:PATCH], z_out, y_out)
    for i, (out, keep) in enumerate(((z_out, z_keep), (y_out, y_keep))):
        outgoing.append(pltpu.make_async_copy(out, keep, sems.at[8, i]))
        outgoing[-1].start()
    for copy in outgoing:
        copy.wait()


def image_kernel(own, oth, cot, held, flipped, z_out, y_out, turned, sems):
    acc = None
    outgoing = []
    for j in range(CHUNKS):
        depth = slice(j * CHUNK, (j + 1) * CHUNK)
        block = jnp.concatenate([own[:, depth], oth[:, depth]], axis=0)
        turned[depth, :] = block.T
        outgoing.append(pltpu.make_async_copy(turned.at[depth], flipped.at[depth], sems.at[j]))
        outgoing[-1].start()
        term = dot_nn(block, held[depth, :])
        acc = term if acc is None else acc + term
    pack(acc, cot[PATCH:], z_out, y_out)
    for copy in outgoing:
        copy.wait()


def from_hbm(*arrays):
    return [pltpu.with_memory_space_constraint(array, pltpu.HBM) for array in arrays]


def project_text(slices, own, oth, cot, weights):
    rows = (PATCH, 4 * HD)
    return pl.pallas_call(
        text_kernel,
        out_shape=[pltpu.HBM((4096, PATCH), BF16)]
        + [pltpu.HBM(rows, BF16)] * 2
        + [jax.ShapeDtypeStruct(rows, BF16)] * 2
        + [jax.ShapeDtypeStruct((4096, 6 * HD), BF16)],
        in_specs=smem(1) + whole(3) + in_hbm(3),
        out_specs=in_hbm(3) + whole(3),
        scratch_shapes=[pltpu.VMEM((4096, PATCH), BF16), pltpu.SemaphoreType.DMA((9, 4))],
        compiler_params=pltpu.CompilerParams(vmem_limit_bytes=SMALL_LIMIT),
        cost_estimate=pl.CostEstimate(
            flops=2 * PATCH * 4096 * 768, bytes_accessed=8_000_000, transcendentals=0
        ),
        name="qkv_text",
    )(slices, own, oth, cot, *from_hbm(*weights))


def project_image(own, oth, cot, held):
    rows = (PATCH, 4 * HD)
    return pl.pallas_call(
        image_kernel,
        out_shape=[pltpu.HBM((4096, PATCH), BF16)] + [jax.ShapeDtypeStruct(rows, BF16)] * 2,
        in_specs=whole(4),
        out_specs=in_hbm(1) + whole(2),
        scratch_shapes=[pltpu.VMEM((4096, PATCH), BF16), pltpu.SemaphoreType.DMA((CHUNKS,))],
        compiler_params=pltpu.CompilerParams(vmem_limit_bytes=SMALL_LIMIT),
        cost_estimate=pl.CostEstimate(
            flops=2 * PATCH * 4096 * 768, bytes_accessed=2_000_000, transcendentals=0
        ),
        name="qkv_image",
    )(own, oth, cot, held)


def ranks(off, shape, dim):
    index = lax.broadcasted_iota(jnp.int32, shape, dim)
    return jnp.where(index < PATCH, 2 * index, 2 * off - 1)


def diagonal_mask(off):
    return ranks(off, (SEQ, 1), 0) <= ranks(off, (1, SEQ), 1)


def fetch(refs, blocks, sems, y, z):
    copies = []
    for base, at, parts in ((0, z, refs[0:8]), (RING, y, refs[8:16])):
        for rel, off in enumerate(OFFSETS):
            slot = base + lax.rem(at + off, RING)
            for half in range(2):
                target = blocks.at[slot, half * PATCH : (half + 1) * PATCH]
                part = parts[2 * rel + half]
                copies.append(pltpu.make_async_copy(part, target, sems.at[len(copies)]))
    first = copies[0:2] + copies[8:10]
    rest = copies[2:8] + copies[10:]
    for copy in first + rest:
        copy.start()
    return first, rest


def own_pairs(meta, advance):
    y, z, off = meta[0], meta[1], meta[2]
    advance([(z, RING + y), (RING + y, z)], diagonal_mask(off))


def other_pairs(table, advance):
    def step(i, carry):
        codes = [table[3 * i + j] for j in range(3)]
        advance([(lax.div(code, 8), lax.rem(code, 8)) for code in codes], None)
        return carry

    lax.fori_loop(0, 5, step, 0)


def flip_all(dest, blocks, cols):
    for i in range(2 * RING):
        dest[i] = blocks[i, :, cols].T


def flip_own(dest, blocks, cols, y, z):
    dest[z] = blocks[z, :, cols].T
    dest[RING + y] = blocks[RING + y, :, cols].T


def stats_kernel(meta, table, *refs):
    z_out, y_out, o_out, blocks, vt, top, total, sems = refs[16:]
    y, z = meta[0], meta[1]
    first, rest = fetch(refs, blocks, sems, y, z)
    top[...] = jnp.full_like(top, NEG_LARGE)
    total[...] = jnp.zeros_like(total)
    o_out[...] = jnp.zeros_like(o_out)

    def advance(pairs, allowed):
        scores = [dot_nt(blocks[k, :, KEY], blocks[q, :, QUERY]) * (SCALE * LOG2E) for q, k in pairs]
        if allowed is not None:
            scores = [jnp.where(allowed, score, NEG_LARGE) for score in scores]
        highs = [jnp.max(score, axis=0, keepdims=True) for score in scores]
        for (q, k), score, high in zip(pairs, scores, highs):
            old = top[q]
            new = jnp.maximum(old, high)
            probs = jnp.exp2(score - new)
            shrink = jnp.exp2(old - new)
            top[q] = new
            total[q] = total[q] * shrink + jnp.sum(probs, axis=0, keepdims=True)
            o_out[q] = o_out[q] * shrink + dot_nn(vt[k], probs.astype(BF16))

    for copy in first:
        copy.wait()
    flip_own(vt, blocks, VALUE, y, z)
    own_pairs(meta, advance)
    for copy in rest:
        copy.wait()
    flip_all(vt, blocks, VALUE)
    other_pairs(table, advance)
    for head, out in ((0, z_out), (1, y_out)):
        for i in range(RING):
            at = head * RING + i
            count = total[at]
            some = count > 0.0
            safe = jnp.where(some, count, 1.0)
            partial = o_out[at] / safe
            o_out[at] = partial
            flipped = blocks[at, :, COT].astype(F32).T
            out[i : i + 1, :] = jnp.where(some, top[at] + jnp.log(safe) * LOG2E, NEG_LARGE)
            out[RING + i : RING + i + 1, :] = jnp.sum(partial * flipped, axis=0, keepdims=True)


def whole(count):
    return [pl.BlockSpec(memory_space=pltpu.VMEM)] * count


def in_hbm(count):
    return [pl.BlockSpec(memory_space=pltpu.HBM)] * count


def smem(count):
    return [pl.BlockSpec(memory_space=pltpu.SMEM)] * count


def attention_stats(meta, table, pieces):
    row = pltpu.VMEM((2 * RING, 1, SEQ), F32)
    return pl.pallas_call(
        stats_kernel,
        out_shape=[jax.ShapeDtypeStruct((2 * RING, SEQ), F32)] * 2
        + [jax.ShapeDtypeStruct((2 * RING, HD, SEQ), F32)],
        in_specs=smem(2) + in_hbm(16),
        out_specs=whole(3),
        scratch_shapes=[
            pltpu.VMEM((2 * RING, SEQ, 4 * HD), BF16),
            pltpu.VMEM((2 * RING, HD, SEQ), BF16),
            row,
            row,
            pltpu.SemaphoreType.DMA((16,)),
        ],
        compiler_params=pltpu.CompilerParams(vmem_limit_bytes=STATS_LIMIT),
        cost_estimate=pl.CostEstimate(
            flops=17 * 2 * 2 * SEQ * SEQ * HD,
            bytes_accessed=5_000_000,
            transcendentals=17 * SEQ * SEQ,
        ),
        name="stats",
    )(meta, table, *pieces)


def grads_kernel(meta, table, *refs):
    o_part = refs[16]
    stats = (refs[17:21], refs[21:25])
    outs = refs[25:35]
    blocks, kt, lse, dots, keep, dq_sum, dk_sum, dv_sum, sems = refs[35:]
    y, z = meta[0], meta[1]
    first, rest = fetch(refs, blocks, sems, y, z)
    dq_sum[...] = jnp.zeros_like(dq_sum)
    dk_sum[...] = jnp.zeros_like(dk_sum)
    dv_sum[...] = jnp.zeros_like(dv_sum)
    for head in range(2):
        parts = [ref[...] for ref in stats[head]]
        logs = [part[:RING] for part in parts]
        top = functools.reduce(jnp.maximum, logs)
        shares = [jnp.exp2(log - top) for log in logs]
        norm = sum(shares)
        full = top + jnp.log(norm) * LOG2E
        dot = sum(share * part[RING:] for share, part in zip(shares, parts)) / norm
        weight = jnp.exp2(logs[0] - full)
        for i in range(RING):
            lse[head * RING + i] = full[i : i + 1]
            dots[head * RING + i] = dot[i : i + 1]
            keep[head * RING + i] = weight[i : i + 1]

    def advance(pairs, allowed):
        for q, k in pairs:
            query, cot = blocks[q, :, QUERY], blocks[q, :, COT]
            probs = jnp.exp2(dot_nt(blocks[k, :, KEY], query) * (SCALE * LOG2E) - lse[q])
            if allowed is not None:
                probs = jnp.where(allowed, probs, 0.0)
            prob_grads = dot_nt(blocks[k, :, VALUE], cot)
            slope = (probs * (prob_grads - dots[q]) * SCALE).astype(BF16)
            dv_sum[k] += dot_nn(probs.astype(BF16), cot)
            dk_sum[k] += dot_nn(slope, query)
            dq_sum[q] += dot_nn(kt[k], slope)

    for copy in first:
        copy.wait()
    flip_own(kt, blocks, KEY, y, z)
    own_pairs(meta, advance)
    for copy in rest:
        copy.wait()
    flip_all(kt, blocks, KEY)
    other_pairs(table, advance)
    half = SEQ // 2
    for base, at, parts in ((0, z, outs[:5]), (RING, y, outs[5:])):
        for rel, shift in enumerate(OFFSETS):
            slot = base + lax.rem(at + shift, RING)
            terms = (
                dq_sum[slot].T.astype(BF16),
                dk_sum[slot].astype(BF16),
                dv_sum[slot].astype(BF16),
                (o_part[slot] * keep[slot]).T.astype(BF16),
            )
            for cols, term in zip((QUERY, KEY, VALUE, COT), terms):
                if rel < 3:
                    parts[rel][:, cols] = term
                else:
                    parts[3][:, cols] = term[:half]
                    parts[4][:, cols] = term[half:]


def attention_grads(meta, table, pieces, o_part, z_stats, y_stats):
    row = pltpu.VMEM((2 * RING, 1, SEQ), F32)
    tall = pltpu.VMEM((2 * RING, SEQ, HD), F32)
    flat = pltpu.VMEM((2 * RING, HD, SEQ), F32)
    full = jax.ShapeDtypeStruct((SEQ, 4 * HD), BF16)
    half = jax.ShapeDtypeStruct((SEQ // 2, 4 * HD), BF16)
    return pl.pallas_call(
        grads_kernel,
        out_shape=([full] * 3 + [half] * 2) * 2,
        in_specs=smem(2) + in_hbm(16) + whole(9),
        out_specs=whole(10),
        scratch_shapes=[
            pltpu.VMEM((2 * RING, SEQ, 4 * HD), BF16),
            pltpu.VMEM((2 * RING, HD, SEQ), BF16),
            row,
            row,
            row,
            flat,
            tall,
            tall,
            pltpu.SemaphoreType.DMA((16,)),
        ],
        compiler_params=pltpu.CompilerParams(vmem_limit_bytes=GRADS_LIMIT),
        cost_estimate=pl.CostEstimate(
            flops=17 * 5 * 2 * SEQ * SEQ * HD,
            bytes_accessed=10_000_000,
            transcendentals=17 * SEQ * SEQ,
        ),
        name="grads",
    )(meta, table, *pieces, o_part, *z_stats, *y_stats)


def tail_kernel(meta, slices, *refs):
    text, image = refs[6:8]
    weights = refs[8:11]
    gz, gy, own, oth, oth_before, oth_far = refs[11:17]
    z_parts, y_parts = refs[17:21], refs[21:25]
    held, products, sems = refs[25:]
    y, z = meta[0], meta[1]
    depths = [block_rows(slices, j) for j in range(8)]
    groups = stream(weights, held, sems, depths)
    for parts, grads in ((refs[:3], gz), (refs[3:6], gy)):
        grads[...] = total([part[...] for part in parts]).astype(BF16)
    width = 3 * HD
    rows = 256
    grads = jnp.concatenate([gz[:, :width], gy[:, :width]], axis=1)
    for rel, shift in enumerate(OFFSETS):
        depth = pl.ds(pl.multiple_of(lax.rem(y + shift, RING) * CHUNK, CHUNK), CHUNK)
        term = dot_nn(text[depth, :], grads[:PATCH]) + dot_nn(image[depth, :], grads[PATCH:])
        products[...] = term.astype(BF16)
        for other, other_shift in enumerate(OFFSETS):
            source = pl.ds(pl.multiple_of(lax.rem(z + other_shift, RING) * rows, rows), rows)
            z_parts[rel][other * rows : (other + 1) * rows, :] = products[source, :width]
            y_parts[other][rel * rows : (rel + 1) * rows, :] = products[source, width:]

    columns = [ref[:, cols] for cols in (QUERY, KEY, VALUE) for ref in (gz, gy)]
    columns = [columns[i] for i in (0, 1, 3, 2, 5, 4)]
    grads = jnp.concatenate(columns, axis=1)
    pieces = [own.at[i] for i in range(RING)]
    pieces += [oth.at[0], oth_before, oth.at[1], oth_far]
    for j, (depth, group) in enumerate(zip(depths, groups)):
        for copy in group:
            copy.wait()
        term = dot_nt(grads, held[depth, :]).astype(BF16)
        pieces[j][:PATCH] = term[:PATCH]
        at = pl.ds(pl.multiple_of(PATCH + slices[j] * 32, 32), 32)
        for i, piece in enumerate(pieces):
            piece[at, :] = term[PATCH + 32 * i : PATCH + 32 * (i + 1)]


def tail_grads(meta, slices, z_parts, y_parts, text, image, weights):
    piece = jax.ShapeDtypeStruct((CHUNK, 3 * HD), BF16)
    return pl.pallas_call(
        tail_kernel,
        out_shape=[jax.ShapeDtypeStruct((SEQ, 4 * HD), BF16)] * 2
        + [jax.ShapeDtypeStruct((RING, SEQ, SEQ), BF16)]
        + [jax.ShapeDtypeStruct((2, SEQ, SEQ), BF16)]
        + [jax.ShapeDtypeStruct((SEQ, SEQ), BF16)] * 2
        + [piece] * 8,
        in_specs=smem(2) + whole(8) + in_hbm(3),
        out_specs=whole(14),
        scratch_shapes=[
            pltpu.VMEM((4096, 6 * HD), BF16),
            pltpu.VMEM((CHUNK, 6 * HD), BF16),
            pltpu.SemaphoreType.DMA((8, 3)),
        ],
        compiler_params=pltpu.CompilerParams(vmem_limit_bytes=STREAM_LIMIT),
        cost_estimate=pl.CostEstimate(
            flops=4 * SEQ * 4096 * 768, bytes_accessed=8_000_000, transcendentals=0
        ),
        name="tail_grads",
    )(meta, slices, *z_parts, *y_parts, text, image, *from_hbm(*weights))


def x_before_kernel(kept, got, out):
    out[...] = total((kept[1], got[...])).astype(BF16)


def x_far_kernel(kept, got, out):
    out[...] = total((kept[3], got[...])).astype(BF16)


def x_rest_kernel(kept, got, own, after):
    own[...] = total((kept[0], got[0])).astype(BF16)
    after[...] = total((kept[2], got[1])).astype(BF16)


def split_kernel(*refs):
    for parts, outs in ((refs[:3], refs[6:10]), (refs[3:6], refs[10:14])):
        for i, out in enumerate(outs):
            rows = slice(i * 256, (i + 1) * 256)
            out[...] = total([part[rows] for part in parts]).astype(out.dtype)


def split_phase(z_sum, y_sum):
    own = jax.ShapeDtypeStruct((256, 3 * HD), F32)
    other = jax.ShapeDtypeStruct((256, 3 * HD), BF16)
    outs = small_call(split_kernel, "split", [own, other, other, other] * 2, (), (*z_sum, *y_sum))
    return outs[:4], outs[4:]


def mixed_kernel(meta, own, before, after, text_out, image_out):
    off = meta[2]
    grads = total((own[...], before[...], after[...])).astype(BF16).astype(F32)
    text = grads[:PATCH]
    row = lax.broadcasted_iota(jnp.int32, (PATCH, 1), 0)
    text_out[:PATCH] = jnp.where(row < off, text, 0.0).astype(BF16)
    text_out[PATCH:] = jnp.where(row < off, 0.0, text).astype(BF16)
    for i in range(8):
        rows = slice(PATCH + 32 * i, PATCH + 32 * (i + 1))
        image_out[:, i * SEQ : (i + 1) * SEQ] = grads[rows].astype(BF16)


def mixed_grads(meta, parts):
    shapes = [jax.ShapeDtypeStruct((SEQ, SEQ), BF16), jax.ShapeDtypeStruct((32, 4096), BF16)]
    return small_call(mixed_kernel, "mixed_grads", shapes, (meta,), parts, 4_000_000_000)


def final_kernel(*refs):
    z_sum = total([ref[...] for ref in refs[:4]])
    y_sum = total([ref[...] for ref in refs[4:8]])
    for cols, out, first, second in (
        (QUERY, refs[8], z_sum, y_sum),
        (KEY, refs[9], y_sum, z_sum),
        (VALUE, refs[10], y_sum, z_sum),
    ):
        out[:, :HD] = first[:, cols]
        out[:, HD:] = second[:, cols]


def final_sums(z_parts, y_parts):
    shape = jax.ShapeDtypeStruct((256, 2 * HD), F32)
    return small_call(final_kernel, "final_sums", [shape] * 3, (), (*z_parts, *y_parts))


def local(text_hidden, patch_rows, image_start, w_query, w_key, w_value, d_attn):
    ctx = lax.axis_index("ctx")
    y, z = ctx // RING, ctx % RING
    images, pieces, width = patch_rows.shape
    owners = image_start // SEQ
    off = jnp.sum(jnp.where(owners == ctx, image_start, 0)) - ctx * SEQ
    meta = jnp.stack([y, z, off]).astype(jnp.int32)
    table = lax.dynamic_index_in_dim(jnp.asarray(pair_table()), ctx, 0, keepdims=False)

    tp = lax.axis_index("tp")
    x, core = tp // 2, tp % 2
    columns = (x + jnp.asarray(OFFSETS, jnp.int32)) % RING
    slices = jnp.concatenate([columns * 2 + core, columns * 2 + 1 - core]).astype(jnp.int32)

    index = jnp.arange(SEQ, dtype=jnp.int32)
    rel = (index - PATCH) // 32
    shift = rel % RING
    shift = jnp.where(shift == 0, 0, jnp.where(shift == 1, 3, shift - 1))
    sender = 2 * ((x + shift) % RING) + jnp.where(rel < RING, core, 1 - core)
    text_pos = jnp.where(index < off, index, index + PATCH)
    image_pos = off + 16 * ((index % 32) // 2) + 2 * sender + index % 2
    pos = jnp.where(index < PATCH, text_pos, image_pos)
    placed = (index[:, None] == pos[None, :]).astype(BF16)

    by_shard = place_patches(owners, patch_rows)
    by_shard, text_hidden = lax.optimization_barrier((by_shard, text_hidden))
    arrived = lax.all_to_all(by_shard, "ctx", split_axis=0, concat_axis=0, tiled=True)
    kept = index[:PATCH, None] < off
    text = jnp.where(kept, text_hidden[:PATCH], text_hidden[PATCH:])
    t_ring = ring_gather(text, send_x)
    arrived, t_ring = lax.optimization_barrier((arrived, t_ring))
    t_far = jnp.concatenate(t_ring[3:], axis=0)
    t_own = jnp.concatenate([*t_ring[:3], t_far], axis=1)
    t_oth = send_core(t_own)

    image = arrived.reshape(images * pieces, width)
    before, after = send_x(image, 1), send_x(image, -1)
    cot = dot_tn(placed, d_attn).astype(BF16)
    weights = (w_query, w_key, w_value)
    half = image.shape[0] // 2
    far = (send_x(before[:half], 1), send_x(after[half:], -1))
    i_own = jnp.concatenate([image, before, after, *far], axis=0)
    i_oth = send_core(i_own)

    text_flipped, z_keep, y_keep, z_text, y_text, held = project_text(
        slices, t_own, t_oth, cot, weights
    )
    image_flipped, z_image, y_image = project_image(i_own, i_oth, cot, held)
    z_keep, y_keep = from_hbm(z_keep, y_keep)

    z_before, z_after = send_z(z_text, 1), send_z(z_text, -1)
    y_before, y_after = send_y(y_text, 1), send_y(y_text, -1)
    z_before, y_before, z_image = lax.optimization_barrier((z_before, y_before, z_image))
    z_image_before, z_image_after = send_z(z_image, 1), send_z(z_image, -1)
    y_image_before, y_image_after = send_y(y_image, 1), send_y(y_image, -1)
    z_ring = (z_keep, z_image, z_before, z_image_before, z_after, z_image_after)
    z_ring += (send_z(z_before, 1), send_z(z_image_after, -1))
    y_ring = (y_keep, y_image, y_before, y_image_before, y_after, y_image_after)
    y_ring += (send_y(y_before, 1), send_y(y_image_after, -1))
    operands = (*z_ring, *y_ring)
    z_stats, y_stats, o_part = attention_stats(meta, table, operands)
    z_stats = [z_stats] + [send_z(z_stats, step) for step in (1, -1, 2)]
    y_stats = [y_stats] + [send_y(y_stats, step) for step in (1, -1, 2)]
    outs = attention_grads(meta, table, operands, o_part, z_stats, y_stats)
    z_parts, y_parts = ring_scatter(outs[:5], send_z), ring_scatter(outs[5:], send_y)
    gz, gy, kept_part, sent_part, sent_before, sent_far, *parts = tail_grads(
        meta, slices, z_parts, y_parts, text_flipped, image_flipped, weights
    )
    x_shape = jax.ShapeDtypeStruct((SEQ, SEQ), BF16)
    got_far, got_before = send_core(sent_far), send_core(sent_before)
    got_part = send_core(sent_part)
    z_own, z_before, z_after, z_far = parts[:4]
    y_own, y_before, y_after, y_far = parts[4:]
    z_far, y_far = send_y(z_far, 1), send_z(y_far, 1)
    (x_far,) = small_call(x_far_kernel, "x_far", [x_shape], (), (kept_part, got_far))
    (x_before,) = small_call(x_before_kernel, "x_before", [x_shape], (), (kept_part, got_before))
    x_far, x_before = send_x(x_far, 1), send_x(x_before, -1)
    x_own, x_after = small_call(x_rest_kernel, "x_rest", [x_shape] * 2, (), (kept_part, got_part))
    x_after, z_before = lax.optimization_barrier((x_after, z_before))
    z_before = send_y(z_before, -1)
    x_after = total((x_after, x_far)).astype(BF16)
    x_after = send_x(x_after, 1)
    z_far, y_far, y_before = lax.optimization_barrier((z_far, y_far, y_before))
    z_sum = (z_own, send_y(total((z_after, z_far)).astype(BF16), 1), z_before)
    y_sum = (y_own, send_z(total((y_after, y_far)).astype(BF16), 1), send_z(y_before, -1))
    d_text, i_grad = mixed_grads(meta, (x_own, x_after, x_before))
    z_sum, y_sum, i_grad = lax.optimization_barrier((z_sum, y_sum, i_grad))

    attended = jnp.concatenate([gz[:, COT], gy[:, COT]], axis=1)
    attn_out = dot_nn(placed, attended).astype(BF16)

    returned = lax.all_to_all(
        i_grad.reshape(images, pieces, width), "ctx", split_axis=0, concat_axis=0, tiled=True
    )
    z_pieces, y_pieces = split_phase(z_sum, y_sum)
    returned, y_pieces = lax.optimization_barrier((returned, y_pieces))
    d_patch = move_patches(take_kernel, "take_patches", owners, returned)
    dw_query, dw_key, dw_value = final_sums(
        direct_scatter(z_pieces, send_z), direct_scatter(y_pieces, send_y)
    )
    return (
        attn_out,
        d_text,
        d_patch,
        dw_query,
        dw_key,
        dw_value,
    )


def solution(mesh):
    in_specs = (
        P("ctx", "tp"),
        P(None, ("ctx", "tp"), None),
        P(),
        P(None, "tp"),
        P(None, "tp"),
        P(None, "tp"),
        P("ctx", "tp"),
    )
    out_specs = (
        P("ctx", "tp"),
        P("ctx", "tp"),
        P(None, ("ctx", "tp"), None),
        P("ctx", "tp"),
        P("ctx", "tp"),
        P("ctx", "tp"),
    )
    return jax.shard_map(local, mesh=mesh, in_specs=in_specs, out_specs=out_specs, check_vma=False)
```

```python
import functools
import math

import jax
import jax.numpy as jnp
import numpy as np
from jax import lax
from jax.experimental import pallas as pl
from jax.experimental.pallas import tpu as pltpu
from jax.sharding import PartitionSpec as P

HD = 128
PATCH = 256
SEQ = 512
RING = 4
OFFSETS = (0, 3, 1, 2)
NEG_LARGE = -1e30
SCALE = 1.0 / math.sqrt(HD)
LOG2E = math.log2(math.e)
SMALL_LIMIT = 8 * 1024 * 1024
STREAM_LIMIT = 15 * 1024 * 1024
STATS_LIMIT = 16 * 1024 * 1024
GRADS_LIMIT = 22 * 1024 * 1024
Z_GROUPS = [[RING * y + z for z in range(RING)] for y in range(RING)]
Y_GROUPS = [[RING * y + z for y in range(RING)] for z in range(RING)]
BF16 = jnp.bfloat16
F32 = jnp.float32


def pair_table():
    rows = []
    for ctx in range(RING * RING):
        y, z = divmod(ctx, RING)
        own = []
        for q in range(RING):
            for k in range(RING):
                if RING * k + z < RING * y + q:
                    own.append(8 * q + RING + k)
                if RING * y + k < RING * q + z:
                    own.append(8 * (RING + q) + k)
        assert len(own) == 15
        rows.append(own)
    return np.asarray(rows, np.int32)


def ctx_send(value, dy, dz):
    perm = [
        (RING * y + z, RING * ((y + dy) % RING) + (z + dz) % RING)
        for y in range(RING)
        for z in range(RING)
    ]
    return lax.ppermute(value, "ctx", perm)


def send_z(value, step):
    return ctx_send(value, 0, step)


def send_y(value, step):
    return ctx_send(value, step, 0)


def send_x(value, step):
    perm = [(2 * x + core, 2 * ((x + step) % RING) + core) for x in range(RING) for core in range(2)]
    return lax.ppermute(value, "tp", perm)


def send_core(value):
    return lax.ppermute(value, "tp", [(i, i ^ 1) for i in range(2 * RING)])


def ring_gather(value, send):
    half = value.shape[0] // 2
    before = send(value, 1)
    after = send(value, -1)
    far_low = send(before[:half], 1)
    far_high = send(after[half:], -1)
    return value, before, after, far_low, far_high


def add_to(piece, part, at):
    total = (lax.slice_in_dim(piece, at, at + part.shape[0]).astype(F32) + part.astype(F32)).astype(BF16)
    return lax.dynamic_update_slice_in_dim(piece, total, at, 0)


def scatter_far(pieces, send):
    own, before, after, far_low, far_high = pieces
    after = add_to(after, send(far_low, 1), 0)
    before = add_to(before, send(far_high, -1), far_low.shape[0])
    return own, before, after


def scatter_near(pieces, send):
    own, before, after = pieces
    return own, send(after, 1), send(before, -1)


def ring_scatter(pieces, send):
    return scatter_near(scatter_far(pieces, send), send)


def direct_scatter(pieces, send):
    own, before, after, far = pieces
    return own, send(before, -1), send(after, 1), send(far, 2)


def total(parts):
    return sum(part.astype(F32) for part in parts)


def dot_nn(a, b):
    return jnp.dot(a, b, preferred_element_type=F32)


def dot_nt(a, b):
    return lax.dot_general(a, b, (((1,), (1,)), ((), ())), preferred_element_type=F32)


def dot_tn(a, b):
    return lax.dot_general(a, b, (((0,), (0,)), ((), ())), preferred_element_type=F32)


def small_call(body, name, out_shape, scalars, operands, flops=2_000_000):
    return pl.pallas_call(
        body,
        out_shape=out_shape,
        in_specs=smem(len(scalars)) + whole(len(operands)),
        out_specs=whole(len(out_shape)),
        compiler_params=pltpu.CompilerParams(vmem_limit_bytes=SMALL_LIMIT),
        cost_estimate=pl.CostEstimate(flops=flops, bytes_accessed=2_000_000, transcendentals=0),
        name=name,
    )(*scalars, *operands)


def place_kernel(owners, patches, out, sems):
    copies = [
        pltpu.make_async_copy(patches.at[k], out.at[owners[k]], sems.at[k])
        for k in range(16)
    ]
    for copy in copies:
        copy.start()
    for copy in copies:
        copy.wait()


def place_patches(owners, patches):
    return pl.pallas_call(
        place_kernel,
        out_shape=jax.ShapeDtypeStruct(patches.shape, BF16),
        in_specs=smem(1) + in_hbm(1),
        out_specs=whole(1)[0],
        scratch_shapes=[pltpu.SemaphoreType.DMA((16,))],
        compiler_params=pltpu.CompilerParams(vmem_limit_bytes=SMALL_LIMIT),
        cost_estimate=pl.CostEstimate(flops=0, bytes_accessed=500_000, transcendentals=0),
        name="place_patches",
    )(owners, *from_hbm(patches))


def take_kernel(owners, returned, out):
    for k in range(16):
        out[k] = returned[owners[k]]


def move_patches(body, name, owners, patches):
    shape = [jax.ShapeDtypeStruct(patches.shape, BF16)]
    return small_call(body, name, shape, (owners,), (patches,))[0]


QUERY, KEY, VALUE, COT = (slice(i * HD, (i + 1) * HD) for i in range(4))
CHUNK = 1024
CHUNKS = 4096 // CHUNK


def pack(acc, cot, z_out, y_out):
    for head, cols, out in ((0, (0, 3, 5), z_out), (1, (1, 2, 4), y_out)):
        for at, col in enumerate(cols):
            out[:, at * HD : (at + 1) * HD] = acc[:, col * HD : (col + 1) * HD].astype(BF16)
        out[:, COT] = cot[:, head * HD : (head + 1) * HD]


def block_rows(slices, j):
    return pl.ds(pl.multiple_of(slices[j] * SEQ, SEQ), SEQ)


def stream(weights, held, sems, depths):
    groups = []
    for j, depth in enumerate(depths):
        groups.append(
            [
                pltpu.make_async_copy(
                    ref.at[depth], held.at[depth, i * 256 : (i + 1) * 256], sems.at[j, i]
                )
                for i, ref in enumerate(weights)
            ]
        )
    for group in groups:
        for copy in group:
            copy.start()
    return groups


def text_kernel(slices, own, oth, cot, wq, wk, wv, flipped, z_keep, y_keep, z_out, y_out, held, turned, sems):
    depths = [block_rows(slices, j) for j in range(8)]
    groups = stream((wq, wk, wv), held, sems, depths)
    acc = None
    outgoing = []
    for j, (depth, group) in enumerate(zip(depths, groups)):
        part = own if j < RING else oth
        block = part[:, (j % RING) * SEQ : (j % RING + 1) * SEQ]
        turned[depth, :] = block.T
        outgoing.append(pltpu.make_async_copy(turned.at[depth], flipped.at[depth], sems.at[j, 3]))
        outgoing[-1].start()
        for copy in group:
            copy.wait()
        term = dot_nn(block, held[depth, :])
        acc = term if acc is None else acc + term
    pack(acc, cot[:PATCH], z_out, y_out)
    for i, (out, keep) in enumerate(((z_out, z_keep), (y_out, y_keep))):
        outgoing.append(pltpu.make_async_copy(out, keep, sems.at[8, i]))
        outgoing[-1].start()
    for copy in outgoing:
        copy.wait()


def image_kernel(own, oth, cot, held, flipped, z_out, y_out, turned, sems):
    acc = None
    outgoing = []
    for j in range(CHUNKS):
        depth = slice(j * CHUNK, (j + 1) * CHUNK)
        block = jnp.concatenate([own[:, depth], oth[:, depth]], axis=0)
        turned[depth, :] = block.T
        outgoing.append(pltpu.make_async_copy(turned.at[depth], flipped.at[depth], sems.at[j]))
        outgoing[-1].start()
        term = dot_nn(block, held[depth, :])
        acc = term if acc is None else acc + term
    pack(acc, cot[PATCH:], z_out, y_out)
    for copy in outgoing:
        copy.wait()


def from_hbm(*arrays):
    return [pltpu.with_memory_space_constraint(array, pltpu.HBM) for array in arrays]


def project_text(slices, own, oth, cot, weights):
    rows = (PATCH, 4 * HD)
    return pl.pallas_call(
        text_kernel,
        out_shape=[pltpu.HBM((4096, PATCH), BF16)]
        + [pltpu.HBM(rows, BF16)] * 2
        + [jax.ShapeDtypeStruct(rows, BF16)] * 2
        + [jax.ShapeDtypeStruct((4096, 6 * HD), BF16)],
        in_specs=smem(1) + whole(3) + in_hbm(3),
        out_specs=in_hbm(3) + whole(3),
        scratch_shapes=[pltpu.VMEM((4096, PATCH), BF16), pltpu.SemaphoreType.DMA((9, 4))],
        compiler_params=pltpu.CompilerParams(vmem_limit_bytes=SMALL_LIMIT),
        cost_estimate=pl.CostEstimate(
            flops=2 * PATCH * 4096 * 768, bytes_accessed=8_000_000, transcendentals=0
        ),
        name="qkv_text",
    )(slices, own, oth, cot, *from_hbm(*weights))


def project_image(own, oth, cot, held):
    rows = (PATCH, 4 * HD)
    return pl.pallas_call(
        image_kernel,
        out_shape=[pltpu.HBM((4096, PATCH), BF16)] + [jax.ShapeDtypeStruct(rows, BF16)] * 2,
        in_specs=whole(4),
        out_specs=in_hbm(1) + whole(2),
        scratch_shapes=[pltpu.VMEM((4096, PATCH), BF16), pltpu.SemaphoreType.DMA((CHUNKS,))],
        compiler_params=pltpu.CompilerParams(vmem_limit_bytes=SMALL_LIMIT),
        cost_estimate=pl.CostEstimate(
            flops=2 * PATCH * 4096 * 768, bytes_accessed=2_000_000, transcendentals=0
        ),
        name="qkv_image",
    )(own, oth, cot, held)


def ranks(off, shape, dim):
    index = lax.broadcasted_iota(jnp.int32, shape, dim)
    return jnp.where(index < PATCH, 2 * index, 2 * off - 1)


def diagonal_mask(off):
    return ranks(off, (SEQ, 1), 0) <= ranks(off, (1, SEQ), 1)


def fetch(refs, blocks, sems, y, z):
    copies = []
    for base, at, parts in ((0, z, refs[0:8]), (RING, y, refs[8:16])):
        for rel, off in enumerate(OFFSETS):
            slot = base + lax.rem(at + off, RING)
            for half in range(2):
                target = blocks.at[slot, half * PATCH : (half + 1) * PATCH]
                part = parts[2 * rel + half]
                copies.append(pltpu.make_async_copy(part, target, sems.at[len(copies)]))
    first = copies[0:2] + copies[8:10]
    rest = copies[2:8] + copies[10:]
    for copy in first + rest:
        copy.start()
    return first, rest


def own_pairs(meta, advance):
    y, z, off = meta[0], meta[1], meta[2]
    advance([(z, RING + y), (RING + y, z)], diagonal_mask(off))


def other_pairs(table, advance):
    def step(i, carry):
        codes = [table[3 * i + j] for j in range(3)]
        advance([(lax.div(code, 8), lax.rem(code, 8)) for code in codes], None)
        return carry

    lax.fori_loop(0, 5, step, 0)


def flip_all(dest, blocks, cols):
    for i in range(2 * RING):
        dest[i] = blocks[i, :, cols].T


def flip_own(dest, blocks, cols, y, z):
    dest[z] = blocks[z, :, cols].T
    dest[RING + y] = blocks[RING + y, :, cols].T


def stats_kernel(meta, table, *refs):
    z_out, y_out, o_out, blocks, vt, top, total, sems = refs[16:]
    y, z = meta[0], meta[1]
    first, rest = fetch(refs, blocks, sems, y, z)
    top[...] = jnp.full_like(top, NEG_LARGE)
    total[...] = jnp.zeros_like(total)
    o_out[...] = jnp.zeros_like(o_out)

    def advance(pairs, allowed):
        scores = [dot_nt(blocks[k, :, KEY], blocks[q, :, QUERY]) * (SCALE * LOG2E) for q, k in pairs]
        if allowed is not None:
            scores = [jnp.where(allowed, score, NEG_LARGE) for score in scores]
        highs = [jnp.max(score, axis=0, keepdims=True) for score in scores]
        for (q, k), score, high in zip(pairs, scores, highs):
            old = top[q]
            new = jnp.maximum(old, high)
            probs = jnp.exp2(score - new)
            shrink = jnp.exp2(old - new)
            top[q] = new
            total[q] = total[q] * shrink + jnp.sum(probs, axis=0, keepdims=True)
            o_out[q] = o_out[q] * shrink + dot_nn(vt[k], probs.astype(BF16))

    for copy in first:
        copy.wait()
    flip_own(vt, blocks, VALUE, y, z)
    own_pairs(meta, advance)
    for copy in rest:
        copy.wait()
    flip_all(vt, blocks, VALUE)
    other_pairs(table, advance)
    for head, out in ((0, z_out), (1, y_out)):
        for i in range(RING):
            at = head * RING + i
            count = total[at]
            some = count > 0.0
            safe = jnp.where(some, count, 1.0)
            partial = o_out[at] / safe
            o_out[at] = partial
            flipped = blocks[at, :, COT].astype(F32).T
            out[i : i + 1, :] = jnp.where(some, top[at] + jnp.log(safe) * LOG2E, NEG_LARGE)
            out[RING + i : RING + i + 1, :] = jnp.sum(partial * flipped, axis=0, keepdims=True)


def whole(count):
    return [pl.BlockSpec(memory_space=pltpu.VMEM)] * count


def in_hbm(count):
    return [pl.BlockSpec(memory_space=pltpu.HBM)] * count


def smem(count):
    return [pl.BlockSpec(memory_space=pltpu.SMEM)] * count


def attention_stats(meta, table, pieces):
    row = pltpu.VMEM((2 * RING, 1, SEQ), F32)
    return pl.pallas_call(
        stats_kernel,
        out_shape=[jax.ShapeDtypeStruct((2 * RING, SEQ), F32)] * 2
        + [jax.ShapeDtypeStruct((2 * RING, HD, SEQ), F32)],
        in_specs=smem(2) + in_hbm(16),
        out_specs=whole(3),
        scratch_shapes=[
            pltpu.VMEM((2 * RING, SEQ, 4 * HD), BF16),
            pltpu.VMEM((2 * RING, HD, SEQ), BF16),
            row,
            row,
            pltpu.SemaphoreType.DMA((16,)),
        ],
        compiler_params=pltpu.CompilerParams(vmem_limit_bytes=STATS_LIMIT),
        cost_estimate=pl.CostEstimate(
            flops=17 * 2 * 2 * SEQ * SEQ * HD,
            bytes_accessed=5_000_000,
            transcendentals=17 * SEQ * SEQ,
        ),
        name="stats",
    )(meta, table, *pieces)


def grads_kernel(meta, table, *refs):
    o_part = refs[16]
    stats = (refs[17:21], refs[21:25])
    outs = refs[25:35]
    blocks, kt, lse, dots, keep, dq_sum, dk_sum, dv_sum, sems = refs[35:]
    y, z = meta[0], meta[1]
    first, rest = fetch(refs, blocks, sems, y, z)
    dq_sum[...] = jnp.zeros_like(dq_sum)
    dk_sum[...] = jnp.zeros_like(dk_sum)
    dv_sum[...] = jnp.zeros_like(dv_sum)
    for head in range(2):
        parts = [ref[...] for ref in stats[head]]
        logs = [part[:RING] for part in parts]
        top = functools.reduce(jnp.maximum, logs)
        shares = [jnp.exp2(log - top) for log in logs]
        norm = sum(shares)
        full = top + jnp.log(norm) * LOG2E
        dot = sum(share * part[RING:] for share, part in zip(shares, parts)) / norm
        weight = jnp.exp2(logs[0] - full)
        for i in range(RING):
            lse[head * RING + i] = full[i : i + 1]
            dots[head * RING + i] = dot[i : i + 1]
            keep[head * RING + i] = weight[i : i + 1]

    def advance(pairs, allowed):
        for q, k in pairs:
            query, cot = blocks[q, :, QUERY], blocks[q, :, COT]
            probs = jnp.exp2(dot_nt(blocks[k, :, KEY], query) * (SCALE * LOG2E) - lse[q])
            if allowed is not None:
                probs = jnp.where(allowed, probs, 0.0)
            prob_grads = dot_nt(blocks[k, :, VALUE], cot)
            slope = (probs * (prob_grads - dots[q]) * SCALE).astype(BF16)
            dv_sum[k] += dot_nn(probs.astype(BF16), cot)
            dk_sum[k] += dot_nn(slope, query)
            dq_sum[q] += dot_nn(kt[k], slope)

    for copy in first:
        copy.wait()
    flip_own(kt, blocks, KEY, y, z)
    own_pairs(meta, advance)
    for copy in rest:
        copy.wait()
    flip_all(kt, blocks, KEY)
    other_pairs(table, advance)
    half = SEQ // 2
    for base, at, parts in ((0, z, outs[:5]), (RING, y, outs[5:])):
        for rel, shift in enumerate(OFFSETS):
            slot = base + lax.rem(at + shift, RING)
            terms = (
                dq_sum[slot].T.astype(BF16),
                dk_sum[slot].astype(BF16),
                dv_sum[slot].astype(BF16),
                (o_part[slot] * keep[slot]).T.astype(BF16),
            )
            for cols, term in zip((QUERY, KEY, VALUE, COT), terms):
                if rel < 3:
                    parts[rel][:, cols] = term
                else:
                    parts[3][:, cols] = term[:half]
                    parts[4][:, cols] = term[half:]


def attention_grads(meta, table, pieces, o_part, z_stats, y_stats):
    row = pltpu.VMEM((2 * RING, 1, SEQ), F32)
    tall = pltpu.VMEM((2 * RING, SEQ, HD), F32)
    flat = pltpu.VMEM((2 * RING, HD, SEQ), F32)
    full = jax.ShapeDtypeStruct((SEQ, 4 * HD), BF16)
    half = jax.ShapeDtypeStruct((SEQ // 2, 4 * HD), BF16)
    return pl.pallas_call(
        grads_kernel,
        out_shape=([full] * 3 + [half] * 2) * 2,
        in_specs=smem(2) + in_hbm(16) + whole(9),
        out_specs=whole(10),
        scratch_shapes=[
            pltpu.VMEM((2 * RING, SEQ, 4 * HD), BF16),
            pltpu.VMEM((2 * RING, HD, SEQ), BF16),
            row,
            row,
            row,
            flat,
            tall,
            tall,
            pltpu.SemaphoreType.DMA((16,)),
        ],
        compiler_params=pltpu.CompilerParams(vmem_limit_bytes=GRADS_LIMIT),
        cost_estimate=pl.CostEstimate(
            flops=17 * 5 * 2 * SEQ * SEQ * HD,
            bytes_accessed=10_000_000,
            transcendentals=17 * SEQ * SEQ,
        ),
        name="grads",
    )(meta, table, *pieces, o_part, *z_stats, *y_stats)


def tail_kernel(meta, slices, *refs):
    text, image = refs[6:8]
    weights = refs[8:11]
    gz, gy, own, oth, oth_before, oth_far = refs[11:17]
    z_parts, y_parts = refs[17:21], refs[21:25]
    held, products, sems = refs[25:]
    y, z = meta[0], meta[1]
    depths = [block_rows(slices, j) for j in range(8)]
    groups = stream(weights, held, sems, depths)
    for parts, grads in ((refs[:3], gz), (refs[3:6], gy)):
        grads[...] = total([part[...] for part in parts]).astype(BF16)
    width = 3 * HD
    rows = 256
    grads = jnp.concatenate([gz[:, :width], gy[:, :width]], axis=1)
    for rel, shift in enumerate(OFFSETS):
        depth = pl.ds(pl.multiple_of(lax.rem(y + shift, RING) * CHUNK, CHUNK), CHUNK)
        term = dot_nn(text[depth, :], grads[:PATCH]) + dot_nn(image[depth, :], grads[PATCH:])
        products[...] = term.astype(BF16)
        for other, other_shift in enumerate(OFFSETS):
            source = pl.ds(pl.multiple_of(lax.rem(z + other_shift, RING) * rows, rows), rows)
            z_parts[rel][other * rows : (other + 1) * rows, :] = products[source, :width]
            y_parts[other][rel * rows : (rel + 1) * rows, :] = products[source, width:]

    columns = [ref[:, cols] for cols in (QUERY, KEY, VALUE) for ref in (gz, gy)]
    columns = [columns[i] for i in (0, 1, 3, 2, 5, 4)]
    grads = jnp.concatenate(columns, axis=1)
    pieces = [own.at[i] for i in range(RING)]
    pieces += [oth.at[0], oth_before, oth.at[1], oth_far]
    for j, (depth, group) in enumerate(zip(depths, groups)):
        for copy in group:
            copy.wait()
        term = dot_nt(grads, held[depth, :]).astype(BF16)
        pieces[j][:PATCH] = term[:PATCH]
        at = pl.ds(pl.multiple_of(PATCH + slices[j] * 32, 32), 32)
        for i, piece in enumerate(pieces):
            piece[at, :] = term[PATCH + 32 * i : PATCH + 32 * (i + 1)]


def tail_grads(meta, slices, z_parts, y_parts, text, image, weights):
    piece = jax.ShapeDtypeStruct((CHUNK, 3 * HD), BF16)
    return pl.pallas_call(
        tail_kernel,
        out_shape=[jax.ShapeDtypeStruct((SEQ, 4 * HD), BF16)] * 2
        + [jax.ShapeDtypeStruct((RING, SEQ, SEQ), BF16)]
        + [jax.ShapeDtypeStruct((2, SEQ, SEQ), BF16)]
        + [jax.ShapeDtypeStruct((SEQ, SEQ), BF16)] * 2
        + [piece] * 8,
        in_specs=smem(2) + whole(8) + in_hbm(3),
        out_specs=whole(14),
        scratch_shapes=[
            pltpu.VMEM((4096, 6 * HD), BF16),
            pltpu.VMEM((CHUNK, 6 * HD), BF16),
            pltpu.SemaphoreType.DMA((8, 3)),
        ],
        compiler_params=pltpu.CompilerParams(vmem_limit_bytes=STREAM_LIMIT),
        cost_estimate=pl.CostEstimate(
            flops=4 * SEQ * 4096 * 768, bytes_accessed=8_000_000, transcendentals=0
        ),
        name="tail_grads",
    )(meta, slices, *z_parts, *y_parts, text, image, *from_hbm(*weights))


def x_before_kernel(kept, got, out):
    out[...] = total((kept[1], got[...])).astype(BF16)


def x_far_kernel(kept, got, out):
    out[...] = total((kept[3], got[...])).astype(BF16)


def x_rest_kernel(kept, got, own, after):
    own[...] = total((kept[0], got[0])).astype(BF16)
    after[...] = total((kept[2], got[1])).astype(BF16)


def split_kernel(*refs):
    for parts, outs in ((refs[:3], refs[6:10]), (refs[3:6], refs[10:14])):
        for i, out in enumerate(outs):
            rows = slice(i * 256, (i + 1) * 256)
            out[...] = total([part[rows] for part in parts]).astype(out.dtype)


def split_phase(z_sum, y_sum):
    own = jax.ShapeDtypeStruct((256, 3 * HD), F32)
    other = jax.ShapeDtypeStruct((256, 3 * HD), BF16)
    outs = small_call(split_kernel, "split", [own, other, other, other] * 2, (), (*z_sum, *y_sum))
    return outs[:4], outs[4:]


def mixed_kernel(meta, own, before, after, text_out, image_out):
    off = meta[2]
    grads = total((own[...], before[...], after[...])).astype(BF16).astype(F32)
    text = grads[:PATCH]
    row = lax.broadcasted_iota(jnp.int32, (PATCH, 1), 0)
    text_out[:PATCH] = jnp.where(row < off, text, 0.0).astype(BF16)
    text_out[PATCH:] = jnp.where(row < off, 0.0, text).astype(BF16)
    for i in range(8):
        rows = slice(PATCH + 32 * i, PATCH + 32 * (i + 1))
        image_out[:, i * SEQ : (i + 1) * SEQ] = grads[rows].astype(BF16)


def mixed_grads(meta, parts):
    shapes = [jax.ShapeDtypeStruct((SEQ, SEQ), BF16), jax.ShapeDtypeStruct((32, 4096), BF16)]
    return small_call(mixed_kernel, "mixed_grads", shapes, (meta,), parts)


def final_kernel(*refs):
    z_sum = total([ref[...] for ref in refs[:4]])
    y_sum = total([ref[...] for ref in refs[4:8]])
    for cols, out, first, second in (
        (QUERY, refs[8], z_sum, y_sum),
        (KEY, refs[9], y_sum, z_sum),
        (VALUE, refs[10], y_sum, z_sum),
    ):
        out[:, :HD] = first[:, cols]
        out[:, HD:] = second[:, cols]


def final_sums(z_parts, y_parts):
    shape = jax.ShapeDtypeStruct((256, 2 * HD), F32)
    return small_call(final_kernel, "final_sums", [shape] * 3, (), (*z_parts, *y_parts))


def local(text_hidden, patch_rows, image_start, w_query, w_key, w_value, d_attn):
    ctx = lax.axis_index("ctx")
    y, z = ctx // RING, ctx % RING
    images, pieces, width = patch_rows.shape
    owners = image_start // SEQ
    off = jnp.sum(jnp.where(owners == ctx, image_start, 0)) - ctx * SEQ
    meta = jnp.stack([y, z, off]).astype(jnp.int32)
    table = lax.dynamic_index_in_dim(jnp.asarray(pair_table()), ctx, 0, keepdims=False)

    tp = lax.axis_index("tp")
    x, core = tp // 2, tp % 2
    columns = (x + jnp.asarray(OFFSETS, jnp.int32)) % RING
    slices = jnp.concatenate([columns * 2 + core, columns * 2 + 1 - core]).astype(jnp.int32)

    index = jnp.arange(SEQ, dtype=jnp.int32)
    rel = (index - PATCH) // 32
    shift = rel % RING
    shift = jnp.where(shift == 0, 0, jnp.where(shift == 1, 3, shift - 1))
    sender = 2 * ((x + shift) % RING) + jnp.where(rel < RING, core, 1 - core)
    text_pos = jnp.where(index < off, index, index + PATCH)
    image_pos = off + 16 * ((index % 32) // 2) + 2 * sender + index % 2
    pos = jnp.where(index < PATCH, text_pos, image_pos)
    placed = (index[:, None] == pos[None, :]).astype(BF16)

    by_shard = place_patches(owners, patch_rows)
    by_shard, text_hidden = lax.optimization_barrier((by_shard, text_hidden))
    arrived = lax.all_to_all(by_shard, "ctx", split_axis=0, concat_axis=0, tiled=True)
    kept = index[:PATCH, None] < off
    text = jnp.where(kept, text_hidden[:PATCH], text_hidden[PATCH:])
    t_ring = ring_gather(text, send_x)
    arrived, t_ring = lax.optimization_barrier((arrived, t_ring))
    t_far = jnp.concatenate(t_ring[3:], axis=0)
    t_own = jnp.concatenate([*t_ring[:3], t_far], axis=1)
    t_oth = send_core(t_own)

    image = arrived.reshape(images * pieces, width)
    before, after = send_x(image, 1), send_x(image, -1)
    cot = dot_tn(placed, d_attn).astype(BF16)
    weights = (w_query, w_key, w_value)
    half = image.shape[0] // 2
    far = (send_x(before[:half], 1), send_x(after[half:], -1))
    i_own = jnp.concatenate([image, before, after, *far], axis=0)
    i_oth = send_core(i_own)

    text_flipped, z_keep, y_keep, z_text, y_text, held = project_text(
        slices, t_own, t_oth, cot, weights
    )
    image_flipped, z_image, y_image = project_image(i_own, i_oth, cot, held)
    z_keep, y_keep = from_hbm(z_keep, y_keep)

    z_before, z_after = send_z(z_text, 1), send_z(z_text, -1)
    y_before, y_after = send_y(y_text, 1), send_y(y_text, -1)
    z_before, y_before, z_image = lax.optimization_barrier((z_before, y_before, z_image))
    z_image_before, z_image_after = send_z(z_image, 1), send_z(z_image, -1)
    y_image_before, y_image_after = send_y(y_image, 1), send_y(y_image, -1)
    z_ring = (z_keep, z_image, z_before, z_image_before, z_after, z_image_after)
    z_ring += (send_z(z_before, 1), send_z(z_image_after, -1))
    y_ring = (y_keep, y_image, y_before, y_image_before, y_after, y_image_after)
    y_ring += (send_y(y_before, 1), send_y(y_image_after, -1))
    operands = (*z_ring, *y_ring)
    z_stats, y_stats, o_part = attention_stats(meta, table, operands)
    z_stats = [z_stats] + [send_z(z_stats, step) for step in (1, -1, 2)]
    y_stats = [y_stats] + [send_y(y_stats, step) for step in (1, -1, 2)]
    outs = attention_grads(meta, table, operands, o_part, z_stats, y_stats)
    z_parts, y_parts = ring_scatter(outs[:5], send_z), ring_scatter(outs[5:], send_y)
    gz, gy, kept_part, sent_part, sent_before, sent_far, *parts = tail_grads(
        meta, slices, z_parts, y_parts, text_flipped, image_flipped, weights
    )
    x_shape = jax.ShapeDtypeStruct((SEQ, SEQ), BF16)
    got_far, got_before = send_core(sent_far), send_core(sent_before)
    got_part = send_core(sent_part)
    z_own, z_before, z_after, z_far = parts[:4]
    y_own, y_before, y_after, y_far = parts[4:]
    z_far, y_far = send_y(z_far, 1), send_z(y_far, 1)
    (x_far,) = small_call(x_far_kernel, "x_far", [x_shape], (), (kept_part, got_far))
    (x_before,) = small_call(x_before_kernel, "x_before", [x_shape], (), (kept_part, got_before))
    x_far, x_before = send_x(x_far, 1), send_x(x_before, -1)
    x_own, x_after = small_call(x_rest_kernel, "x_rest", [x_shape] * 2, (), (kept_part, got_part))
    x_after, z_before = lax.optimization_barrier((x_after, z_before))
    z_before = send_y(z_before, -1)
    x_after = total((x_after, x_far)).astype(BF16)
    x_after = send_x(x_after, 1)
    z_far, y_far, y_before = lax.optimization_barrier((z_far, y_far, y_before))
    z_sum = (z_own, send_y(total((z_after, z_far)).astype(BF16), 1), z_before)
    y_sum = (y_own, send_z(total((y_after, y_far)).astype(BF16), 1), send_z(y_before, -1))
    d_text, i_grad = mixed_grads(meta, (x_own, x_after, x_before))
    z_sum, y_sum, i_grad = lax.optimization_barrier((z_sum, y_sum, i_grad))

    attended = jnp.concatenate([gz[:, COT], gy[:, COT]], axis=1)
    attn_out = dot_nn(placed, attended).astype(BF16)

    z_pieces, y_pieces = split_phase(z_sum, y_sum)
    z_got, y_got = direct_scatter(z_pieces, send_z), direct_scatter(y_pieces, send_y)
    i_grad, z_first = lax.optimization_barrier((i_grad, z_got[1]))
    returned = lax.all_to_all(
        i_grad.reshape(images, pieces, width), "ctx", split_axis=0, concat_axis=0, tiled=True
    )
    d_patch = move_patches(take_kernel, "take_patches", owners, returned)
    dw_query, dw_key, dw_value = final_sums((z_got[0], z_first, *z_got[2:]), y_got)
    return (
        attn_out,
        d_text,
        d_patch,
        dw_query,
        dw_key,
        dw_value,
    )


def solution(mesh):
    in_specs = (
        P("ctx", "tp"),
        P(None, ("ctx", "tp"), None),
        P(),
        P(None, "tp"),
        P(None, "tp"),
        P(None, "tp"),
        P("ctx", "tp"),
    )
    out_specs = (
        P("ctx", "tp"),
        P("ctx", "tp"),
        P(None, ("ctx", "tp"), None),
        P("ctx", "tp"),
        P("ctx", "tp"),
        P("ctx", "tp"),
    )
    return jax.shard_map(local, mesh=mesh, in_specs=in_specs, out_specs=out_specs, check_vma=False)
```

```python
import functools
import math

import jax
import jax.numpy as jnp
import numpy as np
from jax import lax
from jax.experimental import pallas as pl
from jax.experimental.pallas import tpu as pltpu
from jax.sharding import PartitionSpec as P

HD = 128
PATCH = 256
SEQ = 512
RING = 4
OFFSETS = (0, 3, 1, 2)
NEG_LARGE = -1e30
SCALE = 1.0 / math.sqrt(HD)
LOG2E = math.log2(math.e)
SMALL_LIMIT = 8 * 1024 * 1024
STREAM_LIMIT = 15 * 1024 * 1024
STATS_LIMIT = 16 * 1024 * 1024
GRADS_LIMIT = 22 * 1024 * 1024
Z_GROUPS = [[RING * y + z for z in range(RING)] for y in range(RING)]
Y_GROUPS = [[RING * y + z for y in range(RING)] for z in range(RING)]
BF16 = jnp.bfloat16
F32 = jnp.float32


def pair_table():
    rows = []
    for ctx in range(RING * RING):
        y, z = divmod(ctx, RING)
        own = []
        for q in range(RING):
            for k in range(RING):
                if RING * k + z < RING * y + q:
                    own.append(8 * q + RING + k)
                if RING * y + k < RING * q + z:
                    own.append(8 * (RING + q) + k)
        assert len(own) == 15
        rows.append(own)
    return np.asarray(rows, np.int32)


def ctx_send(value, dy, dz):
    perm = [
        (RING * y + z, RING * ((y + dy) % RING) + (z + dz) % RING)
        for y in range(RING)
        for z in range(RING)
    ]
    return lax.ppermute(value, "ctx", perm)


def send_z(value, step):
    return ctx_send(value, 0, step)


def send_y(value, step):
    return ctx_send(value, step, 0)


def send_x(value, step):
    perm = [(2 * x + core, 2 * ((x + step) % RING) + core) for x in range(RING) for core in range(2)]
    return lax.ppermute(value, "tp", perm)


def send_core(value):
    return lax.ppermute(value, "tp", [(i, i ^ 1) for i in range(2 * RING)])


def ring_gather(value, send):
    half = value.shape[0] // 2
    before = send(value, 1)
    after = send(value, -1)
    far_low = send(before[:half], 1)
    far_high = send(after[half:], -1)
    return value, before, after, far_low, far_high


def add_to(piece, part, at):
    total = (lax.slice_in_dim(piece, at, at + part.shape[0]).astype(F32) + part.astype(F32)).astype(BF16)
    return lax.dynamic_update_slice_in_dim(piece, total, at, 0)


def scatter_far(pieces, send):
    own, before, after, far_low, far_high = pieces
    after = add_to(after, send(far_low, 1), 0)
    before = add_to(before, send(far_high, -1), far_low.shape[0])
    return own, before, after


def scatter_near(pieces, send):
    own, before, after = pieces
    return own, send(after, 1), send(before, -1)


def ring_scatter(pieces, send):
    return scatter_near(scatter_far(pieces, send), send)


def direct_scatter(pieces, send):
    own, before, after, far = pieces
    return own, send(before, -1), send(after, 1), send(far, 2)


def total(parts):
    return sum(part.astype(F32) for part in parts)


def dot_nn(a, b):
    return jnp.dot(a, b, preferred_element_type=F32)


def dot_nt(a, b):
    return lax.dot_general(a, b, (((1,), (1,)), ((), ())), preferred_element_type=F32)


def dot_tn(a, b):
    return lax.dot_general(a, b, (((0,), (0,)), ((), ())), preferred_element_type=F32)


def small_call(body, name, out_shape, scalars, operands, flops=2_000_000):
    return pl.pallas_call(
        body,
        out_shape=out_shape,
        in_specs=smem(len(scalars)) + whole(len(operands)),
        out_specs=whole(len(out_shape)),
        compiler_params=pltpu.CompilerParams(vmem_limit_bytes=SMALL_LIMIT),
        cost_estimate=pl.CostEstimate(flops=flops, bytes_accessed=2_000_000, transcendentals=0),
        name=name,
    )(*scalars, *operands)


def place_kernel(owners, patches, out, sems):
    copies = [
        pltpu.make_async_copy(patches.at[k], out.at[owners[k]], sems.at[k])
        for k in range(16)
    ]
    for copy in copies:
        copy.start()
    for copy in copies:
        copy.wait()


def place_patches(owners, patches):
    return pl.pallas_call(
        place_kernel,
        out_shape=jax.ShapeDtypeStruct(patches.shape, BF16),
        in_specs=smem(1) + in_hbm(1),
        out_specs=whole(1)[0],
        scratch_shapes=[pltpu.SemaphoreType.DMA((16,))],
        compiler_params=pltpu.CompilerParams(vmem_limit_bytes=SMALL_LIMIT),
        cost_estimate=pl.CostEstimate(flops=0, bytes_accessed=500_000, transcendentals=0),
        name="place_patches",
    )(owners, *from_hbm(patches))


def take_kernel(owners, returned, out):
    for k in range(16):
        out[k] = returned[owners[k]]


def move_patches(body, name, owners, patches):
    shape = [jax.ShapeDtypeStruct(patches.shape, BF16)]
    return small_call(body, name, shape, (owners,), (patches,))[0]


QUERY, KEY, VALUE, COT = (slice(i * HD, (i + 1) * HD) for i in range(4))
CHUNK = 1024
CHUNKS = 4096 // CHUNK


def pack(acc, cot, z_out, y_out):
    for head, cols, out in ((0, (0, 3, 5), z_out), (1, (1, 2, 4), y_out)):
        for at, col in enumerate(cols):
            out[:, at * HD : (at + 1) * HD] = acc[:, col * HD : (col + 1) * HD].astype(BF16)
        out[:, COT] = cot[:, head * HD : (head + 1) * HD]


def block_rows(slices, j):
    return pl.ds(pl.multiple_of(slices[j] * SEQ, SEQ), SEQ)


def stream(weights, held, sems, depths):
    groups = []
    for j, depth in enumerate(depths):
        groups.append(
            [
                pltpu.make_async_copy(
                    ref.at[depth], held.at[depth, i * 256 : (i + 1) * 256], sems.at[j, i]
                )
                for i, ref in enumerate(weights)
            ]
        )
    for group in groups:
        for copy in group:
            copy.start()
    return groups


def text_kernel(slices, own, oth, cot, wq, wk, wv, flipped, z_keep, y_keep, z_out, y_out, held, turned, sems):
    depths = [block_rows(slices, j) for j in range(8)]
    groups = stream((wq, wk, wv), held, sems, depths)
    acc = None
    outgoing = []
    for j, (depth, group) in enumerate(zip(depths, groups)):
        part = own if j < RING else oth
        block = part[:, (j % RING) * SEQ : (j % RING + 1) * SEQ]
        turned[depth, :] = block.T
        outgoing.append(pltpu.make_async_copy(turned.at[depth], flipped.at[depth], sems.at[j, 3]))
        outgoing[-1].start()
        for copy in group:
            copy.wait()
        term = dot_nn(block, held[depth, :])
        acc = term if acc is None else acc + term
    pack(acc, cot[:PATCH], z_out, y_out)
    for i, (out, keep) in enumerate(((z_out, z_keep), (y_out, y_keep))):
        outgoing.append(pltpu.make_async_copy(out, keep, sems.at[8, i]))
        outgoing[-1].start()
    for copy in outgoing:
        copy.wait()


def image_kernel(own, oth, cot, held, flipped, z_out, y_out, turned, sems):
    acc = None
    outgoing = []
    for j in range(CHUNKS):
        depth = slice(j * CHUNK, (j + 1) * CHUNK)
        block = jnp.concatenate([own[:, depth], oth[:, depth]], axis=0)
        turned[depth, :] = block.T
        outgoing.append(pltpu.make_async_copy(turned.at[depth], flipped.at[depth], sems.at[j]))
        outgoing[-1].start()
        term = dot_nn(block, held[depth, :])
        acc = term if acc is None else acc + term
    pack(acc, cot[PATCH:], z_out, y_out)
    for copy in outgoing:
        copy.wait()


def from_hbm(*arrays):
    return [pltpu.with_memory_space_constraint(array, pltpu.HBM) for array in arrays]


def project_text(slices, own, oth, cot, weights):
    rows = (PATCH, 4 * HD)
    return pl.pallas_call(
        text_kernel,
        out_shape=[pltpu.HBM((4096, PATCH), BF16)]
        + [pltpu.HBM(rows, BF16)] * 2
        + [jax.ShapeDtypeStruct(rows, BF16)] * 2
        + [jax.ShapeDtypeStruct((4096, 6 * HD), BF16)],
        in_specs=smem(1) + whole(3) + in_hbm(3),
        out_specs=in_hbm(3) + whole(3),
        scratch_shapes=[pltpu.VMEM((4096, PATCH), BF16), pltpu.SemaphoreType.DMA((9, 4))],
        compiler_params=pltpu.CompilerParams(vmem_limit_bytes=SMALL_LIMIT),
        cost_estimate=pl.CostEstimate(
            flops=2 * PATCH * 4096 * 768, bytes_accessed=8_000_000, transcendentals=0
        ),
        name="qkv_text",
    )(slices, own, oth, cot, *from_hbm(*weights))


def project_image(own, oth, cot, held):
    rows = (PATCH, 4 * HD)
    return pl.pallas_call(
        image_kernel,
        out_shape=[pltpu.HBM((4096, PATCH), BF16)] + [jax.ShapeDtypeStruct(rows, BF16)] * 2,
        in_specs=whole(4),
        out_specs=in_hbm(1) + whole(2),
        scratch_shapes=[pltpu.VMEM((4096, PATCH), BF16), pltpu.SemaphoreType.DMA((CHUNKS,))],
        compiler_params=pltpu.CompilerParams(vmem_limit_bytes=SMALL_LIMIT),
        cost_estimate=pl.CostEstimate(
            flops=2 * PATCH * 4096 * 768, bytes_accessed=2_000_000, transcendentals=0
        ),
        name="qkv_image",
    )(own, oth, cot, held)


def ranks(off, shape, dim):
    index = lax.broadcasted_iota(jnp.int32, shape, dim)
    return jnp.where(index < PATCH, 2 * index, 2 * off - 1)


def diagonal_mask(off):
    return ranks(off, (SEQ, 1), 0) <= ranks(off, (1, SEQ), 1)


def fetch(refs, blocks, sems, y, z):
    copies = []
    for base, at, parts in ((0, z, refs[0:8]), (RING, y, refs[8:16])):
        for rel, off in enumerate(OFFSETS):
            slot = base + lax.rem(at + off, RING)
            for half in range(2):
                target = blocks.at[slot, half * PATCH : (half + 1) * PATCH]
                part = parts[2 * rel + half]
                copies.append(pltpu.make_async_copy(part, target, sems.at[len(copies)]))
    first = copies[0:2] + copies[8:10]
    rest = copies[2:8] + copies[10:]
    for copy in first + rest:
        copy.start()
    return first, rest


def own_pairs(meta, advance):
    y, z, off = meta[0], meta[1], meta[2]
    advance([(z, RING + y), (RING + y, z)], diagonal_mask(off))


def other_pairs(table, advance):
    def step(i, carry):
        codes = [table[3 * i + j] for j in range(3)]
        advance([(lax.div(code, 8), lax.rem(code, 8)) for code in codes], None)
        return carry

    lax.fori_loop(0, 5, step, 0)


def flip_all(dest, blocks, cols):
    for i in range(2 * RING):
        dest[i] = blocks[i, :, cols].T


def flip_own(dest, blocks, cols, y, z):
    dest[z] = blocks[z, :, cols].T
    dest[RING + y] = blocks[RING + y, :, cols].T


def stats_kernel(meta, table, *refs):
    z_out, y_out, o_out, blocks, vt, top, total, sems = refs[16:]
    y, z = meta[0], meta[1]
    first, rest = fetch(refs, blocks, sems, y, z)
    top[...] = jnp.full_like(top, NEG_LARGE)
    total[...] = jnp.zeros_like(total)
    o_out[...] = jnp.zeros_like(o_out)

    def advance(pairs, allowed):
        scores = [dot_nt(blocks[k, :, KEY], blocks[q, :, QUERY]) * (SCALE * LOG2E) for q, k in pairs]
        if allowed is not None:
            scores = [jnp.where(allowed, score, NEG_LARGE) for score in scores]
        highs = [jnp.max(score, axis=0, keepdims=True) for score in scores]
        for (q, k), score, high in zip(pairs, scores, highs):
            old = top[q]
            new = jnp.maximum(old, high)
            probs = jnp.exp2(score - new)
            shrink = jnp.exp2(old - new)
            top[q] = new
            total[q] = total[q] * shrink + jnp.sum(probs, axis=0, keepdims=True)
            o_out[q] = o_out[q] * shrink + dot_nn(vt[k], probs.astype(BF16))

    for copy in first:
        copy.wait()
    flip_own(vt, blocks, VALUE, y, z)
    own_pairs(meta, advance)
    for copy in rest:
        copy.wait()
    flip_all(vt, blocks, VALUE)
    other_pairs(table, advance)
    for head, out in ((0, z_out), (1, y_out)):
        for i in range(RING):
            at = head * RING + i
            count = total[at]
            some = count > 0.0
            safe = jnp.where(some, count, 1.0)
            partial = o_out[at] / safe
            o_out[at] = partial
            flipped = blocks[at, :, COT].astype(F32).T
            out[i : i + 1, :] = jnp.where(some, top[at] + jnp.log(safe) * LOG2E, NEG_LARGE)
            out[RING + i : RING + i + 1, :] = jnp.sum(partial * flipped, axis=0, keepdims=True)


def whole(count):
    return [pl.BlockSpec(memory_space=pltpu.VMEM)] * count


def in_hbm(count):
    return [pl.BlockSpec(memory_space=pltpu.HBM)] * count


def smem(count):
    return [pl.BlockSpec(memory_space=pltpu.SMEM)] * count


def attention_stats(meta, table, pieces):
    row = pltpu.VMEM((2 * RING, 1, SEQ), F32)
    return pl.pallas_call(
        stats_kernel,
        out_shape=[jax.ShapeDtypeStruct((2 * RING, SEQ), F32)] * 2
        + [jax.ShapeDtypeStruct((2 * RING, HD, SEQ), F32)],
        in_specs=smem(2) + in_hbm(16),
        out_specs=whole(3),
        scratch_shapes=[
            pltpu.VMEM((2 * RING, SEQ, 4 * HD), BF16),
            pltpu.VMEM((2 * RING, HD, SEQ), BF16),
            row,
            row,
            pltpu.SemaphoreType.DMA((16,)),
        ],
        compiler_params=pltpu.CompilerParams(vmem_limit_bytes=STATS_LIMIT),
        cost_estimate=pl.CostEstimate(
            flops=17 * 2 * 2 * SEQ * SEQ * HD,
            bytes_accessed=5_000_000,
            transcendentals=17 * SEQ * SEQ,
        ),
        name="stats",
    )(meta, table, *pieces)


def grads_kernel(meta, table, *refs):
    o_part = refs[16]
    stats = (refs[17:21], refs[21:25])
    outs = refs[25:35]
    blocks, kt, lse, dots, keep, dq_sum, dk_sum, dv_sum, sems = refs[35:]
    y, z = meta[0], meta[1]
    first, rest = fetch(refs, blocks, sems, y, z)
    dq_sum[...] = jnp.zeros_like(dq_sum)
    dk_sum[...] = jnp.zeros_like(dk_sum)
    dv_sum[...] = jnp.zeros_like(dv_sum)
    for head in range(2):
        parts = [ref[...] for ref in stats[head]]
        logs = [part[:RING] for part in parts]
        top = functools.reduce(jnp.maximum, logs)
        shares = [jnp.exp2(log - top) for log in logs]
        norm = sum(shares)
        full = top + jnp.log(norm) * LOG2E
        dot = sum(share * part[RING:] for share, part in zip(shares, parts)) / norm
        weight = jnp.exp2(logs[0] - full)
        for i in range(RING):
            lse[head * RING + i] = full[i : i + 1]
            dots[head * RING + i] = dot[i : i + 1]
            keep[head * RING + i] = weight[i : i + 1]

    def advance(pairs, allowed):
        for q, k in pairs:
            query, cot = blocks[q, :, QUERY], blocks[q, :, COT]
            probs = jnp.exp2(dot_nt(blocks[k, :, KEY], query) * (SCALE * LOG2E) - lse[q])
            if allowed is not None:
                probs = jnp.where(allowed, probs, 0.0)
            prob_grads = dot_nt(blocks[k, :, VALUE], cot)
            slope = (probs * (prob_grads - dots[q]) * SCALE).astype(BF16)
            dv_sum[k] += dot_nn(probs.astype(BF16), cot)
            dk_sum[k] += dot_nn(slope, query)
            dq_sum[q] += dot_nn(kt[k], slope)

    for copy in first:
        copy.wait()
    flip_own(kt, blocks, KEY, y, z)
    own_pairs(meta, advance)
    for copy in rest:
        copy.wait()
    flip_all(kt, blocks, KEY)
    other_pairs(table, advance)
    half = SEQ // 2
    for base, at, parts in ((0, z, outs[:5]), (RING, y, outs[5:])):
        for rel, shift in enumerate(OFFSETS):
            slot = base + lax.rem(at + shift, RING)
            terms = (
                dq_sum[slot].T.astype(BF16),
                dk_sum[slot].astype(BF16),
                dv_sum[slot].astype(BF16),
                (o_part[slot] * keep[slot]).T.astype(BF16),
            )
            for cols, term in zip((QUERY, KEY, VALUE, COT), terms):
                if rel < 3:
                    parts[rel][:, cols] = term
                else:
                    parts[3][:, cols] = term[:half]
                    parts[4][:, cols] = term[half:]


def attention_grads(meta, table, pieces, o_part, z_stats, y_stats):
    row = pltpu.VMEM((2 * RING, 1, SEQ), F32)
    tall = pltpu.VMEM((2 * RING, SEQ, HD), F32)
    flat = pltpu.VMEM((2 * RING, HD, SEQ), F32)
    full = jax.ShapeDtypeStruct((SEQ, 4 * HD), BF16)
    half = jax.ShapeDtypeStruct((SEQ // 2, 4 * HD), BF16)
    return pl.pallas_call(
        grads_kernel,
        out_shape=([full] * 3 + [half] * 2) * 2,
        in_specs=smem(2) + in_hbm(16) + whole(9),
        out_specs=whole(10),
        scratch_shapes=[
            pltpu.VMEM((2 * RING, SEQ, 4 * HD), BF16),
            pltpu.VMEM((2 * RING, HD, SEQ), BF16),
            row,
            row,
            row,
            flat,
            tall,
            tall,
            pltpu.SemaphoreType.DMA((16,)),
        ],
        compiler_params=pltpu.CompilerParams(vmem_limit_bytes=GRADS_LIMIT),
        cost_estimate=pl.CostEstimate(
            flops=17 * 5 * 2 * SEQ * SEQ * HD,
            bytes_accessed=10_000_000,
            transcendentals=17 * SEQ * SEQ,
        ),
        name="grads",
    )(meta, table, *pieces, o_part, *z_stats, *y_stats)


def tail_kernel(meta, slices, *refs):
    text, image = refs[6:8]
    weights = refs[8:11]
    gz, gy, own, oth, oth_before, oth_far = refs[11:17]
    z_parts, y_parts = refs[17:21], refs[21:25]
    held, products, sems = refs[25:]
    y, z = meta[0], meta[1]
    depths = [block_rows(slices, j) for j in range(8)]
    groups = stream(weights, held, sems, depths)
    for parts, grads in ((refs[:3], gz), (refs[3:6], gy)):
        grads[...] = total([part[...] for part in parts]).astype(BF16)
    width = 3 * HD
    rows = 256
    grads = jnp.concatenate([gz[:, :width], gy[:, :width]], axis=1)
    for rel, shift in enumerate(OFFSETS):
        depth = pl.ds(pl.multiple_of(lax.rem(y + shift, RING) * CHUNK, CHUNK), CHUNK)
        term = dot_nn(text[depth, :], grads[:PATCH]) + dot_nn(image[depth, :], grads[PATCH:])
        products[...] = term.astype(BF16)
        for other, other_shift in enumerate(OFFSETS):
            source = pl.ds(pl.multiple_of(lax.rem(z + other_shift, RING) * rows, rows), rows)
            z_parts[rel][other * rows : (other + 1) * rows, :] = products[source, :width]
            y_parts[other][rel * rows : (rel + 1) * rows, :] = products[source, width:]

    columns = [ref[:, cols] for cols in (QUERY, KEY, VALUE) for ref in (gz, gy)]
    columns = [columns[i] for i in (0, 1, 3, 2, 5, 4)]
    grads = jnp.concatenate(columns, axis=1)
    pieces = [own.at[i] for i in range(RING)]
    pieces += [oth.at[0], oth_before, oth.at[1], oth_far]
    for j, (depth, group) in enumerate(zip(depths, groups)):
        for copy in group:
            copy.wait()
        term = dot_nt(grads, held[depth, :]).astype(BF16)
        pieces[j][:PATCH] = term[:PATCH]
        at = pl.ds(pl.multiple_of(PATCH + slices[j] * 32, 32), 32)
        for i, piece in enumerate(pieces):
            piece[at, :] = term[PATCH + 32 * i : PATCH + 32 * (i + 1)]


def tail_grads(meta, slices, z_parts, y_parts, text, image, weights):
    piece = jax.ShapeDtypeStruct((CHUNK, 3 * HD), BF16)
    return pl.pallas_call(
        tail_kernel,
        out_shape=[jax.ShapeDtypeStruct((SEQ, 4 * HD), BF16)] * 2
        + [jax.ShapeDtypeStruct((RING, SEQ, SEQ), BF16)]
        + [jax.ShapeDtypeStruct((2, SEQ, SEQ), BF16)]
        + [jax.ShapeDtypeStruct((SEQ, SEQ), BF16)] * 2
        + [piece] * 8,
        in_specs=smem(2) + whole(8) + in_hbm(3),
        out_specs=whole(14),
        scratch_shapes=[
            pltpu.VMEM((4096, 6 * HD), BF16),
            pltpu.VMEM((CHUNK, 6 * HD), BF16),
            pltpu.SemaphoreType.DMA((8, 3)),
        ],
        compiler_params=pltpu.CompilerParams(vmem_limit_bytes=STREAM_LIMIT),
        cost_estimate=pl.CostEstimate(
            flops=4 * SEQ * 4096 * 768, bytes_accessed=8_000_000, transcendentals=0
        ),
        name="tail_grads",
    )(meta, slices, *z_parts, *y_parts, text, image, *from_hbm(*weights))


def x_before_kernel(kept, got, out):
    out[...] = total((kept[1], got[...])).astype(BF16)


def x_far_kernel(kept, got, out):
    out[...] = total((kept[3], got[...])).astype(BF16)


def x_rest_kernel(kept, got, own, after):
    own[...] = total((kept[0], got[0])).astype(BF16)
    after[...] = total((kept[2], got[1])).astype(BF16)


def split_kernel(*refs):
    for parts, outs in ((refs[:3], refs[6:10]), (refs[3:6], refs[10:14])):
        for i, out in enumerate(outs):
            rows = slice(i * 256, (i + 1) * 256)
            out[...] = total([part[rows] for part in parts]).astype(out.dtype)


def split_phase(z_sum, y_sum):
    own = jax.ShapeDtypeStruct((256, 3 * HD), F32)
    other = jax.ShapeDtypeStruct((256, 3 * HD), BF16)
    outs = small_call(split_kernel, "split", [own, other, other, other] * 2, (), (*z_sum, *y_sum))
    return outs[:4], outs[4:]


def mixed_kernel(meta, own, before, after, text_out, image_out):
    off = meta[2]
    grads = total((own[...], before[...], after[...])).astype(BF16).astype(F32)
    text = grads[:PATCH]
    row = lax.broadcasted_iota(jnp.int32, (PATCH, 1), 0)
    text_out[:PATCH] = jnp.where(row < off, text, 0.0).astype(BF16)
    text_out[PATCH:] = jnp.where(row < off, 0.0, text).astype(BF16)
    for i in range(8):
        rows = slice(PATCH + 32 * i, PATCH + 32 * (i + 1))
        image_out[:, i * SEQ : (i + 1) * SEQ] = grads[rows].astype(BF16)


def mixed_grads(meta, parts):
    shapes = [jax.ShapeDtypeStruct((SEQ, SEQ), BF16), jax.ShapeDtypeStruct((32, 4096), BF16)]
    return small_call(mixed_kernel, "mixed_grads", shapes, (meta,), parts)


def final_kernel(*refs):
    z_sum = total([ref[...] for ref in refs[:4]])
    y_sum = total([ref[...] for ref in refs[4:8]])
    for cols, out, first, second in (
        (QUERY, refs[8], z_sum, y_sum),
        (KEY, refs[9], y_sum, z_sum),
        (VALUE, refs[10], y_sum, z_sum),
    ):
        out[:, :HD] = first[:, cols]
        out[:, HD:] = second[:, cols]


def final_sums(z_parts, y_parts):
    shape = jax.ShapeDtypeStruct((256, 2 * HD), F32)
    return small_call(final_kernel, "final_sums", [shape] * 3, (), (*z_parts, *y_parts))


def local(text_hidden, patch_rows, image_start, w_query, w_key, w_value, d_attn):
    ctx = lax.axis_index("ctx")
    y, z = ctx // RING, ctx % RING
    images, pieces, width = patch_rows.shape
    owners = image_start // SEQ
    off = jnp.sum(jnp.where(owners == ctx, image_start, 0)) - ctx * SEQ
    meta = jnp.stack([y, z, off]).astype(jnp.int32)
    table = lax.dynamic_index_in_dim(jnp.asarray(pair_table()), ctx, 0, keepdims=False)

    tp = lax.axis_index("tp")
    x, core = tp // 2, tp % 2
    columns = (x + jnp.asarray(OFFSETS, jnp.int32)) % RING
    slices = jnp.concatenate([columns * 2 + core, columns * 2 + 1 - core]).astype(jnp.int32)

    index = jnp.arange(SEQ, dtype=jnp.int32)
    rel = (index - PATCH) // 32
    shift = rel % RING
    shift = jnp.where(shift == 0, 0, jnp.where(shift == 1, 3, shift - 1))
    sender = 2 * ((x + shift) % RING) + jnp.where(rel < RING, core, 1 - core)
    text_pos = jnp.where(index < off, index, index + PATCH)
    image_pos = off + 16 * ((index % 32) // 2) + 2 * sender + index % 2
    pos = jnp.where(index < PATCH, text_pos, image_pos)
    placed = (index[:, None] == pos[None, :]).astype(BF16)

    by_shard = place_patches(owners, patch_rows)
    by_shard, text_hidden = lax.optimization_barrier((by_shard, text_hidden))
    arrived = lax.all_to_all(by_shard, "ctx", split_axis=0, concat_axis=0, tiled=True)
    kept = index[:PATCH, None] < off
    text = jnp.where(kept, text_hidden[:PATCH], text_hidden[PATCH:])
    t_ring = ring_gather(text, send_x)
    arrived, t_ring = lax.optimization_barrier((arrived, t_ring))
    t_far = jnp.concatenate(t_ring[3:], axis=0)
    t_own = jnp.concatenate([*t_ring[:3], t_far], axis=1)
    t_oth = send_core(t_own)

    image = arrived.reshape(images * pieces, width)
    before, after = send_x(image, 1), send_x(image, -1)
    cot = dot_tn(placed, d_attn).astype(BF16)
    weights = (w_query, w_key, w_value)
    half = image.shape[0] // 2
    far = (send_x(before[:half], 1), send_x(after[half:], -1))
    i_own = jnp.concatenate([image, before, after, *far], axis=0)
    i_oth = send_core(i_own)

    text_flipped, z_keep, y_keep, z_text, y_text, held = project_text(
        slices, t_own, t_oth, cot, weights
    )
    image_flipped, z_image, y_image = project_image(i_own, i_oth, cot, held)
    z_keep, y_keep = from_hbm(z_keep, y_keep)

    z_before, z_after = send_z(z_text, 1), send_z(z_text, -1)
    y_before, y_after = send_y(y_text, 1), send_y(y_text, -1)
    z_before, y_before, z_image = lax.optimization_barrier((z_before, y_before, z_image))
    z_image_before, z_image_after = send_z(z_image, 1), send_z(z_image, -1)
    y_image_before, y_image_after = send_y(y_image, 1), send_y(y_image, -1)
    z_ring = (z_keep, z_image, z_before, z_image_before, z_after, z_image_after)
    z_ring += (send_z(z_before, 1), send_z(z_image_after, -1))
    y_ring = (y_keep, y_image, y_before, y_image_before, y_after, y_image_after)
    y_ring += (send_y(y_before, 1), send_y(y_image_after, -1))
    operands = (*z_ring, *y_ring)
    z_stats, y_stats, o_part = attention_stats(meta, table, operands)
    z_stats = [z_stats] + [send_z(z_stats, step) for step in (1, -1, 2)]
    y_stats = [y_stats] + [send_y(y_stats, step) for step in (1, -1, 2)]
    outs = attention_grads(meta, table, operands, o_part, z_stats, y_stats)
    z_parts, y_parts = ring_scatter(outs[:5], send_z), ring_scatter(outs[5:], send_y)
    gz, gy, kept_part, sent_part, sent_before, sent_far, *parts = tail_grads(
        meta, slices, z_parts, y_parts, text_flipped, image_flipped, weights
    )
    x_shape = jax.ShapeDtypeStruct((SEQ, SEQ), BF16)
    got_far, got_before = send_core(sent_far), send_core(sent_before)
    got_part = send_core(sent_part)
    z_own, z_before, z_after, z_far = parts[:4]
    y_own, y_before, y_after, y_far = parts[4:]
    z_far, y_far = send_y(z_far, 1), send_z(y_far, 1)
    (x_far,) = small_call(x_far_kernel, "x_far", [x_shape], (), (kept_part, got_far))
    (x_before,) = small_call(x_before_kernel, "x_before", [x_shape], (), (kept_part, got_before))
    x_far, x_before = send_x(x_far, 1), send_x(x_before, -1)
    x_own, x_after = small_call(x_rest_kernel, "x_rest", [x_shape] * 2, (), (kept_part, got_part))
    x_after, z_before = lax.optimization_barrier((x_after, z_before))
    z_before = send_y(z_before, -1)
    x_after = total((x_after, x_far)).astype(BF16)
    x_after = send_x(x_after, 1)
    z_far, y_far, y_before = lax.optimization_barrier((z_far, y_far, y_before))
    z_sum = (z_own, send_y(total((z_after, z_far)).astype(BF16), 1), z_before)
    y_sum = (y_own, send_z(total((y_after, y_far)).astype(BF16), 1), send_z(y_before, -1))
    d_text, i_grad = mixed_grads(meta, (x_own, x_after, x_before))
    z_sum, y_sum, i_grad = lax.optimization_barrier((z_sum, y_sum, i_grad))

    attended = jnp.concatenate([gz[:, COT], gy[:, COT]], axis=1)
    attn_out = dot_nn(placed, attended).astype(BF16)

    returned = lax.all_to_all(
        i_grad.reshape(images, pieces, width), "ctx", split_axis=0, concat_axis=0, tiled=True
    )
    d_patch = move_patches(take_kernel, "take_patches", owners, returned)
    z_pieces, y_pieces = split_phase(z_sum, y_sum)
    z_got, y_got = direct_scatter(z_pieces, send_z), direct_scatter(y_pieces, send_y)
    dw_query, dw_key, dw_value = final_sums(z_got, y_got)
    return (
        attn_out,
        d_text,
        d_patch,
        dw_query,
        dw_key,
        dw_value,
    )


def solution(mesh):
    in_specs = (
        P("ctx", "tp"),
        P(None, ("ctx", "tp"), None),
        P(),
        P(None, "tp"),
        P(None, "tp"),
        P(None, "tp"),
        P("ctx", "tp"),
    )
    out_specs = (
        P("ctx", "tp"),
        P("ctx", "tp"),
        P(None, ("ctx", "tp"), None),
        P("ctx", "tp"),
        P("ctx", "tp"),
        P("ctx", "tp"),
    )
    return jax.shard_map(local, mesh=mesh, in_specs=in_specs, out_specs=out_specs, check_vma=False)
```

```python
import functools
import math

import jax
import jax.numpy as jnp
import numpy as np
from jax import lax
from jax.experimental import pallas as pl
from jax.experimental.pallas import tpu as pltpu
from jax.sharding import PartitionSpec as P

HD = 128
PATCH = 256
SEQ = 512
RING = 4
OFFSETS = (0, 3, 1, 2)
NEG_LARGE = -1e30
SCALE = 1.0 / math.sqrt(HD)
LOG2E = math.log2(math.e)
SMALL_LIMIT = 8 * 1024 * 1024
STREAM_LIMIT = 15 * 1024 * 1024
STATS_LIMIT = 16 * 1024 * 1024
GRADS_LIMIT = 22 * 1024 * 1024
Z_GROUPS = [[RING * y + z for z in range(RING)] for y in range(RING)]
Y_GROUPS = [[RING * y + z for y in range(RING)] for z in range(RING)]
BF16 = jnp.bfloat16
F32 = jnp.float32


def pair_table():
    rows = []
    for ctx in range(RING * RING):
        y, z = divmod(ctx, RING)
        own = []
        for q in range(RING):
            for k in range(RING):
                if RING * k + z < RING * y + q:
                    own.append(8 * q + RING + k)
                if RING * y + k < RING * q + z:
                    own.append(8 * (RING + q) + k)
        assert len(own) == 15
        rows.append(own)
    return np.asarray(rows, np.int32)


def ctx_send(value, dy, dz):
    perm = [
        (RING * y + z, RING * ((y + dy) % RING) + (z + dz) % RING)
        for y in range(RING)
        for z in range(RING)
    ]
    return lax.ppermute(value, "ctx", perm)


def send_z(value, step):
    return ctx_send(value, 0, step)


def send_y(value, step):
    return ctx_send(value, step, 0)


def send_x(value, step):
    perm = [(2 * x + core, 2 * ((x + step) % RING) + core) for x in range(RING) for core in range(2)]
    return lax.ppermute(value, "tp", perm)


def send_core(value):
    return lax.ppermute(value, "tp", [(i, i ^ 1) for i in range(2 * RING)])


def ring_gather(value, send):
    half = value.shape[0] // 2
    before = send(value, 1)
    after = send(value, -1)
    far_low = send(before[:half], 1)
    far_high = send(after[half:], -1)
    return value, before, after, far_low, far_high


def add_to(piece, part, at):
    total = (lax.slice_in_dim(piece, at, at + part.shape[0]).astype(F32) + part.astype(F32)).astype(BF16)
    return lax.dynamic_update_slice_in_dim(piece, total, at, 0)


def scatter_far(pieces, send):
    own, before, after, far_low, far_high = pieces
    after = add_to(after, send(far_low, 1), 0)
    before = add_to(before, send(far_high, -1), far_low.shape[0])
    return own, before, after


def scatter_near(pieces, send):
    own, before, after = pieces
    return own, send(after, 1), send(before, -1)


def ring_scatter(pieces, send):
    return scatter_near(scatter_far(pieces, send), send)


def direct_scatter(pieces, send):
    own, before, after, far = pieces
    return own, send(before, -1), send(after, 1), send(far, 2)


def total(parts):
    return sum(part.astype(F32) for part in parts)


def dot_nn(a, b):
    return jnp.dot(a, b, preferred_element_type=F32)


def dot_nt(a, b):
    return lax.dot_general(a, b, (((1,), (1,)), ((), ())), preferred_element_type=F32)


def dot_tn(a, b):
    return lax.dot_general(a, b, (((0,), (0,)), ((), ())), preferred_element_type=F32)


def small_call(body, name, out_shape, scalars, operands, flops=2_000_000):
    return pl.pallas_call(
        body,
        out_shape=out_shape,
        in_specs=smem(len(scalars)) + whole(len(operands)),
        out_specs=whole(len(out_shape)),
        compiler_params=pltpu.CompilerParams(vmem_limit_bytes=SMALL_LIMIT),
        cost_estimate=pl.CostEstimate(flops=flops, bytes_accessed=2_000_000, transcendentals=0),
        name=name,
    )(*scalars, *operands)


def place_kernel(owners, patches, out, sems):
    copies = [
        pltpu.make_async_copy(patches.at[k], out.at[owners[k]], sems.at[k])
        for k in range(16)
    ]
    for copy in copies:
        copy.start()
    for copy in copies:
        copy.wait()


def place_patches(owners, patches):
    return pl.pallas_call(
        place_kernel,
        out_shape=jax.ShapeDtypeStruct(patches.shape, BF16),
        in_specs=smem(1) + in_hbm(1),
        out_specs=whole(1)[0],
        scratch_shapes=[pltpu.SemaphoreType.DMA((16,))],
        compiler_params=pltpu.CompilerParams(vmem_limit_bytes=SMALL_LIMIT),
        cost_estimate=pl.CostEstimate(flops=0, bytes_accessed=500_000, transcendentals=0),
        name="place_patches",
    )(owners, *from_hbm(patches))


def take_kernel(owners, returned, out):
    for k in range(16):
        out[k] = returned[owners[k]]


def move_patches(body, name, owners, patches):
    shape = [jax.ShapeDtypeStruct(patches.shape, BF16)]
    return small_call(body, name, shape, (owners,), (patches,))[0]


QUERY, KEY, VALUE, COT = (slice(i * HD, (i + 1) * HD) for i in range(4))
CHUNK = 1024
CHUNKS = 4096 // CHUNK


def pack(acc, cot, z_out, y_out):
    for head, cols, out in ((0, (0, 3, 5), z_out), (1, (1, 2, 4), y_out)):
        for at, col in enumerate(cols):
            out[:, at * HD : (at + 1) * HD] = acc[:, col * HD : (col + 1) * HD].astype(BF16)
        out[:, COT] = cot[:, head * HD : (head + 1) * HD]


def block_rows(slices, j):
    return pl.ds(pl.multiple_of(slices[j] * SEQ, SEQ), SEQ)


def stream(weights, held, sems, depths):
    groups = []
    for j, depth in enumerate(depths):
        groups.append(
            [
                pltpu.make_async_copy(
                    ref.at[depth], held.at[depth, i * 256 : (i + 1) * 256], sems.at[j, i]
                )
                for i, ref in enumerate(weights)
            ]
        )
    for group in groups:
        for copy in group:
            copy.start()
    return groups


def text_kernel(slices, own, oth, cot, wq, wk, wv, flipped, z_keep, y_keep, z_out, y_out, held, turned, sems):
    depths = [block_rows(slices, j) for j in range(8)]
    groups = stream((wq, wk, wv), held, sems, depths)
    acc = None
    outgoing = []
    for j, (depth, group) in enumerate(zip(depths, groups)):
        part = own if j < RING else oth
        block = part[:, (j % RING) * SEQ : (j % RING + 1) * SEQ]
        turned[depth, :] = block.T
        outgoing.append(pltpu.make_async_copy(turned.at[depth], flipped.at[depth], sems.at[j, 3]))
        outgoing[-1].start()
        for copy in group:
            copy.wait()
        term = dot_nn(block, held[depth, :])
        acc = term if acc is None else acc + term
    pack(acc, cot[:PATCH], z_out, y_out)
    for i, (out, keep) in enumerate(((z_out, z_keep), (y_out, y_keep))):
        outgoing.append(pltpu.make_async_copy(out, keep, sems.at[8, i]))
        outgoing[-1].start()
    for copy in outgoing:
        copy.wait()


def image_kernel(own, oth, cot, held, flipped, z_out, y_out, turned, sems):
    acc = None
    outgoing = []
    for j in range(CHUNKS):
        depth = slice(j * CHUNK, (j + 1) * CHUNK)
        block = jnp.concatenate([own[:, depth], oth[:, depth]], axis=0)
        turned[depth, :] = block.T
        outgoing.append(pltpu.make_async_copy(turned.at[depth], flipped.at[depth], sems.at[j]))
        outgoing[-1].start()
        term = dot_nn(block, held[depth, :])
        acc = term if acc is None else acc + term
    pack(acc, cot[PATCH:], z_out, y_out)
    for copy in outgoing:
        copy.wait()


def from_hbm(*arrays):
    return [pltpu.with_memory_space_constraint(array, pltpu.HBM) for array in arrays]


def project_text(slices, own, oth, cot, weights):
    rows = (PATCH, 4 * HD)
    return pl.pallas_call(
        text_kernel,
        out_shape=[pltpu.HBM((4096, PATCH), BF16)]
        + [pltpu.HBM(rows, BF16)] * 2
        + [jax.ShapeDtypeStruct(rows, BF16)] * 2
        + [jax.ShapeDtypeStruct((4096, 6 * HD), BF16)],
        in_specs=smem(1) + whole(3) + in_hbm(3),
        out_specs=in_hbm(3) + whole(3),
        scratch_shapes=[pltpu.VMEM((4096, PATCH), BF16), pltpu.SemaphoreType.DMA((9, 4))],
        compiler_params=pltpu.CompilerParams(vmem_limit_bytes=SMALL_LIMIT),
        cost_estimate=pl.CostEstimate(
            flops=2 * PATCH * 4096 * 768, bytes_accessed=8_000_000, transcendentals=0
        ),
        name="qkv_text",
    )(slices, own, oth, cot, *from_hbm(*weights))


def project_image(own, oth, cot, held):
    rows = (PATCH, 4 * HD)
    return pl.pallas_call(
        image_kernel,
        out_shape=[pltpu.HBM((4096, PATCH), BF16)] + [jax.ShapeDtypeStruct(rows, BF16)] * 2,
        in_specs=whole(4),
        out_specs=in_hbm(1) + whole(2),
        scratch_shapes=[pltpu.VMEM((4096, PATCH), BF16), pltpu.SemaphoreType.DMA((CHUNKS,))],
        compiler_params=pltpu.CompilerParams(vmem_limit_bytes=SMALL_LIMIT),
        cost_estimate=pl.CostEstimate(
            flops=2 * PATCH * 4096 * 768, bytes_accessed=2_000_000, transcendentals=0
        ),
        name="qkv_image",
    )(own, oth, cot, held)


def ranks(off, shape, dim):
    index = lax.broadcasted_iota(jnp.int32, shape, dim)
    return jnp.where(index < PATCH, 2 * index, 2 * off - 1)


def diagonal_mask(off):
    return ranks(off, (SEQ, 1), 0) <= ranks(off, (1, SEQ), 1)


def fetch(refs, blocks, sems, y, z):
    copies = []
    for base, at, parts in ((0, z, refs[0:8]), (RING, y, refs[8:16])):
        for rel, off in enumerate(OFFSETS):
            slot = base + lax.rem(at + off, RING)
            for half in range(2):
                target = blocks.at[slot, half * PATCH : (half + 1) * PATCH]
                part = parts[2 * rel + half]
                copies.append(pltpu.make_async_copy(part, target, sems.at[len(copies)]))
    first = copies[0:2] + copies[8:10]
    rest = copies[2:8] + copies[10:]
    for copy in first + rest:
        copy.start()
    return first, rest


def own_pairs(meta, advance):
    y, z, off = meta[0], meta[1], meta[2]
    advance([(z, RING + y), (RING + y, z)], diagonal_mask(off))


def other_pairs(table, advance):
    def step(i, carry):
        codes = [table[3 * i + j] for j in range(3)]
        advance([(lax.div(code, 8), lax.rem(code, 8)) for code in codes], None)
        return carry

    lax.fori_loop(0, 5, step, 0)


def flip_all(dest, blocks, cols):
    for i in range(2 * RING):
        dest[i] = blocks[i, :, cols].T


def flip_own(dest, blocks, cols, y, z):
    dest[z] = blocks[z, :, cols].T
    dest[RING + y] = blocks[RING + y, :, cols].T


def stats_kernel(meta, table, *refs):
    z_out, y_out, o_out, blocks, vt, top, total, sems = refs[16:]
    y, z = meta[0], meta[1]
    first, rest = fetch(refs, blocks, sems, y, z)
    top[...] = jnp.full_like(top, NEG_LARGE)
    total[...] = jnp.zeros_like(total)
    o_out[...] = jnp.zeros_like(o_out)

    def advance(pairs, allowed):
        scores = [dot_nt(blocks[k, :, KEY], blocks[q, :, QUERY]) * (SCALE * LOG2E) for q, k in pairs]
        if allowed is not None:
            scores = [jnp.where(allowed, score, NEG_LARGE) for score in scores]
        highs = [jnp.max(score, axis=0, keepdims=True) for score in scores]
        for (q, k), score, high in zip(pairs, scores, highs):
            old = top[q]
            new = jnp.maximum(old, high)
            probs = jnp.exp2(score - new)
            shrink = jnp.exp2(old - new)
            top[q] = new
            total[q] = total[q] * shrink + jnp.sum(probs, axis=0, keepdims=True)
            o_out[q] = o_out[q] * shrink + dot_nn(vt[k], probs.astype(BF16))

    for copy in first:
        copy.wait()
    flip_own(vt, blocks, VALUE, y, z)
    own_pairs(meta, advance)
    for copy in rest:
        copy.wait()
    flip_all(vt, blocks, VALUE)
    other_pairs(table, advance)
    for head, out in ((0, z_out), (1, y_out)):
        for i in range(RING):
            at = head * RING + i
            count = total[at]
            some = count > 0.0
            safe = jnp.where(some, count, 1.0)
            partial = o_out[at] / safe
            o_out[at] = partial
            flipped = blocks[at, :, COT].astype(F32).T
            out[i : i + 1, :] = jnp.where(some, top[at] + jnp.log(safe) * LOG2E, NEG_LARGE)
            out[RING + i : RING + i + 1, :] = jnp.sum(partial * flipped, axis=0, keepdims=True)


def whole(count):
    return [pl.BlockSpec(memory_space=pltpu.VMEM)] * count


def in_hbm(count):
    return [pl.BlockSpec(memory_space=pltpu.HBM)] * count


def smem(count):
    return [pl.BlockSpec(memory_space=pltpu.SMEM)] * count


def attention_stats(meta, table, pieces):
    row = pltpu.VMEM((2 * RING, 1, SEQ), F32)
    return pl.pallas_call(
        stats_kernel,
        out_shape=[jax.ShapeDtypeStruct((2 * RING, SEQ), F32)] * 2
        + [jax.ShapeDtypeStruct((2 * RING, HD, SEQ), F32)],
        in_specs=smem(2) + in_hbm(16),
        out_specs=whole(3),
        scratch_shapes=[
            pltpu.VMEM((2 * RING, SEQ, 4 * HD), BF16),
            pltpu.VMEM((2 * RING, HD, SEQ), BF16),
            row,
            row,
            pltpu.SemaphoreType.DMA((16,)),
        ],
        compiler_params=pltpu.CompilerParams(vmem_limit_bytes=STATS_LIMIT),
        cost_estimate=pl.CostEstimate(
            flops=17 * 2 * 2 * SEQ * SEQ * HD,
            bytes_accessed=5_000_000,
            transcendentals=17 * SEQ * SEQ,
        ),
        name="stats",
    )(meta, table, *pieces)


def grads_kernel(meta, table, *refs):
    o_part = refs[16]
    stats = (refs[17:21], refs[21:25])
    outs = refs[25:35]
    blocks, kt, lse, dots, keep, dq_sum, dk_sum, dv_sum, sems = refs[35:]
    y, z = meta[0], meta[1]
    first, rest = fetch(refs, blocks, sems, y, z)
    dq_sum[...] = jnp.zeros_like(dq_sum)
    dk_sum[...] = jnp.zeros_like(dk_sum)
    dv_sum[...] = jnp.zeros_like(dv_sum)
    for head in range(2):
        parts = [ref[...] for ref in stats[head]]
        logs = [part[:RING] for part in parts]
        top = functools.reduce(jnp.maximum, logs)
        shares = [jnp.exp2(log - top) for log in logs]
        norm = sum(shares)
        full = top + jnp.log(norm) * LOG2E
        dot = sum(share * part[RING:] for share, part in zip(shares, parts)) / norm
        weight = jnp.exp2(logs[0] - full)
        for i in range(RING):
            lse[head * RING + i] = full[i : i + 1]
            dots[head * RING + i] = dot[i : i + 1]
            keep[head * RING + i] = weight[i : i + 1]

    def advance(pairs, allowed):
        for q, k in pairs:
            query, cot = blocks[q, :, QUERY], blocks[q, :, COT]
            probs = jnp.exp2(dot_nt(blocks[k, :, KEY], query) * (SCALE * LOG2E) - lse[q])
            if allowed is not None:
                probs = jnp.where(allowed, probs, 0.0)
            prob_grads = dot_nt(blocks[k, :, VALUE], cot)
            slope = (probs * (prob_grads - dots[q]) * SCALE).astype(BF16)
            dv_sum[k] += dot_nn(probs.astype(BF16), cot)
            dk_sum[k] += dot_nn(slope, query)
            dq_sum[q] += dot_nn(kt[k], slope)

    for copy in first:
        copy.wait()
    flip_own(kt, blocks, KEY, y, z)
    own_pairs(meta, advance)
    for copy in rest:
        copy.wait()
    flip_all(kt, blocks, KEY)
    other_pairs(table, advance)
    half = SEQ // 2
    for base, at, parts in ((0, z, outs[:5]), (RING, y, outs[5:])):
        for rel, shift in enumerate(OFFSETS):
            slot = base + lax.rem(at + shift, RING)
            terms = (
                dq_sum[slot].T.astype(BF16),
                dk_sum[slot].astype(BF16),
                dv_sum[slot].astype(BF16),
                (o_part[slot] * keep[slot]).T.astype(BF16),
            )
            for cols, term in zip((QUERY, KEY, VALUE, COT), terms):
                if rel < 3:
                    parts[rel][:, cols] = term
                else:
                    parts[3][:, cols] = term[:half]
                    parts[4][:, cols] = term[half:]


def attention_grads(meta, table, pieces, o_part, z_stats, y_stats):
    row = pltpu.VMEM((2 * RING, 1, SEQ), F32)
    tall = pltpu.VMEM((2 * RING, SEQ, HD), F32)
    flat = pltpu.VMEM((2 * RING, HD, SEQ), F32)
    full = jax.ShapeDtypeStruct((SEQ, 4 * HD), BF16)
    half = jax.ShapeDtypeStruct((SEQ // 2, 4 * HD), BF16)
    return pl.pallas_call(
        grads_kernel,
        out_shape=([full] * 3 + [half] * 2) * 2,
        in_specs=smem(2) + in_hbm(16) + whole(9),
        out_specs=whole(10),
        scratch_shapes=[
            pltpu.VMEM((2 * RING, SEQ, 4 * HD), BF16),
            pltpu.VMEM((2 * RING, HD, SEQ), BF16),
            row,
            row,
            row,
            flat,
            tall,
            tall,
            pltpu.SemaphoreType.DMA((16,)),
        ],
        compiler_params=pltpu.CompilerParams(vmem_limit_bytes=GRADS_LIMIT),
        cost_estimate=pl.CostEstimate(
            flops=17 * 5 * 2 * SEQ * SEQ * HD,
            bytes_accessed=10_000_000,
            transcendentals=17 * SEQ * SEQ,
        ),
        name="grads",
    )(meta, table, *pieces, o_part, *z_stats, *y_stats)


def tail_kernel(meta, slices, *refs):
    text, image = refs[6:8]
    weights = refs[8:11]
    gz, gy, own, oth, oth_before, oth_far = refs[11:17]
    z_parts, y_parts = refs[17:21], refs[21:25]
    held, products, sems = refs[25:]
    y, z = meta[0], meta[1]
    depths = [block_rows(slices, j) for j in range(8)]
    groups = stream(weights, held, sems, depths)
    for parts, grads in ((refs[:3], gz), (refs[3:6], gy)):
        grads[...] = total([part[...] for part in parts]).astype(BF16)
    width = 3 * HD
    rows = 256
    grads = jnp.concatenate([gz[:, :width], gy[:, :width]], axis=1)
    for rel, shift in enumerate(OFFSETS):
        depth = pl.ds(pl.multiple_of(lax.rem(y + shift, RING) * CHUNK, CHUNK), CHUNK)
        term = dot_nn(text[depth, :], grads[:PATCH]) + dot_nn(image[depth, :], grads[PATCH:])
        products[...] = term.astype(BF16)
        for other, other_shift in enumerate(OFFSETS):
            source = pl.ds(pl.multiple_of(lax.rem(z + other_shift, RING) * rows, rows), rows)
            z_parts[rel][other * rows : (other + 1) * rows, :] = products[source, :width]
            y_parts[other][rel * rows : (rel + 1) * rows, :] = products[source, width:]

    columns = [ref[:, cols] for cols in (QUERY, KEY, VALUE) for ref in (gz, gy)]
    columns = [columns[i] for i in (0, 1, 3, 2, 5, 4)]
    grads = jnp.concatenate(columns, axis=1)
    pieces = [own.at[i] for i in range(RING)]
    pieces += [oth.at[0], oth_before, oth.at[1], oth_far]
    for j, (depth, group) in enumerate(zip(depths, groups)):
        for copy in group:
            copy.wait()
        term = dot_nt(grads, held[depth, :]).astype(BF16)
        pieces[j][:PATCH] = term[:PATCH]
        at = pl.ds(pl.multiple_of(PATCH + slices[j] * 32, 32), 32)
        for i, piece in enumerate(pieces):
            piece[at, :] = term[PATCH + 32 * i : PATCH + 32 * (i + 1)]


def tail_grads(meta, slices, z_parts, y_parts, text, image, weights):
    piece = jax.ShapeDtypeStruct((CHUNK, 3 * HD), BF16)
    return pl.pallas_call(
        tail_kernel,
        out_shape=[jax.ShapeDtypeStruct((SEQ, 4 * HD), BF16)] * 2
        + [jax.ShapeDtypeStruct((RING, SEQ, SEQ), BF16)]
        + [jax.ShapeDtypeStruct((2, SEQ, SEQ), BF16)]
        + [jax.ShapeDtypeStruct((SEQ, SEQ), BF16)] * 2
        + [piece] * 8,
        in_specs=smem(2) + whole(8) + in_hbm(3),
        out_specs=whole(14),
        scratch_shapes=[
            pltpu.VMEM((4096, 6 * HD), BF16),
            pltpu.VMEM((CHUNK, 6 * HD), BF16),
            pltpu.SemaphoreType.DMA((8, 3)),
        ],
        compiler_params=pltpu.CompilerParams(vmem_limit_bytes=STREAM_LIMIT),
        cost_estimate=pl.CostEstimate(
            flops=4 * SEQ * 4096 * 768, bytes_accessed=8_000_000, transcendentals=0
        ),
        name="tail_grads",
    )(meta, slices, *z_parts, *y_parts, text, image, *from_hbm(*weights))


def x_before_kernel(kept, got, out):
    out[...] = total((kept[1], got[...])).astype(BF16)


def x_far_kernel(kept, got, out):
    out[...] = total((kept[3], got[...])).astype(BF16)


def x_rest_kernel(kept, got, own, after):
    own[...] = total((kept[0], got[0])).astype(BF16)
    after[...] = total((kept[2], got[1])).astype(BF16)


def split_kernel(*refs):
    for parts, outs in ((refs[:3], refs[6:10]), (refs[3:6], refs[10:14])):
        for i, out in enumerate(outs):
            rows = slice(i * 256, (i + 1) * 256)
            out[...] = total([part[rows] for part in parts]).astype(out.dtype)


def split_phase(z_sum, y_sum):
    own = jax.ShapeDtypeStruct((256, 3 * HD), F32)
    other = jax.ShapeDtypeStruct((256, 3 * HD), BF16)
    outs = small_call(split_kernel, "split", [own, other, other, other] * 2, (), (*z_sum, *y_sum))
    return outs[:4], outs[4:]


def mixed_kernel(meta, own, before, after, text_out, image_out):
    off = meta[2]
    grads = total((own[...], before[...], after[...])).astype(BF16).astype(F32)
    text = grads[:PATCH]
    row = lax.broadcasted_iota(jnp.int32, (PATCH, 1), 0)
    text_out[:PATCH] = jnp.where(row < off, text, 0.0).astype(BF16)
    text_out[PATCH:] = jnp.where(row < off, 0.0, text).astype(BF16)
    for i in range(8):
        rows = slice(PATCH + 32 * i, PATCH + 32 * (i + 1))
        image_out[:, i * SEQ : (i + 1) * SEQ] = grads[rows].astype(BF16)


def mixed_grads(meta, parts):
    shapes = [jax.ShapeDtypeStruct((SEQ, SEQ), BF16), jax.ShapeDtypeStruct((32, 4096), BF16)]
    return small_call(mixed_kernel, "mixed_grads", shapes, (meta,), parts)


def final_kernel(*refs):
    z_sum = total([ref[...] for ref in refs[:4]])
    y_sum = total([ref[...] for ref in refs[4:8]])
    for cols, out, first, second in (
        (QUERY, refs[8], z_sum, y_sum),
        (KEY, refs[9], y_sum, z_sum),
        (VALUE, refs[10], y_sum, z_sum),
    ):
        out[:, :HD] = first[:, cols]
        out[:, HD:] = second[:, cols]


def final_sums(z_parts, y_parts):
    shape = jax.ShapeDtypeStruct((256, 2 * HD), F32)
    return small_call(final_kernel, "final_sums", [shape] * 3, (), (*z_parts, *y_parts))


def local(text_hidden, patch_rows, image_start, w_query, w_key, w_value, d_attn):
    ctx = lax.axis_index("ctx")
    y, z = ctx // RING, ctx % RING
    images, pieces, width = patch_rows.shape
    owners = image_start // SEQ
    off = jnp.sum(jnp.where(owners == ctx, image_start, 0)) - ctx * SEQ
    meta = jnp.stack([y, z, off]).astype(jnp.int32)
    table = lax.dynamic_index_in_dim(jnp.asarray(pair_table()), ctx, 0, keepdims=False)

    tp = lax.axis_index("tp")
    x, core = tp // 2, tp % 2
    columns = (x + jnp.asarray(OFFSETS, jnp.int32)) % RING
    slices = jnp.concatenate([columns * 2 + core, columns * 2 + 1 - core]).astype(jnp.int32)

    index = jnp.arange(SEQ, dtype=jnp.int32)
    rel = (index - PATCH) // 32
    shift = rel % RING
    shift = jnp.where(shift == 0, 0, jnp.where(shift == 1, 3, shift - 1))
    sender = 2 * ((x + shift) % RING) + jnp.where(rel < RING, core, 1 - core)
    text_pos = jnp.where(index < off, index, index + PATCH)
    image_pos = off + 16 * ((index % 32) // 2) + 2 * sender + index % 2
    pos = jnp.where(index < PATCH, text_pos, image_pos)
    placed = (index[:, None] == pos[None, :]).astype(BF16)

    by_shard = place_patches(owners, patch_rows)
    by_shard, text_hidden = lax.optimization_barrier((by_shard, text_hidden))
    arrived = lax.all_to_all(by_shard, "ctx", split_axis=0, concat_axis=0, tiled=True)
    kept = index[:PATCH, None] < off
    text = jnp.where(kept, text_hidden[:PATCH], text_hidden[PATCH:])
    t_ring = ring_gather(text, send_x)
    arrived, t_ring = lax.optimization_barrier((arrived, t_ring))
    t_far = jnp.concatenate(t_ring[3:], axis=0)
    t_own = jnp.concatenate([*t_ring[:3], t_far], axis=1)
    t_oth = send_core(t_own)

    image = arrived.reshape(images * pieces, width)
    before, after = send_x(image, 1), send_x(image, -1)
    cot = dot_tn(placed, d_attn).astype(BF16)
    weights = (w_query, w_key, w_value)
    half = image.shape[0] // 2
    far = (send_x(before[:half], 1), send_x(after[half:], -1))
    text_flipped, z_keep, y_keep, z_text, y_text, held = project_text(
        slices, t_own, t_oth, cot, weights
    )
    far, z_text = lax.optimization_barrier((far, z_text))
    i_own = jnp.concatenate([image, before, after, *far], axis=0)
    i_oth = send_core(i_own)

    image_flipped, z_image, y_image = project_image(i_own, i_oth, cot, held)
    z_keep, y_keep = from_hbm(z_keep, y_keep)

    z_before, z_after = send_z(z_text, 1), send_z(z_text, -1)
    y_before, y_after = send_y(y_text, 1), send_y(y_text, -1)
    z_before, y_before, z_image = lax.optimization_barrier((z_before, y_before, z_image))
    z_image_before, z_image_after = send_z(z_image, 1), send_z(z_image, -1)
    y_image_before, y_image_after = send_y(y_image, 1), send_y(y_image, -1)
    z_ring = (z_keep, z_image, z_before, z_image_before, z_after, z_image_after)
    z_ring += (send_z(z_before, 1), send_z(z_image_after, -1))
    y_ring = (y_keep, y_image, y_before, y_image_before, y_after, y_image_after)
    y_ring += (send_y(y_before, 1), send_y(y_image_after, -1))
    operands = (*z_ring, *y_ring)
    z_stats, y_stats, o_part = attention_stats(meta, table, operands)
    z_stats = [z_stats] + [send_z(z_stats, step) for step in (1, -1, 2)]
    y_stats = [y_stats] + [send_y(y_stats, step) for step in (1, -1, 2)]
    outs = attention_grads(meta, table, operands, o_part, z_stats, y_stats)
    z_parts, y_parts = ring_scatter(outs[:5], send_z), ring_scatter(outs[5:], send_y)
    gz, gy, kept_part, sent_part, sent_before, sent_far, *parts = tail_grads(
        meta, slices, z_parts, y_parts, text_flipped, image_flipped, weights
    )
    x_shape = jax.ShapeDtypeStruct((SEQ, SEQ), BF16)
    got_far, got_before = send_core(sent_far), send_core(sent_before)
    got_part = send_core(sent_part)
    z_own, z_before, z_after, z_far = parts[:4]
    y_own, y_before, y_after, y_far = parts[4:]
    z_far, y_far = send_y(z_far, 1), send_z(y_far, 1)
    (x_far,) = small_call(x_far_kernel, "x_far", [x_shape], (), (kept_part, got_far))
    (x_before,) = small_call(x_before_kernel, "x_before", [x_shape], (), (kept_part, got_before))
    x_far, x_before = send_x(x_far, 1), send_x(x_before, -1)
    x_own, x_after = small_call(x_rest_kernel, "x_rest", [x_shape] * 2, (), (kept_part, got_part))
    x_after, z_before = lax.optimization_barrier((x_after, z_before))
    z_before = send_y(z_before, -1)
    x_after = total((x_after, x_far)).astype(BF16)
    x_after = send_x(x_after, 1)
    z_far, y_far, y_before = lax.optimization_barrier((z_far, y_far, y_before))
    z_sum = (z_own, send_y(total((z_after, z_far)).astype(BF16), 1), z_before)
    y_sum = (y_own, send_z(total((y_after, y_far)).astype(BF16), 1), send_z(y_before, -1))
    d_text, i_grad = mixed_grads(meta, (x_own, x_after, x_before))
    z_sum, y_sum, i_grad = lax.optimization_barrier((z_sum, y_sum, i_grad))

    attended = jnp.concatenate([gz[:, COT], gy[:, COT]], axis=1)
    attn_out = dot_nn(placed, attended).astype(BF16)

    returned = lax.all_to_all(
        i_grad.reshape(images, pieces, width), "ctx", split_axis=0, concat_axis=0, tiled=True
    )
    d_patch = move_patches(take_kernel, "take_patches", owners, returned)
    z_pieces, y_pieces = split_phase(z_sum, y_sum)
    z_got, y_got = direct_scatter(z_pieces, send_z), direct_scatter(y_pieces, send_y)
    dw_query, dw_key, dw_value = final_sums(z_got, y_got)
    return (
        attn_out,
        d_text,
        d_patch,
        dw_query,
        dw_key,
        dw_value,
    )


def solution(mesh):
    in_specs = (
        P("ctx", "tp"),
        P(None, ("ctx", "tp"), None),
        P(),
        P(None, "tp"),
        P(None, "tp"),
        P(None, "tp"),
        P("ctx", "tp"),
    )
    out_specs = (
        P("ctx", "tp"),
        P("ctx", "tp"),
        P(None, ("ctx", "tp"), None),
        P("ctx", "tp"),
        P("ctx", "tp"),
        P("ctx", "tp"),
    )
    return jax.shard_map(local, mesh=mesh, in_specs=in_specs, out_specs=out_specs, check_vma=False)
```

```python
import functools
import math

import jax
import jax.numpy as jnp
import numpy as np
from jax import lax
from jax.experimental import pallas as pl
from jax.experimental.pallas import tpu as pltpu
from jax.sharding import PartitionSpec as P

HD = 128
PATCH = 256
SEQ = 512
RING = 4
OFFSETS = (0, 3, 1, 2)
NEG_LARGE = -1e30
SCALE = 1.0 / math.sqrt(HD)
LOG2E = math.log2(math.e)
SMALL_LIMIT = 8 * 1024 * 1024
STREAM_LIMIT = 15 * 1024 * 1024
STATS_LIMIT = 16 * 1024 * 1024
GRADS_LIMIT = 22 * 1024 * 1024
Z_GROUPS = [[RING * y + z for z in range(RING)] for y in range(RING)]
Y_GROUPS = [[RING * y + z for y in range(RING)] for z in range(RING)]
BF16 = jnp.bfloat16
F32 = jnp.float32


def pair_table():
    rows = []
    for ctx in range(RING * RING):
        y, z = divmod(ctx, RING)
        own = []
        for q in range(RING):
            for k in range(RING):
                if RING * k + z < RING * y + q:
                    own.append(8 * q + RING + k)
                if RING * y + k < RING * q + z:
                    own.append(8 * (RING + q) + k)
        assert len(own) == 15
        rows.append(own)
    return np.asarray(rows, np.int32)


def ctx_send(value, dy, dz):
    perm = [
        (RING * y + z, RING * ((y + dy) % RING) + (z + dz) % RING)
        for y in range(RING)
        for z in range(RING)
    ]
    return lax.ppermute(value, "ctx", perm)


def send_z(value, step):
    return ctx_send(value, 0, step)


def send_y(value, step):
    return ctx_send(value, step, 0)


def send_x(value, step):
    perm = [(2 * x + core, 2 * ((x + step) % RING) + core) for x in range(RING) for core in range(2)]
    return lax.ppermute(value, "tp", perm)


def send_core(value):
    return lax.ppermute(value, "tp", [(i, i ^ 1) for i in range(2 * RING)])


def ring_gather(value, send):
    half = value.shape[0] // 2
    before = send(value, 1)
    after = send(value, -1)
    far_low = send(before[:half], 1)
    far_high = send(after[half:], -1)
    return value, before, after, far_low, far_high


def add_to(piece, part, at):
    total = (lax.slice_in_dim(piece, at, at + part.shape[0]).astype(F32) + part.astype(F32)).astype(BF16)
    return lax.dynamic_update_slice_in_dim(piece, total, at, 0)


def scatter_far(pieces, send):
    own, before, after, far_low, far_high = pieces
    after = add_to(after, send(far_low, 1), 0)
    before = add_to(before, send(far_high, -1), far_low.shape[0])
    return own, before, after


def scatter_near(pieces, send):
    own, before, after = pieces
    return own, send(after, 1), send(before, -1)


def ring_scatter(pieces, send):
    return scatter_near(scatter_far(pieces, send), send)


def direct_scatter(pieces, send):
    own, before, after, far = pieces
    return own, send(before, -1), send(after, 1), send(far, 2)


def total(parts):
    return sum(part.astype(F32) for part in parts)


def dot_nn(a, b):
    return jnp.dot(a, b, preferred_element_type=F32)


def dot_nt(a, b):
    return lax.dot_general(a, b, (((1,), (1,)), ((), ())), preferred_element_type=F32)


def dot_tn(a, b):
    return lax.dot_general(a, b, (((0,), (0,)), ((), ())), preferred_element_type=F32)


def small_call(body, name, out_shape, scalars, operands, flops=2_000_000):
    return pl.pallas_call(
        body,
        out_shape=out_shape,
        in_specs=smem(len(scalars)) + whole(len(operands)),
        out_specs=whole(len(out_shape)),
        compiler_params=pltpu.CompilerParams(vmem_limit_bytes=SMALL_LIMIT),
        cost_estimate=pl.CostEstimate(flops=flops, bytes_accessed=2_000_000, transcendentals=0),
        name=name,
    )(*scalars, *operands)


def place_kernel(owners, patches, out, sems):
    copies = [
        pltpu.make_async_copy(patches.at[k], out.at[owners[k]], sems.at[k])
        for k in range(16)
    ]
    for copy in copies:
        copy.start()
    for copy in copies:
        copy.wait()


def place_patches(owners, patches):
    return pl.pallas_call(
        place_kernel,
        out_shape=jax.ShapeDtypeStruct(patches.shape, BF16),
        in_specs=smem(1) + in_hbm(1),
        out_specs=whole(1)[0],
        scratch_shapes=[pltpu.SemaphoreType.DMA((16,))],
        compiler_params=pltpu.CompilerParams(vmem_limit_bytes=SMALL_LIMIT),
        cost_estimate=pl.CostEstimate(flops=0, bytes_accessed=500_000, transcendentals=0),
        name="place_patches",
    )(owners, *from_hbm(patches))


def take_kernel(owners, returned, out):
    for k in range(16):
        out[k] = returned[owners[k]]


def move_patches(body, name, owners, patches):
    shape = [jax.ShapeDtypeStruct(patches.shape, BF16)]
    return small_call(body, name, shape, (owners,), (patches,))[0]


QUERY, KEY, VALUE, COT = (slice(i * HD, (i + 1) * HD) for i in range(4))
CHUNK = 1024
CHUNKS = 4096 // CHUNK


def pack(acc, cot, z_out, y_out):
    for head, cols, out in ((0, (0, 3, 5), z_out), (1, (1, 2, 4), y_out)):
        for at, col in enumerate(cols):
            out[:, at * HD : (at + 1) * HD] = acc[:, col * HD : (col + 1) * HD].astype(BF16)
        out[:, COT] = cot[:, head * HD : (head + 1) * HD]


def block_rows(slices, j):
    return pl.ds(pl.multiple_of(slices[j] * SEQ, SEQ), SEQ)


def stream(weights, held, sems, depths):
    groups = []
    for j, depth in enumerate(depths):
        groups.append(
            [
                pltpu.make_async_copy(
                    ref.at[depth], held.at[depth, i * 256 : (i + 1) * 256], sems.at[j, i]
                )
                for i, ref in enumerate(weights)
            ]
        )
    for group in groups:
        for copy in group:
            copy.start()
    return groups


def text_kernel(slices, own, oth, cot, wq, wk, wv, flipped, z_keep, y_keep, z_out, y_out, held, turned, sems):
    depths = [block_rows(slices, j) for j in range(8)]
    groups = stream((wq, wk, wv), held, sems, depths)
    acc = None
    outgoing = []
    for j, (depth, group) in enumerate(zip(depths, groups)):
        part = own if j < RING else oth
        block = part[:, (j % RING) * SEQ : (j % RING + 1) * SEQ]
        turned[depth, :] = block.T
        outgoing.append(pltpu.make_async_copy(turned.at[depth], flipped.at[depth], sems.at[j, 3]))
        outgoing[-1].start()
        for copy in group:
            copy.wait()
        term = dot_nn(block, held[depth, :])
        acc = term if acc is None else acc + term
    pack(acc, cot[:PATCH], z_out, y_out)
    for i, (out, keep) in enumerate(((z_out, z_keep), (y_out, y_keep))):
        outgoing.append(pltpu.make_async_copy(out, keep, sems.at[8, i]))
        outgoing[-1].start()
    for copy in outgoing:
        copy.wait()


def image_kernel(own, oth, cot, held, flipped, z_out, y_out, turned, sems):
    acc = None
    outgoing = []
    for j in range(CHUNKS):
        depth = slice(j * CHUNK, (j + 1) * CHUNK)
        block = jnp.concatenate([own[:, depth], oth[:, depth]], axis=0)
        turned[depth, :] = block.T
        outgoing.append(pltpu.make_async_copy(turned.at[depth], flipped.at[depth], sems.at[j]))
        outgoing[-1].start()
        term = dot_nn(block, held[depth, :])
        acc = term if acc is None else acc + term
    pack(acc, cot[PATCH:], z_out, y_out)
    for copy in outgoing:
        copy.wait()


def from_hbm(*arrays):
    return [pltpu.with_memory_space_constraint(array, pltpu.HBM) for array in arrays]


def project_text(slices, own, oth, cot, weights):
    rows = (PATCH, 4 * HD)
    return pl.pallas_call(
        text_kernel,
        out_shape=[pltpu.HBM((4096, PATCH), BF16)]
        + [pltpu.HBM(rows, BF16)] * 2
        + [jax.ShapeDtypeStruct(rows, BF16)] * 2
        + [jax.ShapeDtypeStruct((4096, 6 * HD), BF16)],
        in_specs=smem(1) + whole(3) + in_hbm(3),
        out_specs=in_hbm(3) + whole(3),
        scratch_shapes=[pltpu.VMEM((4096, PATCH), BF16), pltpu.SemaphoreType.DMA((9, 4))],
        compiler_params=pltpu.CompilerParams(vmem_limit_bytes=SMALL_LIMIT),
        cost_estimate=pl.CostEstimate(
            flops=2 * PATCH * 4096 * 768, bytes_accessed=8_000_000, transcendentals=0
        ),
        name="qkv_text",
    )(slices, own, oth, cot, *from_hbm(*weights))


def project_image(own, oth, cot, held):
    rows = (PATCH, 4 * HD)
    return pl.pallas_call(
        image_kernel,
        out_shape=[pltpu.HBM((4096, PATCH), BF16)] + [jax.ShapeDtypeStruct(rows, BF16)] * 2,
        in_specs=whole(4),
        out_specs=in_hbm(1) + whole(2),
        scratch_shapes=[pltpu.VMEM((4096, PATCH), BF16), pltpu.SemaphoreType.DMA((CHUNKS,))],
        compiler_params=pltpu.CompilerParams(vmem_limit_bytes=SMALL_LIMIT),
        cost_estimate=pl.CostEstimate(
            flops=2 * PATCH * 4096 * 768, bytes_accessed=2_000_000, transcendentals=0
        ),
        name="qkv_image",
    )(own, oth, cot, held)


def ranks(off, shape, dim):
    index = lax.broadcasted_iota(jnp.int32, shape, dim)
    return jnp.where(index < PATCH, 2 * index, 2 * off - 1)


def diagonal_mask(off):
    return ranks(off, (SEQ, 1), 0) <= ranks(off, (1, SEQ), 1)


def fetch(refs, blocks, sems, y, z):
    copies = []
    for base, at, parts in ((0, z, refs[0:8]), (RING, y, refs[8:16])):
        for rel, off in enumerate(OFFSETS):
            slot = base + lax.rem(at + off, RING)
            for half in range(2):
                target = blocks.at[slot, half * PATCH : (half + 1) * PATCH]
                part = parts[2 * rel + half]
                copies.append(pltpu.make_async_copy(part, target, sems.at[len(copies)]))
    first = copies[0:2] + copies[8:10]
    rest = copies[2:8] + copies[10:]
    for copy in first + rest:
        copy.start()
    return first, rest


def own_pairs(meta, advance):
    y, z, off = meta[0], meta[1], meta[2]
    advance([(z, RING + y), (RING + y, z)], diagonal_mask(off))


def other_pairs(table, advance):
    def step(i, carry):
        codes = [table[3 * i + j] for j in range(3)]
        advance([(lax.div(code, 8), lax.rem(code, 8)) for code in codes], None)
        return carry

    lax.fori_loop(0, 5, step, 0)


def flip_all(dest, blocks, cols):
    for i in range(2 * RING):
        dest[i] = blocks[i, :, cols].T


def flip_own(dest, blocks, cols, y, z):
    dest[z] = blocks[z, :, cols].T
    dest[RING + y] = blocks[RING + y, :, cols].T


def stats_kernel(meta, table, *refs):
    z_out, y_out, o_out, blocks, vt, top, total, sems = refs[16:]
    y, z = meta[0], meta[1]
    first, rest = fetch(refs, blocks, sems, y, z)
    top[...] = jnp.full_like(top, NEG_LARGE)
    total[...] = jnp.zeros_like(total)
    o_out[...] = jnp.zeros_like(o_out)

    def advance(pairs, allowed):
        scores = [dot_nt(blocks[k, :, KEY], blocks[q, :, QUERY]) * (SCALE * LOG2E) for q, k in pairs]
        if allowed is not None:
            scores = [jnp.where(allowed, score, NEG_LARGE) for score in scores]
        highs = [jnp.max(score, axis=0, keepdims=True) for score in scores]
        for (q, k), score, high in zip(pairs, scores, highs):
            old = top[q]
            new = jnp.maximum(old, high)
            probs = jnp.exp2(score - new)
            shrink = jnp.exp2(old - new)
            top[q] = new
            total[q] = total[q] * shrink + jnp.sum(probs, axis=0, keepdims=True)
            o_out[q] = o_out[q] * shrink + dot_nn(vt[k], probs.astype(BF16))

    for copy in first:
        copy.wait()
    flip_own(vt, blocks, VALUE, y, z)
    own_pairs(meta, advance)
    for copy in rest:
        copy.wait()
    flip_all(vt, blocks, VALUE)
    other_pairs(table, advance)
    for head, out in ((0, z_out), (1, y_out)):
        for i in range(RING):
            at = head * RING + i
            count = total[at]
            some = count > 0.0
            safe = jnp.where(some, count, 1.0)
            partial = o_out[at] / safe
            o_out[at] = partial
            flipped = blocks[at, :, COT].astype(F32).T
            out[i : i + 1, :] = jnp.where(some, top[at] + jnp.log(safe) * LOG2E, NEG_LARGE)
            out[RING + i : RING + i + 1, :] = jnp.sum(partial * flipped, axis=0, keepdims=True)


def whole(count):
    return [pl.BlockSpec(memory_space=pltpu.VMEM)] * count


def in_hbm(count):
    return [pl.BlockSpec(memory_space=pltpu.HBM)] * count


def smem(count):
    return [pl.BlockSpec(memory_space=pltpu.SMEM)] * count


def attention_stats(meta, table, pieces):
    row = pltpu.VMEM((2 * RING, 1, SEQ), F32)
    return pl.pallas_call(
        stats_kernel,
        out_shape=[jax.ShapeDtypeStruct((2 * RING, SEQ), F32)] * 2
        + [jax.ShapeDtypeStruct((2 * RING, HD, SEQ), F32)],
        in_specs=smem(2) + in_hbm(16),
        out_specs=whole(3),
        scratch_shapes=[
            pltpu.VMEM((2 * RING, SEQ, 4 * HD), BF16),
            pltpu.VMEM((2 * RING, HD, SEQ), BF16),
            row,
            row,
            pltpu.SemaphoreType.DMA((16,)),
        ],
        compiler_params=pltpu.CompilerParams(vmem_limit_bytes=STATS_LIMIT),
        cost_estimate=pl.CostEstimate(
            flops=17 * 2 * 2 * SEQ * SEQ * HD,
            bytes_accessed=5_000_000,
            transcendentals=17 * SEQ * SEQ,
        ),
        name="stats",
    )(meta, table, *pieces)


def grads_kernel(meta, table, *refs):
    o_part = refs[16]
    stats = (refs[17:21], refs[21:25])
    outs = refs[25:35]
    blocks, kt, lse, dots, keep, dq_sum, dk_sum, dv_sum, sems = refs[35:]
    y, z = meta[0], meta[1]
    first, rest = fetch(refs, blocks, sems, y, z)
    dq_sum[...] = jnp.zeros_like(dq_sum)
    dk_sum[...] = jnp.zeros_like(dk_sum)
    dv_sum[...] = jnp.zeros_like(dv_sum)
    for head in range(2):
        parts = [ref[...] for ref in stats[head]]
        logs = [part[:RING] for part in parts]
        top = functools.reduce(jnp.maximum, logs)
        shares = [jnp.exp2(log - top) for log in logs]
        norm = sum(shares)
        full = top + jnp.log(norm) * LOG2E
        dot = sum(share * part[RING:] for share, part in zip(shares, parts)) / norm
        weight = jnp.exp2(logs[0] - full)
        for i in range(RING):
            lse[head * RING + i] = full[i : i + 1]
            dots[head * RING + i] = dot[i : i + 1]
            keep[head * RING + i] = weight[i : i + 1]

    def advance(pairs, allowed):
        for q, k in pairs:
            query, cot = blocks[q, :, QUERY], blocks[q, :, COT]
            probs = jnp.exp2(dot_nt(blocks[k, :, KEY], query) * (SCALE * LOG2E) - lse[q])
            if allowed is not None:
                probs = jnp.where(allowed, probs, 0.0)
            prob_grads = dot_nt(blocks[k, :, VALUE], cot)
            slope = (probs * (prob_grads - dots[q]) * SCALE).astype(BF16)
            dv_sum[k] += dot_nn(probs.astype(BF16), cot)
            dk_sum[k] += dot_nn(slope, query)
            dq_sum[q] += dot_nn(kt[k], slope)

    for copy in first:
        copy.wait()
    flip_own(kt, blocks, KEY, y, z)
    own_pairs(meta, advance)
    for copy in rest:
        copy.wait()
    flip_all(kt, blocks, KEY)
    other_pairs(table, advance)
    half = SEQ // 2
    for base, at, parts in ((0, z, outs[:5]), (RING, y, outs[5:])):
        for rel, shift in enumerate(OFFSETS):
            slot = base + lax.rem(at + shift, RING)
            terms = (
                dq_sum[slot].T.astype(BF16),
                dk_sum[slot].astype(BF16),
                dv_sum[slot].astype(BF16),
                (o_part[slot] * keep[slot]).T.astype(BF16),
            )
            for cols, term in zip((QUERY, KEY, VALUE, COT), terms):
                if rel < 3:
                    parts[rel][:, cols] = term
                else:
                    parts[3][:, cols] = term[:half]
                    parts[4][:, cols] = term[half:]


def attention_grads(meta, table, pieces, o_part, z_stats, y_stats):
    row = pltpu.VMEM((2 * RING, 1, SEQ), F32)
    tall = pltpu.VMEM((2 * RING, SEQ, HD), F32)
    flat = pltpu.VMEM((2 * RING, HD, SEQ), F32)
    full = jax.ShapeDtypeStruct((SEQ, 4 * HD), BF16)
    half = jax.ShapeDtypeStruct((SEQ // 2, 4 * HD), BF16)
    return pl.pallas_call(
        grads_kernel,
        out_shape=([full] * 3 + [half] * 2) * 2,
        in_specs=smem(2) + in_hbm(16) + whole(9),
        out_specs=whole(10),
        scratch_shapes=[
            pltpu.VMEM((2 * RING, SEQ, 4 * HD), BF16),
            pltpu.VMEM((2 * RING, HD, SEQ), BF16),
            row,
            row,
            row,
            flat,
            tall,
            tall,
            pltpu.SemaphoreType.DMA((16,)),
        ],
        compiler_params=pltpu.CompilerParams(vmem_limit_bytes=GRADS_LIMIT),
        cost_estimate=pl.CostEstimate(
            flops=17 * 5 * 2 * SEQ * SEQ * HD,
            bytes_accessed=10_000_000,
            transcendentals=17 * SEQ * SEQ,
        ),
        name="grads",
    )(meta, table, *pieces, o_part, *z_stats, *y_stats)


def tail_kernel(meta, slices, *refs):
    text, image = refs[6:8]
    weights = refs[8:11]
    gz, gy, own, oth, oth_before, oth_far = refs[11:17]
    z_parts, y_parts = refs[17:21], refs[21:25]
    held, products, sems = refs[25:]
    y, z = meta[0], meta[1]
    depths = [block_rows(slices, j) for j in range(8)]
    groups = stream(weights, held, sems, depths)
    for parts, grads in ((refs[:3], gz), (refs[3:6], gy)):
        grads[...] = total([part[...] for part in parts]).astype(BF16)
    width = 3 * HD
    rows = 256
    grads = jnp.concatenate([gz[:, :width], gy[:, :width]], axis=1)
    for rel, shift in enumerate(OFFSETS):
        depth = pl.ds(pl.multiple_of(lax.rem(y + shift, RING) * CHUNK, CHUNK), CHUNK)
        term = dot_nn(text[depth, :], grads[:PATCH]) + dot_nn(image[depth, :], grads[PATCH:])
        products[...] = term.astype(BF16)
        for other, other_shift in enumerate(OFFSETS):
            source = pl.ds(pl.multiple_of(lax.rem(z + other_shift, RING) * rows, rows), rows)
            z_parts[rel][other * rows : (other + 1) * rows, :] = products[source, :width]
            y_parts[other][rel * rows : (rel + 1) * rows, :] = products[source, width:]

    columns = [ref[:, cols] for cols in (QUERY, KEY, VALUE) for ref in (gz, gy)]
    columns = [columns[i] for i in (0, 1, 3, 2, 5, 4)]
    grads = jnp.concatenate(columns, axis=1)
    pieces = [own.at[i] for i in range(RING)]
    pieces += [oth.at[0], oth_before, oth.at[1], oth_far]
    for j, (depth, group) in enumerate(zip(depths, groups)):
        for copy in group:
            copy.wait()
        term = dot_nt(grads, held[depth, :]).astype(BF16)
        pieces[j][:PATCH] = term[:PATCH]
        at = pl.ds(pl.multiple_of(PATCH + slices[j] * 32, 32), 32)
        for i, piece in enumerate(pieces):
            piece[at, :] = term[PATCH + 32 * i : PATCH + 32 * (i + 1)]


def tail_grads(meta, slices, z_parts, y_parts, text, image, weights):
    piece = jax.ShapeDtypeStruct((CHUNK, 3 * HD), BF16)
    return pl.pallas_call(
        tail_kernel,
        out_shape=[jax.ShapeDtypeStruct((SEQ, 4 * HD), BF16)] * 2
        + [jax.ShapeDtypeStruct((RING, SEQ, SEQ), BF16)]
        + [jax.ShapeDtypeStruct((2, SEQ, SEQ), BF16)]
        + [jax.ShapeDtypeStruct((SEQ, SEQ), BF16)] * 2
        + [piece] * 8,
        in_specs=smem(2) + whole(8) + in_hbm(3),
        out_specs=whole(14),
        scratch_shapes=[
            pltpu.VMEM((4096, 6 * HD), BF16),
            pltpu.VMEM((CHUNK, 6 * HD), BF16),
            pltpu.SemaphoreType.DMA((8, 3)),
        ],
        compiler_params=pltpu.CompilerParams(vmem_limit_bytes=STREAM_LIMIT),
        cost_estimate=pl.CostEstimate(
            flops=4 * SEQ * 4096 * 768, bytes_accessed=8_000_000, transcendentals=0
        ),
        name="tail_grads",
    )(meta, slices, *z_parts, *y_parts, text, image, *from_hbm(*weights))


def x_before_kernel(kept, got, out):
    out[...] = total((kept[1], got[...])).astype(BF16)


def x_far_kernel(kept, got, out):
    out[...] = total((kept[3], got[...])).astype(BF16)


def x_rest_kernel(kept, got, own, after):
    own[...] = total((kept[0], got[0])).astype(BF16)
    after[...] = total((kept[2], got[1])).astype(BF16)


def split_kernel(*refs):
    for parts, outs in ((refs[:3], refs[6:10]), (refs[3:6], refs[10:14])):
        for i, out in enumerate(outs):
            rows = slice(i * 256, (i + 1) * 256)
            out[...] = total([part[rows] for part in parts]).astype(out.dtype)


def split_phase(z_sum, y_sum):
    own = jax.ShapeDtypeStruct((256, 3 * HD), F32)
    other = jax.ShapeDtypeStruct((256, 3 * HD), BF16)
    outs = small_call(split_kernel, "split", [own, other, other, other] * 2, (), (*z_sum, *y_sum))
    return outs[:4], outs[4:]


def mixed_kernel(meta, own, before, after, text_out, image_out):
    off = meta[2]
    grads = total((own[...], before[...], after[...])).astype(BF16).astype(F32)
    text = grads[:PATCH]
    row = lax.broadcasted_iota(jnp.int32, (PATCH, 1), 0)
    text_out[:PATCH] = jnp.where(row < off, text, 0.0).astype(BF16)
    text_out[PATCH:] = jnp.where(row < off, 0.0, text).astype(BF16)
    for i in range(8):
        rows = slice(PATCH + 32 * i, PATCH + 32 * (i + 1))
        image_out[:, i * SEQ : (i + 1) * SEQ] = grads[rows].astype(BF16)


def mixed_grads(meta, parts):
    shapes = [jax.ShapeDtypeStruct((SEQ, SEQ), BF16), jax.ShapeDtypeStruct((32, 4096), BF16)]
    return small_call(mixed_kernel, "mixed_grads", shapes, (meta,), parts)


def final_kernel(*refs):
    z_sum = total([ref[...] for ref in refs[:4]])
    y_sum = total([ref[...] for ref in refs[4:8]])
    for cols, out, first, second in (
        (QUERY, refs[8], z_sum, y_sum),
        (KEY, refs[9], y_sum, z_sum),
        (VALUE, refs[10], y_sum, z_sum),
    ):
        out[:, :HD] = first[:, cols]
        out[:, HD:] = second[:, cols]


def final_sums(z_parts, y_parts):
    shape = jax.ShapeDtypeStruct((256, 2 * HD), F32)
    return small_call(final_kernel, "final_sums", [shape] * 3, (), (*z_parts, *y_parts))


def local(text_hidden, patch_rows, image_start, w_query, w_key, w_value, d_attn):
    ctx = lax.axis_index("ctx")
    y, z = ctx // RING, ctx % RING
    images, pieces, width = patch_rows.shape
    owners = image_start // SEQ
    off = jnp.sum(jnp.where(owners == ctx, image_start, 0)) - ctx * SEQ
    meta = jnp.stack([y, z, off]).astype(jnp.int32)
    table = lax.dynamic_index_in_dim(jnp.asarray(pair_table()), ctx, 0, keepdims=False)

    tp = lax.axis_index("tp")
    x, core = tp // 2, tp % 2
    columns = (x + jnp.asarray(OFFSETS, jnp.int32)) % RING
    slices = jnp.concatenate([columns * 2 + core, columns * 2 + 1 - core]).astype(jnp.int32)

    index = jnp.arange(SEQ, dtype=jnp.int32)
    rel = (index - PATCH) // 32
    shift = rel % RING
    shift = jnp.where(shift == 0, 0, jnp.where(shift == 1, 3, shift - 1))
    sender = 2 * ((x + shift) % RING) + jnp.where(rel < RING, core, 1 - core)
    text_pos = jnp.where(index < off, index, index + PATCH)
    image_pos = off + 16 * ((index % 32) // 2) + 2 * sender + index % 2
    pos = jnp.where(index < PATCH, text_pos, image_pos)
    placed = (index[:, None] == pos[None, :]).astype(BF16)

    by_shard = place_patches(owners, patch_rows)
    by_shard, text_hidden = lax.optimization_barrier((by_shard, text_hidden))
    arrived = lax.all_to_all(by_shard, "ctx", split_axis=0, concat_axis=0, tiled=True)
    kept = index[:PATCH, None] < off
    text = jnp.where(kept, text_hidden[:PATCH], text_hidden[PATCH:])
    t_ring = ring_gather(text, send_x)
    arrived, t_ring = lax.optimization_barrier((arrived, t_ring))
    t_far = jnp.concatenate(t_ring[3:], axis=0)
    t_own = jnp.concatenate([*t_ring[:3], t_far], axis=1)
    t_oth = send_core(t_own)

    image = arrived.reshape(images * pieces, width)
    before, after = send_x(image, 1), send_x(image, -1)
    cot = dot_tn(placed, d_attn).astype(BF16)
    weights = (w_query, w_key, w_value)
    half = image.shape[0] // 2
    far = (send_x(before[:half], 1), send_x(after[half:], -1))
    text_flipped, z_keep, y_keep, z_text, y_text, held = project_text(
        slices, t_own, t_oth, cot, weights
    )
    far, z_text = lax.optimization_barrier((far, z_text))
    i_own = jnp.concatenate([image, before, after, *far], axis=0)
    i_oth = send_core(i_own)

    image_flipped, z_image, y_image = project_image(i_own, i_oth, cot, held)
    z_keep, y_keep = from_hbm(z_keep, y_keep)

    z_before, z_after = send_z(z_text, 1), send_z(z_text, -1)
    y_before, y_after = send_y(y_text, 1), send_y(y_text, -1)
    z_before, y_before, _ = lax.optimization_barrier((z_before, y_before, z_image))
    z_image_before, z_image_after = send_z(z_image, 1), send_z(z_image, -1)
    y_image_before, y_image_after = send_y(y_image, 1), send_y(y_image, -1)
    z_ring = (z_keep, z_image, z_before, z_image_before, z_after, z_image_after)
    z_ring += (send_z(z_before, 1), send_z(z_image_after, -1))
    y_ring = (y_keep, y_image, y_before, y_image_before, y_after, y_image_after)
    y_ring += (send_y(y_before, 1), send_y(y_image_after, -1))
    operands = (*z_ring, *y_ring)
    z_stats, y_stats, o_part = attention_stats(meta, table, operands)
    z_stats = [z_stats] + [send_z(z_stats, step) for step in (1, -1, 2)]
    y_stats = [y_stats] + [send_y(y_stats, step) for step in (1, -1, 2)]
    outs = attention_grads(meta, table, operands, o_part, z_stats, y_stats)
    z_parts, y_parts = ring_scatter(outs[:5], send_z), ring_scatter(outs[5:], send_y)
    gz, gy, kept_part, sent_part, sent_before, sent_far, *parts = tail_grads(
        meta, slices, z_parts, y_parts, text_flipped, image_flipped, weights
    )
    x_shape = jax.ShapeDtypeStruct((SEQ, SEQ), BF16)
    got_far, got_before = send_core(sent_far), send_core(sent_before)
    got_part = send_core(sent_part)
    z_own, z_before, z_after, z_far = parts[:4]
    y_own, y_before, y_after, y_far = parts[4:]
    z_far, y_far = send_y(z_far, 1), send_z(y_far, 1)
    (x_far,) = small_call(x_far_kernel, "x_far", [x_shape], (), (kept_part, got_far))
    (x_before,) = small_call(x_before_kernel, "x_before", [x_shape], (), (kept_part, got_before))
    x_far, x_before = send_x(x_far, 1), send_x(x_before, -1)
    x_own, x_after = small_call(x_rest_kernel, "x_rest", [x_shape] * 2, (), (kept_part, got_part))
    x_after, z_before = lax.optimization_barrier((x_after, z_before))
    z_before = send_y(z_before, -1)
    x_after = total((x_after, x_far)).astype(BF16)
    x_after = send_x(x_after, 1)
    z_far, y_far, y_before = lax.optimization_barrier((z_far, y_far, y_before))
    z_sum = (z_own, send_y(total((z_after, z_far)).astype(BF16), 1), z_before)
    y_sum = (y_own, send_z(total((y_after, y_far)).astype(BF16), 1), send_z(y_before, -1))
    d_text, i_grad = mixed_grads(meta, (x_own, x_after, x_before))
    z_sum, y_sum, i_grad = lax.optimization_barrier((z_sum, y_sum, i_grad))

    attended = jnp.concatenate([gz[:, COT], gy[:, COT]], axis=1)
    attn_out = dot_nn(placed, attended).astype(BF16)

    returned = lax.all_to_all(
        i_grad.reshape(images, pieces, width), "ctx", split_axis=0, concat_axis=0, tiled=True
    )
    d_patch = move_patches(take_kernel, "take_patches", owners, returned)
    z_pieces, y_pieces = split_phase(z_sum, y_sum)
    z_got, y_got = direct_scatter(z_pieces, send_z), direct_scatter(y_pieces, send_y)
    dw_query, dw_key, dw_value = final_sums(z_got, y_got)
    return (
        attn_out,
        d_text,
        d_patch,
        dw_query,
        dw_key,
        dw_value,
    )


def solution(mesh):
    in_specs = (
        P("ctx", "tp"),
        P(None, ("ctx", "tp"), None),
        P(),
        P(None, "tp"),
        P(None, "tp"),
        P(None, "tp"),
        P("ctx", "tp"),
    )
    out_specs = (
        P("ctx", "tp"),
        P("ctx", "tp"),
        P(None, ("ctx", "tp"), None),
        P("ctx", "tp"),
        P("ctx", "tp"),
        P("ctx", "tp"),
    )
    return jax.shard_map(local, mesh=mesh, in_specs=in_specs, out_specs=out_specs, check_vma=False)
```

```python
import functools
import math

import jax
import jax.numpy as jnp
import numpy as np
from jax import lax
from jax.experimental import pallas as pl
from jax.experimental.pallas import tpu as pltpu
from jax.sharding import PartitionSpec as P

HD = 128
PATCH = 256
SEQ = 512
RING = 4
OFFSETS = (0, 3, 1, 2)
NEG_LARGE = -1e30
SCALE = 1.0 / math.sqrt(HD)
LOG2E = math.log2(math.e)
SMALL_LIMIT = 8 * 1024 * 1024
STREAM_LIMIT = 15 * 1024 * 1024
STATS_LIMIT = 16 * 1024 * 1024
GRADS_LIMIT = 24 * 1024 * 1024
Z_GROUPS = [[RING * y + z for z in range(RING)] for y in range(RING)]
Y_GROUPS = [[RING * y + z for y in range(RING)] for z in range(RING)]
BF16 = jnp.bfloat16
F32 = jnp.float32


def pair_table():
    rows = []
    for ctx in range(RING * RING):
        y, z = divmod(ctx, RING)
        own = []
        for q in range(RING):
            for k in range(RING):
                if RING * k + z < RING * y + q:
                    own.append(8 * q + RING + k)
                if RING * y + k < RING * q + z:
                    own.append(8 * (RING + q) + k)
        assert len(own) == 15
        rows.append(own)
    return np.asarray(rows, np.int32)


def ctx_send(value, dy, dz):
    perm = [
        (RING * y + z, RING * ((y + dy) % RING) + (z + dz) % RING)
        for y in range(RING)
        for z in range(RING)
    ]
    return lax.ppermute(value, "ctx", perm)


def send_z(value, step):
    return ctx_send(value, 0, step)


def send_y(value, step):
    return ctx_send(value, step, 0)


def send_x(value, step):
    perm = [(2 * x + core, 2 * ((x + step) % RING) + core) for x in range(RING) for core in range(2)]
    return lax.ppermute(value, "tp", perm)


def send_core(value):
    return lax.ppermute(value, "tp", [(i, i ^ 1) for i in range(2 * RING)])


def ring_gather(value, send):
    half = value.shape[0] // 2
    before = send(value, 1)
    after = send(value, -1)
    far_low = send(before[:half], 1)
    far_high = send(after[half:], -1)
    return value, before, after, far_low, far_high


def add_to(piece, part, at):
    total = (lax.slice_in_dim(piece, at, at + part.shape[0]).astype(F32) + part.astype(F32)).astype(BF16)
    return lax.dynamic_update_slice_in_dim(piece, total, at, 0)


def scatter_far(pieces, send):
    own, before, after, far_low, far_high = pieces
    after = add_to(after, send(far_low, 1), 0)
    before = add_to(before, send(far_high, -1), far_low.shape[0])
    return own, before, after


def scatter_near(pieces, send):
    own, before, after = pieces
    return own, send(after, 1), send(before, -1)


def ring_scatter(pieces, send):
    return scatter_near(scatter_far(pieces, send), send)


def direct_scatter(pieces, send):
    own, before, after, far = pieces
    return own, send(before, -1), send(after, 1), send(far, 2)


def total(parts):
    return sum(part.astype(F32) for part in parts)


def dot_nn(a, b):
    return jnp.dot(a, b, preferred_element_type=F32)


def dot_nt(a, b):
    return lax.dot_general(a, b, (((1,), (1,)), ((), ())), preferred_element_type=F32)


def dot_tn(a, b):
    return lax.dot_general(a, b, (((0,), (0,)), ((), ())), preferred_element_type=F32)


def small_call(body, name, out_shape, scalars, operands, flops=2_000_000):
    return pl.pallas_call(
        body,
        out_shape=out_shape,
        in_specs=smem(len(scalars)) + whole(len(operands)),
        out_specs=whole(len(out_shape)),
        compiler_params=pltpu.CompilerParams(vmem_limit_bytes=SMALL_LIMIT),
        cost_estimate=pl.CostEstimate(flops=flops, bytes_accessed=2_000_000, transcendentals=0),
        name=name,
    )(*scalars, *operands)


def place_kernel(owners, patches, out, sems):
    copies = [
        pltpu.make_async_copy(patches.at[k], out.at[owners[k]], sems.at[k])
        for k in range(16)
    ]
    for copy in copies:
        copy.start()
    for copy in copies:
        copy.wait()


def place_patches(owners, patches):
    return pl.pallas_call(
        place_kernel,
        out_shape=jax.ShapeDtypeStruct(patches.shape, BF16),
        in_specs=smem(1) + in_hbm(1),
        out_specs=whole(1)[0],
        scratch_shapes=[pltpu.SemaphoreType.DMA((16,))],
        compiler_params=pltpu.CompilerParams(vmem_limit_bytes=SMALL_LIMIT),
        cost_estimate=pl.CostEstimate(flops=0, bytes_accessed=500_000, transcendentals=0),
        name="place_patches",
    )(owners, *from_hbm(patches))


def take_kernel(owners, returned, out):
    for k in range(16):
        out[k] = returned[owners[k]]


def move_patches(body, name, owners, patches):
    shape = [jax.ShapeDtypeStruct(patches.shape, BF16)]
    return small_call(body, name, shape, (owners,), (patches,))[0]


QUERY, KEY, VALUE, COT = (slice(i * HD, (i + 1) * HD) for i in range(4))
CHUNK = 1024
CHUNKS = 4096 // CHUNK


def pack(acc, cot, z_out, y_out):
    for head, cols, out in ((0, (0, 3, 5), z_out), (1, (1, 2, 4), y_out)):
        for at, col in enumerate(cols):
            out[:, at * HD : (at + 1) * HD] = acc[:, col * HD : (col + 1) * HD].astype(BF16)
        out[:, COT] = cot[:, head * HD : (head + 1) * HD]


def block_rows(slices, j):
    return pl.ds(pl.multiple_of(slices[j] * SEQ, SEQ), SEQ)


def stream(weights, held, sems, depths):
    groups = []
    for j, depth in enumerate(depths):
        groups.append(
            [
                pltpu.make_async_copy(
                    ref.at[depth], held.at[depth, i * 256 : (i + 1) * 256], sems.at[j, i]
                )
                for i, ref in enumerate(weights)
            ]
        )
    for group in groups:
        for copy in group:
            copy.start()
    return groups


def text_kernel(slices, own, oth, cot, wq, wk, wv, flipped, z_keep, y_keep, z_out, y_out, held, turned, sems):
    depths = [block_rows(slices, j) for j in range(8)]
    groups = stream((wq, wk, wv), held, sems, depths)
    acc = None
    outgoing = []
    for j, (depth, group) in enumerate(zip(depths, groups)):
        part = own if j < RING else oth
        block = part[:, (j % RING) * SEQ : (j % RING + 1) * SEQ]
        turned[depth, :] = block.T
        outgoing.append(pltpu.make_async_copy(turned.at[depth], flipped.at[depth], sems.at[j, 3]))
        outgoing[-1].start()
        for copy in group:
            copy.wait()
        term = dot_nn(block, held[depth, :])
        acc = term if acc is None else acc + term
    pack(acc, cot[:PATCH], z_out, y_out)
    for i, (out, keep) in enumerate(((z_out, z_keep), (y_out, y_keep))):
        outgoing.append(pltpu.make_async_copy(out, keep, sems.at[8, i]))
        outgoing[-1].start()
    for copy in outgoing:
        copy.wait()


def image_kernel(own, oth, cot, held, flipped, z_out, y_out, turned, sems):
    acc = None
    outgoing = []
    for j in range(CHUNKS):
        depth = slice(j * CHUNK, (j + 1) * CHUNK)
        block = jnp.concatenate([own[:, depth], oth[:, depth]], axis=0)
        turned[depth, :] = block.T
        outgoing.append(pltpu.make_async_copy(turned.at[depth], flipped.at[depth], sems.at[j]))
        outgoing[-1].start()
        term = dot_nn(block, held[depth, :])
        acc = term if acc is None else acc + term
    pack(acc, cot[PATCH:], z_out, y_out)
    for copy in outgoing:
        copy.wait()


def from_hbm(*arrays):
    return [pltpu.with_memory_space_constraint(array, pltpu.HBM) for array in arrays]


def project_text(slices, own, oth, cot, weights):
    rows = (PATCH, 4 * HD)
    return pl.pallas_call(
        text_kernel,
        out_shape=[pltpu.HBM((4096, PATCH), BF16)]
        + [pltpu.HBM(rows, BF16)] * 2
        + [jax.ShapeDtypeStruct(rows, BF16)] * 2
        + [jax.ShapeDtypeStruct((4096, 6 * HD), BF16)],
        in_specs=smem(1) + whole(3) + in_hbm(3),
        out_specs=in_hbm(3) + whole(3),
        scratch_shapes=[pltpu.VMEM((4096, PATCH), BF16), pltpu.SemaphoreType.DMA((9, 4))],
        compiler_params=pltpu.CompilerParams(vmem_limit_bytes=SMALL_LIMIT),
        cost_estimate=pl.CostEstimate(
            flops=2 * PATCH * 4096 * 768, bytes_accessed=8_000_000, transcendentals=0
        ),
        name="qkv_text",
    )(slices, own, oth, cot, *from_hbm(*weights))


def project_image(own, oth, cot, held):
    rows = (PATCH, 4 * HD)
    return pl.pallas_call(
        image_kernel,
        out_shape=[pltpu.HBM((4096, PATCH), BF16)] + [jax.ShapeDtypeStruct(rows, BF16)] * 2,
        in_specs=whole(4),
        out_specs=in_hbm(1) + whole(2),
        scratch_shapes=[pltpu.VMEM((4096, PATCH), BF16), pltpu.SemaphoreType.DMA((CHUNKS,))],
        compiler_params=pltpu.CompilerParams(vmem_limit_bytes=SMALL_LIMIT),
        cost_estimate=pl.CostEstimate(
            flops=2 * PATCH * 4096 * 768, bytes_accessed=2_000_000, transcendentals=0
        ),
        name="qkv_image",
    )(own, oth, cot, held)


def ranks(off, shape, dim):
    index = lax.broadcasted_iota(jnp.int32, shape, dim)
    return jnp.where(index < PATCH, 2 * index, 2 * off - 1)


def diagonal_mask(off):
    return ranks(off, (SEQ, 1), 0) <= ranks(off, (1, SEQ), 1)


def fetch(refs, blocks, sems, y, z):
    copies = []
    for base, at, parts in ((0, z, refs[0:8]), (RING, y, refs[8:16])):
        for rel, off in enumerate(OFFSETS):
            slot = base + lax.rem(at + off, RING)
            for half in range(2):
                target = blocks.at[slot, half * PATCH : (half + 1) * PATCH]
                part = parts[2 * rel + half]
                copies.append(pltpu.make_async_copy(part, target, sems.at[len(copies)]))
    first = copies[0:2] + copies[8:10]
    rest = copies[2:8] + copies[10:]
    for copy in first + rest:
        copy.start()
    return first, rest


def own_pairs(meta, advance):
    y, z, off = meta[0], meta[1], meta[2]
    advance([(z, RING + y), (RING + y, z)], diagonal_mask(off))


def other_pairs(table, advance, width):
    def step(i, carry):
        codes = [table[width * i + j] for j in range(width)]
        advance([(lax.div(code, 8), lax.rem(code, 8)) for code in codes], None)
        return carry

    lax.fori_loop(0, 15 // width, step, 0)


def flip_all(dest, blocks, cols):
    for i in range(2 * RING):
        dest[i] = blocks[i, :, cols].T


def flip_own(dest, blocks, cols, y, z):
    dest[z] = blocks[z, :, cols].T
    dest[RING + y] = blocks[RING + y, :, cols].T


def stats_kernel(meta, table, *refs):
    z_out, y_out, o_out, blocks, vt, top, total, sems = refs[16:]
    y, z = meta[0], meta[1]
    first, rest = fetch(refs, blocks, sems, y, z)
    top[...] = jnp.full_like(top, NEG_LARGE)
    total[...] = jnp.zeros_like(total)
    o_out[...] = jnp.zeros_like(o_out)

    def advance(pairs, allowed):
        scores = [dot_nt(blocks[k, :, KEY], blocks[q, :, QUERY]) * (SCALE * LOG2E) for q, k in pairs]
        if allowed is not None:
            scores = [jnp.where(allowed, score, NEG_LARGE) for score in scores]
        highs = [jnp.max(score, axis=0, keepdims=True) for score in scores]
        for (q, k), score, high in zip(pairs, scores, highs):
            old = top[q]
            new = jnp.maximum(old, high)
            probs = jnp.exp2(score - new)
            shrink = jnp.exp2(old - new)
            top[q] = new
            total[q] = total[q] * shrink + jnp.sum(probs, axis=0, keepdims=True)
            o_out[q] = o_out[q] * shrink + dot_nn(vt[k], probs.astype(BF16))

    for copy in first:
        copy.wait()
    flip_own(vt, blocks, VALUE, y, z)
    own_pairs(meta, advance)
    for copy in rest:
        copy.wait()
    flip_all(vt, blocks, VALUE)
    other_pairs(table, advance, 3)
    for head, out in ((0, z_out), (1, y_out)):
        for i in range(RING):
            at = head * RING + i
            count = total[at]
            some = count > 0.0
            safe = jnp.where(some, count, 1.0)
            partial = o_out[at] / safe
            o_out[at] = partial
            flipped = blocks[at, :, COT].astype(F32).T
            out[i : i + 1, :] = jnp.where(some, top[at] + jnp.log(safe) * LOG2E, NEG_LARGE)
            out[RING + i : RING + i + 1, :] = jnp.sum(partial * flipped, axis=0, keepdims=True)


def whole(count):
    return [pl.BlockSpec(memory_space=pltpu.VMEM)] * count


def in_hbm(count):
    return [pl.BlockSpec(memory_space=pltpu.HBM)] * count


def smem(count):
    return [pl.BlockSpec(memory_space=pltpu.SMEM)] * count


def attention_stats(meta, table, pieces):
    row = pltpu.VMEM((2 * RING, 1, SEQ), F32)
    return pl.pallas_call(
        stats_kernel,
        out_shape=[jax.ShapeDtypeStruct((2 * RING, SEQ), F32)] * 2
        + [jax.ShapeDtypeStruct((2 * RING, HD, SEQ), F32)],
        in_specs=smem(2) + in_hbm(16),
        out_specs=whole(3),
        scratch_shapes=[
            pltpu.VMEM((2 * RING, SEQ, 4 * HD), BF16),
            pltpu.VMEM((2 * RING, HD, SEQ), BF16),
            row,
            row,
            pltpu.SemaphoreType.DMA((16,)),
        ],
        compiler_params=pltpu.CompilerParams(vmem_limit_bytes=STATS_LIMIT),
        cost_estimate=pl.CostEstimate(
            flops=17 * 2 * 2 * SEQ * SEQ * HD,
            bytes_accessed=5_000_000,
            transcendentals=17 * SEQ * SEQ,
        ),
        name="stats",
    )(meta, table, *pieces)


def grads_kernel(meta, table, *refs):
    o_part = refs[16]
    stats = (refs[17:21], refs[21:25])
    outs = refs[25:35]
    blocks, kt, lse, dots, keep, dq_sum, dk_sum, dv_sum, sems = refs[35:]
    y, z = meta[0], meta[1]
    first, rest = fetch(refs, blocks, sems, y, z)
    dq_sum[...] = jnp.zeros_like(dq_sum)
    dk_sum[...] = jnp.zeros_like(dk_sum)
    dv_sum[...] = jnp.zeros_like(dv_sum)
    for head in range(2):
        parts = [ref[...] for ref in stats[head]]
        logs = [part[:RING] for part in parts]
        top = functools.reduce(jnp.maximum, logs)
        shares = [jnp.exp2(log - top) for log in logs]
        norm = sum(shares)
        full = top + jnp.log(norm) * LOG2E
        dot = sum(share * part[RING:] for share, part in zip(shares, parts)) / norm
        weight = jnp.exp2(logs[0] - full)
        for i in range(RING):
            lse[head * RING + i] = full[i : i + 1]
            dots[head * RING + i] = dot[i : i + 1]
            keep[head * RING + i] = weight[i : i + 1]

    def advance(pairs, allowed):
        for q, k in pairs:
            query, cot = blocks[q, :, QUERY], blocks[q, :, COT]
            probs = jnp.exp2(dot_nt(blocks[k, :, KEY], query) * (SCALE * LOG2E) - lse[q])
            if allowed is not None:
                probs = jnp.where(allowed, probs, 0.0)
            prob_grads = dot_nt(blocks[k, :, VALUE], cot)
            slope = (probs * (prob_grads - dots[q]) * SCALE).astype(BF16)
            dv_sum[k] += dot_nn(probs.astype(BF16), cot)
            dk_sum[k] += dot_nn(slope, query)
            dq_sum[q] += dot_nn(kt[k], slope)

    for copy in first:
        copy.wait()
    flip_own(kt, blocks, KEY, y, z)
    own_pairs(meta, advance)
    for copy in rest:
        copy.wait()
    flip_all(kt, blocks, KEY)
    other_pairs(table, advance, 5)
    half = SEQ // 2
    for base, at, parts in ((0, z, outs[:5]), (RING, y, outs[5:])):
        for rel, shift in enumerate(OFFSETS):
            slot = base + lax.rem(at + shift, RING)
            terms = (
                dq_sum[slot].T.astype(BF16),
                dk_sum[slot].astype(BF16),
                dv_sum[slot].astype(BF16),
                (o_part[slot] * keep[slot]).T.astype(BF16),
            )
            for cols, term in zip((QUERY, KEY, VALUE, COT), terms):
                if rel < 3:
                    parts[rel][:, cols] = term
                else:
                    parts[3][:, cols] = term[:half]
                    parts[4][:, cols] = term[half:]


def attention_grads(meta, table, pieces, o_part, z_stats, y_stats):
    row = pltpu.VMEM((2 * RING, 1, SEQ), F32)
    tall = pltpu.VMEM((2 * RING, SEQ, HD), F32)
    flat = pltpu.VMEM((2 * RING, HD, SEQ), F32)
    full = jax.ShapeDtypeStruct((SEQ, 4 * HD), BF16)
    half = jax.ShapeDtypeStruct((SEQ // 2, 4 * HD), BF16)
    return pl.pallas_call(
        grads_kernel,
        out_shape=([full] * 3 + [half] * 2) * 2,
        in_specs=smem(2) + in_hbm(16) + whole(9),
        out_specs=whole(10),
        scratch_shapes=[
            pltpu.VMEM((2 * RING, SEQ, 4 * HD), BF16),
            pltpu.VMEM((2 * RING, HD, SEQ), BF16),
            row,
            row,
            row,
            flat,
            tall,
            tall,
            pltpu.SemaphoreType.DMA((16,)),
        ],
        compiler_params=pltpu.CompilerParams(vmem_limit_bytes=GRADS_LIMIT),
        cost_estimate=pl.CostEstimate(
            flops=17 * 5 * 2 * SEQ * SEQ * HD,
            bytes_accessed=10_000_000,
            transcendentals=17 * SEQ * SEQ,
        ),
        name="grads",
    )(meta, table, *pieces, o_part, *z_stats, *y_stats)


def tail_kernel(meta, slices, *refs):
    text, image = refs[6:8]
    weights = refs[8:11]
    gz, gy, own, oth, oth_before, oth_far = refs[11:17]
    z_parts, y_parts = refs[17:21], refs[21:25]
    held, products, sems = refs[25:]
    y, z = meta[0], meta[1]
    depths = [block_rows(slices, j) for j in range(8)]
    groups = stream(weights, held, sems, depths)
    for parts, grads in ((refs[:3], gz), (refs[3:6], gy)):
        grads[...] = total([part[...] for part in parts]).astype(BF16)
    width = 3 * HD
    rows = 256
    grads = jnp.concatenate([gz[:, :width], gy[:, :width]], axis=1)
    for rel, shift in enumerate(OFFSETS):
        depth = pl.ds(pl.multiple_of(lax.rem(y + shift, RING) * CHUNK, CHUNK), CHUNK)
        term = dot_nn(text[depth, :], grads[:PATCH]) + dot_nn(image[depth, :], grads[PATCH:])
        products[...] = term.astype(BF16)
        for other, other_shift in enumerate(OFFSETS):
            source = pl.ds(pl.multiple_of(lax.rem(z + other_shift, RING) * rows, rows), rows)
            z_parts[rel][other * rows : (other + 1) * rows, :] = products[source, :width]
            y_parts[other][rel * rows : (rel + 1) * rows, :] = products[source, width:]

    columns = [ref[:, cols] for cols in (QUERY, KEY, VALUE) for ref in (gz, gy)]
    columns = [columns[i] for i in (0, 1, 3, 2, 5, 4)]
    grads = jnp.concatenate(columns, axis=1)
    pieces = [own.at[i] for i in range(RING)]
    pieces += [oth.at[0], oth_before, oth.at[1], oth_far]
    for j, (depth, group) in enumerate(zip(depths, groups)):
        for copy in group:
            copy.wait()
        term = dot_nt(grads, held[depth, :]).astype(BF16)
        pieces[j][:PATCH] = term[:PATCH]
        at = pl.ds(pl.multiple_of(PATCH + slices[j] * 32, 32), 32)
        for i, piece in enumerate(pieces):
            piece[at, :] = term[PATCH + 32 * i : PATCH + 32 * (i + 1)]


def tail_grads(meta, slices, z_parts, y_parts, text, image, weights):
    piece = jax.ShapeDtypeStruct((CHUNK, 3 * HD), BF16)
    return pl.pallas_call(
        tail_kernel,
        out_shape=[jax.ShapeDtypeStruct((SEQ, 4 * HD), BF16)] * 2
        + [jax.ShapeDtypeStruct((RING, SEQ, SEQ), BF16)]
        + [jax.ShapeDtypeStruct((2, SEQ, SEQ), BF16)]
        + [jax.ShapeDtypeStruct((SEQ, SEQ), BF16)] * 2
        + [piece] * 8,
        in_specs=smem(2) + whole(8) + in_hbm(3),
        out_specs=whole(14),
        scratch_shapes=[
            pltpu.VMEM((4096, 6 * HD), BF16),
            pltpu.VMEM((CHUNK, 6 * HD), BF16),
            pltpu.SemaphoreType.DMA((8, 3)),
        ],
        compiler_params=pltpu.CompilerParams(vmem_limit_bytes=STREAM_LIMIT),
        cost_estimate=pl.CostEstimate(
            flops=4 * SEQ * 4096 * 768, bytes_accessed=8_000_000, transcendentals=0
        ),
        name="tail_grads",
    )(meta, slices, *z_parts, *y_parts, text, image, *from_hbm(*weights))


def x_before_kernel(kept, got, out):
    out[...] = total((kept[1], got[...])).astype(BF16)


def x_far_kernel(kept, got, out):
    out[...] = total((kept[3], got[...])).astype(BF16)


def x_rest_kernel(kept, got, own, after):
    own[...] = total((kept[0], got[0])).astype(BF16)
    after[...] = total((kept[2], got[1])).astype(BF16)


def split_kernel(*refs):
    for parts, outs in ((refs[:3], refs[6:10]), (refs[3:6], refs[10:14])):
        for i, out in enumerate(outs):
            rows = slice(i * 256, (i + 1) * 256)
            out[...] = total([part[rows] for part in parts]).astype(out.dtype)


def split_phase(z_sum, y_sum):
    own = jax.ShapeDtypeStruct((256, 3 * HD), F32)
    other = jax.ShapeDtypeStruct((256, 3 * HD), BF16)
    outs = small_call(split_kernel, "split", [own, other, other, other] * 2, (), (*z_sum, *y_sum))
    return outs[:4], outs[4:]


def mixed_kernel(meta, own, before, after, text_out, image_out):
    off = meta[2]
    grads = total((own[...], before[...], after[...])).astype(BF16).astype(F32)
    text = grads[:PATCH]
    row = lax.broadcasted_iota(jnp.int32, (PATCH, 1), 0)
    text_out[:PATCH] = jnp.where(row < off, text, 0.0).astype(BF16)
    text_out[PATCH:] = jnp.where(row < off, 0.0, text).astype(BF16)
    for i in range(8):
        rows = slice(PATCH + 32 * i, PATCH + 32 * (i + 1))
        image_out[:, i * SEQ : (i + 1) * SEQ] = grads[rows].astype(BF16)


def mixed_grads(meta, parts):
    shapes = [jax.ShapeDtypeStruct((SEQ, SEQ), BF16), jax.ShapeDtypeStruct((32, 4096), BF16)]
    return small_call(mixed_kernel, "mixed_grads", shapes, (meta,), parts)


def final_kernel(*refs):
    z_sum = total([ref[...] for ref in refs[:4]])
    y_sum = total([ref[...] for ref in refs[4:8]])
    for cols, out, first, second in (
        (QUERY, refs[8], z_sum, y_sum),
        (KEY, refs[9], y_sum, z_sum),
        (VALUE, refs[10], y_sum, z_sum),
    ):
        out[:, :HD] = first[:, cols]
        out[:, HD:] = second[:, cols]


def final_sums(z_parts, y_parts):
    shape = jax.ShapeDtypeStruct((256, 2 * HD), F32)
    return small_call(final_kernel, "final_sums", [shape] * 3, (), (*z_parts, *y_parts))


def local(text_hidden, patch_rows, image_start, w_query, w_key, w_value, d_attn):
    ctx = lax.axis_index("ctx")
    y, z = ctx // RING, ctx % RING
    images, pieces, width = patch_rows.shape
    owners = image_start // SEQ
    off = jnp.sum(jnp.where(owners == ctx, image_start, 0)) - ctx * SEQ
    meta = jnp.stack([y, z, off]).astype(jnp.int32)
    table = lax.dynamic_index_in_dim(jnp.asarray(pair_table()), ctx, 0, keepdims=False)

    tp = lax.axis_index("tp")
    x, core = tp // 2, tp % 2
    columns = (x + jnp.asarray(OFFSETS, jnp.int32)) % RING
    slices = jnp.concatenate([columns * 2 + core, columns * 2 + 1 - core]).astype(jnp.int32)

    index = jnp.arange(SEQ, dtype=jnp.int32)
    rel = (index - PATCH) // 32
    shift = rel % RING
    shift = jnp.where(shift == 0, 0, jnp.where(shift == 1, 3, shift - 1))
    sender = 2 * ((x + shift) % RING) + jnp.where(rel < RING, core, 1 - core)
    text_pos = jnp.where(index < off, index, index + PATCH)
    image_pos = off + 16 * ((index % 32) // 2) + 2 * sender + index % 2
    pos = jnp.where(index < PATCH, text_pos, image_pos)
    placed = (index[:, None] == pos[None, :]).astype(BF16)

    by_shard = place_patches(owners, patch_rows)
    by_shard, text_hidden = lax.optimization_barrier((by_shard, text_hidden))
    arrived = lax.all_to_all(by_shard, "ctx", split_axis=0, concat_axis=0, tiled=True)
    kept = index[:PATCH, None] < off
    text = jnp.where(kept, text_hidden[:PATCH], text_hidden[PATCH:])
    t_ring = ring_gather(text, send_x)
    arrived, t_ring = lax.optimization_barrier((arrived, t_ring))
    t_far = jnp.concatenate(t_ring[3:], axis=0)
    t_own = jnp.concatenate([*t_ring[:3], t_far], axis=1)
    t_oth = send_core(t_own)

    image = arrived.reshape(images * pieces, width)
    before, after = send_x(image, 1), send_x(image, -1)
    cot = dot_tn(placed, d_attn).astype(BF16)
    weights = (w_query, w_key, w_value)
    half = image.shape[0] // 2
    far = (send_x(before[:half], 1), send_x(after[half:], -1))
    text_flipped, z_keep, y_keep, z_text, y_text, held = project_text(
        slices, t_own, t_oth, cot, weights
    )
    far, z_text = lax.optimization_barrier((far, z_text))
    i_own = jnp.concatenate([image, before, after, *far], axis=0)
    i_oth = send_core(i_own)

    image_flipped, z_image, y_image = project_image(i_own, i_oth, cot, held)
    z_keep, y_keep = from_hbm(z_keep, y_keep)

    z_before, z_after = send_z(z_text, 1), send_z(z_text, -1)
    y_before, y_after = send_y(y_text, 1), send_y(y_text, -1)
    z_before, y_before, _ = lax.optimization_barrier((z_before, y_before, z_image))
    z_image_before, z_image_after = send_z(z_image, 1), send_z(z_image, -1)
    y_image_before, y_image_after = send_y(y_image, 1), send_y(y_image, -1)
    z_ring = (z_keep, z_image, z_before, z_image_before, z_after, z_image_after)
    z_ring += (send_z(z_before, 1), send_z(z_image_after, -1))
    y_ring = (y_keep, y_image, y_before, y_image_before, y_after, y_image_after)
    y_ring += (send_y(y_before, 1), send_y(y_image_after, -1))
    operands = (*z_ring, *y_ring)
    z_stats, y_stats, o_part = attention_stats(meta, table, operands)
    z_stats = [z_stats] + [send_z(z_stats, step) for step in (1, -1, 2)]
    y_stats = [y_stats] + [send_y(y_stats, step) for step in (1, -1, 2)]
    outs = attention_grads(meta, table, operands, o_part, z_stats, y_stats)
    z_parts, y_parts = ring_scatter(outs[:5], send_z), ring_scatter(outs[5:], send_y)
    gz, gy, kept_part, sent_part, sent_before, sent_far, *parts = tail_grads(
        meta, slices, z_parts, y_parts, text_flipped, image_flipped, weights
    )
    x_shape = jax.ShapeDtypeStruct((SEQ, SEQ), BF16)
    got_far, got_before = send_core(sent_far), send_core(sent_before)
    got_part = send_core(sent_part)
    z_own, z_before, z_after, z_far = parts[:4]
    y_own, y_before, y_after, y_far = parts[4:]
    z_far, y_far = send_y(z_far, 1), send_z(y_far, 1)
    (x_far,) = small_call(x_far_kernel, "x_far", [x_shape], (), (kept_part, got_far))
    (x_before,) = small_call(x_before_kernel, "x_before", [x_shape], (), (kept_part, got_before))
    x_far, x_before = send_x(x_far, 1), send_x(x_before, -1)
    x_own, x_after = small_call(x_rest_kernel, "x_rest", [x_shape] * 2, (), (kept_part, got_part))
    x_after, z_before = lax.optimization_barrier((x_after, z_before))
    z_before = send_y(z_before, -1)
    x_after = total((x_after, x_far)).astype(BF16)
    x_after = send_x(x_after, 1)
    z_far, y_far, y_before = lax.optimization_barrier((z_far, y_far, y_before))
    z_sum = (z_own, send_y(total((z_after, z_far)).astype(BF16), 1), z_before)
    y_sum = (y_own, send_z(total((y_after, y_far)).astype(BF16), 1), send_z(y_before, -1))
    d_text, i_grad = mixed_grads(meta, (x_own, x_after, x_before))
    z_sum, y_sum, i_grad = lax.optimization_barrier((z_sum, y_sum, i_grad))

    attended = jnp.concatenate([gz[:, COT], gy[:, COT]], axis=1)
    attn_out = dot_nn(placed, attended).astype(BF16)

    returned = lax.all_to_all(
        i_grad.reshape(images, pieces, width), "ctx", split_axis=0, concat_axis=0, tiled=True
    )
    d_patch = move_patches(take_kernel, "take_patches", owners, returned)
    z_pieces, y_pieces = split_phase(z_sum, y_sum)
    z_got, y_got = direct_scatter(z_pieces, send_z), direct_scatter(y_pieces, send_y)
    dw_query, dw_key, dw_value = final_sums(z_got, y_got)
    return (
        attn_out,
        d_text,
        d_patch,
        dw_query,
        dw_key,
        dw_value,
    )


def solution(mesh):
    in_specs = (
        P("ctx", "tp"),
        P(None, ("ctx", "tp"), None),
        P(),
        P(None, "tp"),
        P(None, "tp"),
        P(None, "tp"),
        P("ctx", "tp"),
    )
    out_specs = (
        P("ctx", "tp"),
        P("ctx", "tp"),
        P(None, ("ctx", "tp"), None),
        P("ctx", "tp"),
        P("ctx", "tp"),
        P("ctx", "tp"),
    )
    return jax.shard_map(local, mesh=mesh, in_specs=in_specs, out_specs=out_specs, check_vma=False)
```
